32 devices in a mesh: clu: 8 (over y, x, core), col: 4 (over z).
Axes of the slice: x: 2, y: 2, z: 4, core: 2. Of those that a mesh axis runs over, the one named last changes fastest.
Arguments:
- positions: float32 [1024, 2, 128], P(('clu', 'col')), may hold values from -4 to 4
- tension: float32 [1024, 128], P(('clu', 'col')), may hold values from -6 to 6
- bending: float32 [1024], P(('clu', 'col')), may hold values from 0.3 to 3
- moved_order: int32 [32, 32], P(('clu', 'col')), may hold values from 0 to 31, each once within a row
- move_destination: int32 [768, 1], P(('clu', 'col')), may hold values from 0 to 7; in each aligned block of 24 rows (0 to 23, 24 to 47, ...) at most 6 rows name the same one
- move_target: int32 [768], P(('clu', 'col')), may hold values from 0 to 31
- far_range: int32 [1024, 1], P(('clu', 'col')), may hold values from 0 to 3; in each aligned block of 32 rows (0 to 31, 32 to 63, ...) at most 16 rows name the same one
- old_basis: bfloat16 [128, 2048], P(None, 'col'), may hold values from -6 to 6
- source_nodes: bfloat16 [2, 2048], P(None, 'col'), may hold values from -4 to 4
Outputs:
- force: float32 [1024, 2, 128], P(('clu', 'col'))
- near_velocity: float32 [1024, 2, 128], P(('clu', 'col'))
- new_basis: float32 [1024, 64, 2, 128], P(('clu', 'col'))
The draws below stay inside these ranges and needn't reach their ends.
Inputs may be any that keep to these rules, and one draw needn't show every extreme that they name: `moved_order`: each row of a device lists its 32 vesicles once each; the first 24 are the moved ones. `move_destination`: among the 24 rows of one device no cluster is named more than 6 times. `far_range`: among the 32 rows of one device no column range is named more than 16 times.
All inputs are finite; a program needn't handle non-finite values.
Results may differ from the reference program's by a relative error of at most 0.0045.
Values may be sent and summed in bfloat16 or wider, within the bound.
No kernel may reach another device: no remote copies, remote signals or barrier semaphores. Data moves between devices by JAX's collectives and lax.ppermute only.
A program may use at most 64 MiB of HBM per device.

```python
import math
import jax
import jax.numpy as jnp
import numpy as np
from jax import lax

NODES = 128
RANK = 64
V_DEV = 32
SRC = 512
MOVE_DEV = 24
CAP = 6
CAPF = 16
VES = 1024
MOVES = 768
SRC_ALL = 2048
N_CLU = 8
N_COL = 4


def with_ends(entries, stream_key, smallest, high):
    longest = entries.shape.index(max(entries.shape))
    spots = []
    for shift in (0, 1):
        where = [jax.random.randint(jax.random.fold_in(stream_key, axis), (), 0, length) for axis, length in enumerate(entries.shape)]
        where[longest] = (where[longest] + shift) % entries.shape[longest]
        spots.append(tuple(where))
    return entries.at[spots[0]].set(smallest).at[spots[1]].set(high)


def block_levels(rng, dims, pieces, low, largest):
    loudness = 1.0
    for axis_at, blocks in pieces:
        heights = jax.random.uniform(jax.random.fold_in(jax.random.fold_in(rng, 6), axis_at), (blocks,), jnp.float32, low / len(pieces), largest / len(pieces))
        loudness = loudness * jnp.repeat(jnp.exp(heights), dims[axis_at] // blocks).reshape((-1,) + (1,) * (len(dims) - 1 - axis_at))
    return loudness


def deal_out(own_key, own, number, rows, number_of, top, limit, lean):
    ranking = jax.random.permutation(own_key, number_of)
    packed, ordinary = load_shares(number_of, rows * top, limit, lean, True), load_shares(number_of, rows * top, limit, lean, False)
    places = jnp.arange(number_of)

    def named(lengths, rotation):
        used = int((lengths > 0).sum())
        fixed = max(1, used // 4)
        shifted = fixed + (places - fixed + rotation * (used - fixed)) % max(1, number_of - fixed)
        return jnp.zeros((number_of,), jnp.int32).at[ranking[jnp.where(places < fixed, places, shifted)]].set(jnp.asarray(lengths, jnp.int32))

    lengths = jnp.where(number % 4 == 0, named(packed, number // 4), named(ordinary, number - number // 4 - 1))
    mixed = jax.random.permutation(jax.random.fold_in(own, 3), number_of)
    donor, taker = mixed[0:number_of // 2 * 2:2], mixed[1:number_of // 2 * 2:2]
    room = jnp.minimum(lengths[donor] - 1, limit - lengths[taker]) // 2
    room = jnp.where((donor == ranking[0]) | (taker == ranking[0]) | (lengths[taker] == 0), 0, jnp.maximum(room, 0))
    shifted = jax.random.randint(jax.random.fold_in(own, 4), (number_of // 2,), 0, 1 << 20) % (room + 1)
    lengths = lengths.at[donor].add(-shifted).at[taker].add(shifted)
    labels = jnp.searchsorted(jnp.cumsum(lengths), jnp.arange(rows * top), side="right").astype(jnp.int32)
    table = labels.reshape(top, rows).T
    table = table[jax.random.permutation(jax.random.fold_in(own, 1), rows)]
    rotation = jax.random.randint(jax.random.fold_in(own, 2), (rows, 1), 0, top)
    return jnp.take_along_axis(table, (jnp.arange(top)[None, :] + rotation) % top, axis=1)


def load_shares(number_of, total, reach, skew, full):
    weights = [(1 << 20) // math.isqrt(grade ** skew) + 1 for grade in range(1, number_of + 1)]
    largest = reach if full else min(reach, max(-(-total // number_of), total * weights[0] // sum(weights)))
    least = 1 if total - largest >= number_of - 1 else 0
    holding, surplus = [largest] + [least] * (number_of - 1), total - largest - least * (number_of - 1)
    while surplus > 0:
        free = [i for i in range(1, number_of) if holding[i] < largest] or [i for i in range(1, number_of) if holding[i] < reach]
        pool, remaining = sum([weights[i] for i in free]), surplus
        for i in free:
            extra = min(reach - holding[i], max(1, remaining * weights[i] // pool), surplus)
            holding[i] = holding[i] + extra
            surplus = surplus - extra
    return np.array(holding)


def noise(rng, shape, scale, bound, shards=(), held_as=jnp.bfloat16):
    drawn = scale * jax.random.normal(rng, shape, jnp.float32)
    if shards:
        drawn = drawn * block_levels(rng, shape, shards, -0.22, 0.18)
    return jnp.clip(drawn, -bound, bound).astype(held_as)


def setup_inputs(seed: int = 0) -> dict:
    streams_of = jax.random.split(jax.random.key(seed), 10)
    positions = noise(streams_of[0], (VES, 2, NODES), 1.0, 4.0, ((0, 32),), jnp.float32)
    tension = noise(streams_of[1], (VES, NODES), 1.0, 6.0, ((0, 32),), jnp.float32)
    bending = jnp.clip(jnp.exp(math.log(3.0) - 2.3025851 * jax.random.uniform(streams_of[2], (VES,), jnp.float32) ** block_levels(streams_of[2], (VES,), ((0, 32),), -0.2, 0.2)), 0.3, 3.0)
    moved_order = jax.vmap(lambda own: jax.random.permutation(own, V_DEV))(jax.random.split(streams_of[3], (N_CLU * N_COL))).reshape((N_CLU * N_COL, V_DEV)).astype(jnp.int32)
    move_destination_keys = jax.random.split(jax.random.fold_in(streams_of[4], 1), MOVES // MOVE_DEV)
    move_destination_turns = jax.random.permutation(jax.random.fold_in(streams_of[4], 3), MOVES // MOVE_DEV)
    move_destination = jax.vmap(lambda own, number: deal_out(jax.random.fold_in(streams_of[4], 2), own, number, MOVE_DEV, N_CLU, 1, CAP, 2))(move_destination_keys, move_destination_turns).reshape((MOVES, 1))
    move_target = with_ends(jax.random.randint(streams_of[5], (MOVES,), 0, V_DEV), jax.random.fold_in(streams_of[5], 1), 0, V_DEV - 1).astype(jnp.int32)
    far_range_keys = jax.random.split(jax.random.fold_in(streams_of[6], 1), VES // V_DEV)
    far_range_turns = jax.random.permutation(jax.random.fold_in(streams_of[6], 3), VES // V_DEV)
    far_range = jax.vmap(lambda own, number: deal_out(jax.random.fold_in(streams_of[6], 2), own, number, V_DEV, N_COL, 1, CAPF, 2))(far_range_keys, far_range_turns).reshape((VES, 1))
    old_basis = noise(streams_of[7], (2 * RANK, SRC_ALL), 1.0, 6.0, ((1, 4),))
    source_nodes = noise(streams_of[8], (2, SRC_ALL), 1.0, 4.0, ((1, 4),))
    return dict(positions=positions, tension=tension, bending=bending, moved_order=moved_order, move_destination=move_destination, move_target=move_target, far_range=far_range, old_basis=old_basis, source_nodes=source_nodes)


EPS_SQUARED = 0.01

def spectral_tables(node_count):
    half_count = node_count // 2
    node_index = lax.broadcasted_iota(jnp.int32, (node_count, half_count + 1), 0)
    wave_index = lax.broadcasted_iota(jnp.int32, (node_count, half_count + 1), 1)
    phase_angle = (node_index * wave_index % node_count).astype(jnp.float32) * (2.0 * math.pi / node_count)
    cosine_table = jnp.cos(phase_angle)
    sine_table = jnp.sin(phase_angle)
    wavenumber = lax.broadcasted_iota(jnp.int32, (half_count + 1,), 0).astype(jnp.float32)
    inside = jnp.logical_and(wavenumber > 0, wavenumber < half_count)
    first_weight = jnp.where(inside, 2.0 * wavenumber / half_count, 0.0).astype(jnp.float32)
    fourth_weight = jnp.where(inside, 2.0 * (wavenumber / half_count) ** 4, jnp.where(wavenumber == half_count, 1.0, 0.0)).astype(jnp.float32)
    highest = lax.Precision.HIGHEST
    derivative = (jnp.dot(cosine_table * first_weight, sine_table.T, precision=highest) - jnp.dot(sine_table * first_weight, cosine_table.T, precision=highest)) / node_count
    bending_table = (jnp.dot(cosine_table * fourth_weight, cosine_table.T, precision=highest) + jnp.dot(sine_table * fourth_weight, sine_table.T, precision=highest)) / node_count
    return (derivative, bending_table)

def membrane_force(positions, tension, bending, derivative, bending_table):
    vesicles, node_count = (positions.shape[0], positions.shape[2])
    highest = lax.Precision.HIGHEST
    flat_rows = positions.reshape(vesicles * 2, node_count)
    slope = jnp.dot(flat_rows, derivative.T, precision=highest).reshape(vesicles, 2, node_count)
    fourth = jnp.dot(flat_rows, bending_table.T, precision=highest).reshape(vesicles, 2, node_count)
    pulled = (tension[:, None, :] * slope).reshape(vesicles * 2, node_count)
    tension_part = jnp.dot(pulled, derivative.T, precision=highest).reshape(vesicles, 2, node_count)
    return tension_part - bending[:, None, None] * fourth

def near_velocity_block(target_nodes, source_nodes, source_force):
    delta_x = target_nodes[0][:, None] - source_nodes[0][None, :]
    delta_y = target_nodes[1][:, None] - source_nodes[1][None, :]
    spread = delta_x * delta_x + delta_y * delta_y + EPS_SQUARED
    log_part = -0.5 * jnp.log(spread)
    push_x = source_force[0][None, :]
    push_y = source_force[1][None, :]
    along = (delta_x * push_x + delta_y * push_y) / spread
    speed_x = lax.optimization_barrier(jnp.sum(log_part * push_x + delta_x * along, axis=1))
    speed_y = lax.optimization_barrier(jnp.sum(log_part * push_y + delta_y * along, axis=1))
    return jnp.stack([speed_x, speed_y]) / target_nodes.shape[1]

def far_kernel(targets, sources):
    delta_x = targets[..., 0, None, :] - sources[..., 0, :, None]
    delta_y = targets[..., 1, None, :] - sources[..., 1, :, None]
    spread = delta_x * delta_x + delta_y * delta_y + EPS_SQUARED
    log_part = -0.5 * jnp.log(spread)
    first_first = log_part + delta_x * delta_x / spread
    first_second = delta_x * delta_y / spread
    second_second = log_part + delta_y * delta_y / spread
    upper_rows = jnp.stack([first_first, first_second], axis=-3)
    lower_rows = jnp.stack([first_second, second_second], axis=-3)
    return jnp.stack([upper_rows, lower_rows], axis=-4).astype(jnp.bfloat16)

def reference(positions, tension, bending, moved_order, move_destination, move_target, far_range, old_basis, source_nodes):
    highest = lax.Precision.HIGHEST
    derivative, bending_table = spectral_tables(NODES)
    force = membrane_force(positions, tension, bending, derivative, bending_table)
    move_ids = jnp.arange(MOVES, dtype=jnp.int32)
    device_ids = move_ids // MOVE_DEV
    within = move_ids % MOVE_DEV
    source_ves = device_ids * V_DEV + moved_order[device_ids, within].astype(jnp.int32)
    target_ves = (move_destination[:, 0].astype(jnp.int32) * N_COL + device_ids % N_COL) * V_DEV + move_target.astype(jnp.int32)

    def near_rows(which):
        sources = lax.dynamic_slice_in_dim(source_ves, which * MOVE_DEV, MOVE_DEV, 0)
        targets = lax.dynamic_slice_in_dim(target_ves, which * MOVE_DEV, MOVE_DEV, 0)
        return jax.vmap(near_velocity_block)(positions[targets], positions[sources], force[sources])
    speeds = lax.map(near_rows, jnp.arange(MOVES // MOVE_DEV, dtype=jnp.int32)).reshape(MOVES, 2, NODES)
    near_velocity = jnp.zeros((VES, 2, NODES), jnp.float32).at[target_ves].add(speeds)
    chosen_all = far_range[:, 0].astype(jnp.int32)

    def far_rows(which):
        rows = lax.dynamic_slice_in_dim(positions, which * V_DEV, V_DEV, 0)
        chosen = lax.dynamic_slice_in_dim(chosen_all, which * V_DEV, V_DEV, 0)

        def take_range(index):
            start = (index * SRC).astype(jnp.int32)
            return (lax.dynamic_slice_in_dim(old_basis, start, SRC, 1), lax.dynamic_slice_in_dim(source_nodes, start, SRC, 1))
        basis_rows, source_rows = jax.vmap(take_range)(chosen)
        kernel = far_kernel(rows, source_rows.astype(jnp.float32))
        stacked = basis_rows.reshape(V_DEV, 2, RANK, SRC).astype(jnp.float32)
        return jnp.einsum('geks,gedsn->gkdn', stacked, kernel.astype(jnp.float32), precision=highest)
    sketch = lax.map(far_rows, jnp.arange(VES // V_DEV, dtype=jnp.int32)).reshape(VES, RANK, 2 * NODES)
    gram = jnp.einsum('vkm,vjm->kj', sketch, sketch, precision=highest)
    lower_factor = jnp.linalg.cholesky(gram)
    lower_inverse = jax.scipy.linalg.solve_triangular(lower_factor, jnp.eye(RANK, dtype=jnp.float32), lower=True)
    scale_factor = math.sqrt(2.0 * NODES * VES)
    new_basis = jnp.einsum('kj,vjm->vkm', lower_inverse, sketch, precision=highest).reshape(VES, RANK, 2, NODES) * scale_factor
    return (force, near_velocity, new_basis)
```

```python
import functools
import math

import jax
import jax.numpy as jnp
import numpy as np
from jax import lax
from jax.experimental import pallas as pl
from jax.experimental.pallas import tpu as pltpu
from jax.sharding import PartitionSpec as P

EPS_SQUARED = 0.01
F32 = jnp.float32
BF16 = jnp.bfloat16
HIGHEST = lax.Precision.HIGHEST
BLOCK = 8
MIB = 1 << 20

NT = (((1,), (1,)), ((), ()))
NN = (((1,), (0,)), ((), ()))


def spectral_tables(node_count):
    half = node_count // 2
    j = np.arange(node_count)[:, None]
    k = np.arange(half + 1)[None, :]
    phase = (j * k % node_count) * (2.0 * math.pi / node_count)
    c, s = np.cos(phase), np.sin(phase)
    k = np.arange(half + 1, dtype=np.float64)
    inside = (k > 0) & (k < half)
    u = np.where(inside, 2.0 * k / half, 0.0)
    w = np.where(inside, 2.0 * (k / half) ** 4, np.where(k == half, 1.0, 0.0))
    derivative = ((c * u) @ s.T - (s * u) @ c.T) / node_count
    bending_table = ((c * w) @ c.T + (s * w) @ s.T) / node_count
    return derivative.T.astype(np.float32), bending_table.T.astype(np.float32)


def iota(shape, axis):
    return lax.broadcasted_iota(jnp.int32, shape, axis)


def dot(a, b, dims=NN, precision=None):
    return lax.dot_general(a, b, dims, precision=precision, preferred_element_type=F32)


def reciprocal(x):
    r = pl.reciprocal(x, approx=True)
    return r * (2.0 - x * r)


def force_kernel(clu_count, slot_cap, clu_ref, pos_ref, ten_ref, bend_ref, order_ref, dest_ref,
                 target_ref, deriv_ref, table_ref, force_ref, *piece_refs):
    vesicles = ten_ref.shape[0]
    moves = target_ref.shape[1]
    x = pos_ref[pl.ds(0, vesicles, stride=2), :]
    y = pos_ref[pl.ds(1, vesicles, stride=2), :]
    rows = jnp.concatenate([x, y], axis=0)
    deriv = deriv_ref[...]
    tension = jnp.concatenate([ten_ref[...]] * 2, axis=0)
    eye = iota((vesicles, vesicles), 0) == iota((vesicles, vesicles), 1)
    bend = jnp.sum(jnp.where(eye, bend_ref[...], 0.0), axis=1, keepdims=True)
    bend = jnp.concatenate([bend] * 2, axis=0)
    slope = dot(rows, deriv, precision=HIGHEST)
    fourth = dot(rows, table_ref[...], precision=HIGHEST)
    force = dot(tension * slope, deriv, precision=HIGHEST) - bend * fourth
    force_x, force_y = force[:vesicles], force[vesicles:]
    force_ref[pl.ds(0, vesicles, stride=2), :] = force_x
    force_ref[pl.ds(1, vesicles, stride=2), :] = force_y

    slots = clu_count * BLOCK
    relative = lax.rem(dest_ref[...] - clu_ref[0] + clu_count, clu_count)
    hot = (iota((clu_count, moves), 0) == relative).astype(F32)
    earlier = (iota((moves, moves), 0) < iota((moves, moves), 1)).astype(F32)
    rank = jnp.sum(dot(hot, earlier) * hot, axis=0, keepdims=True).astype(jnp.int32)
    slot = relative * BLOCK + rank
    pack = (iota((slots, moves), 0) == slot).astype(F32)
    pick = (iota((vesicles, moves), 0) == order_ref[:, :moves]).astype(F32)
    select = dot(pack, pick, NT)
    carried = jnp.concatenate([x, y, force_x, force_y], axis=1)
    packed = dot(select, carried, precision=HIGHEST)
    tag = jnp.sum(pack * (target_ref[...] + 1).astype(F32), axis=1, keepdims=True)
    tag = jnp.broadcast_to(tag, (slots, x.shape[1]))
    for k in range(clu_count):
        here = slice(k * BLOCK, (k + 1) * BLOCK)
        piece_refs[k][...] = jnp.concatenate([packed[here], tag[here]], axis=1)


def near_kernel(clu_count, slot_cap, pos_ref, *refs):
    piece_refs, near_ref, arrived, aim_x, aim_y, speed_x, speed_y = (
        refs[:clu_count], *refs[clu_count:])
    vesicles = pos_ref.shape[0] // 2
    nodes = pos_ref.shape[1]
    for k in range(clu_count):
        arrived[k] = piece_refs[k][...]
    slots = clu_count * BLOCK
    tag = arrived[:, :, 4 * nodes:].reshape(slots, nodes)[:, :vesicles]
    hot = (tag == (iota((slots, vesicles), 1) + 1).astype(F32)).astype(F32)
    x = pos_ref[pl.ds(0, vesicles, stride=2), :]
    y = pos_ref[pl.ds(1, vesicles, stride=2), :]
    aim_x[...] = dot(hot, x, precision=HIGHEST).reshape(clu_count, BLOCK, nodes)
    aim_y[...] = dot(hot, y, precision=HIGHEST).reshape(clu_count, BLOCK, nodes)

    def piece(k, _):
        data = arrived[k]
        turned = [data[:, c * nodes:(c + 1) * nodes].T for c in range(4)]
        tx, ty = aim_x[k], aim_y[k]
        rows_x, rows_y = [], []
        for h in range(slot_cap):
            sx, sy, fx, fy = [jnp.broadcast_to(t[:, h:h + 1], (nodes, nodes)) for t in turned]
            dx = tx[h:h + 1] - sx
            dy = ty[h:h + 1] - sy
            spread = dx * dx + dy * dy + EPS_SQUARED
            log_part = -0.5 * jnp.log(spread)
            along = (dx * fx + dy * fy) * reciprocal(spread)
            rows_x.append(jnp.sum(log_part * fx + dx * along, axis=0, keepdims=True))
            rows_y.append(jnp.sum(log_part * fy + dy * along, axis=0, keepdims=True))
        rows_x += [jnp.zeros((1, nodes), F32)] * (BLOCK - slot_cap)
        rows_y += [jnp.zeros((1, nodes), F32)] * (BLOCK - slot_cap)
        speed_x[k] = jnp.concatenate(rows_x, axis=0)
        speed_y[k] = jnp.concatenate(rows_y, axis=0)
        return 0

    lax.fori_loop(0, clu_count, piece, 0)
    turned_hot = hot.T
    near_ref[pl.ds(0, vesicles, stride=2), :] = dot(
        turned_hot, speed_x[...].reshape(slots, nodes), precision=HIGHEST) / nodes
    near_ref[pl.ds(1, vesicles, stride=2), :] = dot(
        turned_hot, speed_y[...].reshape(slots, nodes), precision=HIGHEST) / nodes


def far_kernel(col_count, index_ref, range_ref, pos_ref, own_ref, nodes_ref, *refs):
    count = 2 * (col_count - 1)
    piece_refs, (high_ref, low_ref, gram_ref, basis, spots, wide) = refs[:count], refs[count:]
    vesicles = pos_ref.shape[0] // 2
    nodes = pos_ref.shape[1]
    rows, sources = own_ref.shape
    half, rank = rows // 2, rows // 2
    core, col = index_ref[0], index_ref[1]
    basis[col] = own_ref[...]
    spots[col, 0:2] = nodes_ref[...].astype(F32)
    for k in range(1, col_count):
        where = lax.rem(col - k + col_count, col_count)
        mine, other = piece_refs[2 * k - 2], piece_refs[2 * k - 1]
        basis[where, pl.ds(pl.multiple_of(core * half, half), half), :] = mine[0:half]
        basis[where, pl.ds(pl.multiple_of((1 - core) * half, half), half), :] = other[0:half]
        spots[where, 0:2] = mine[half:half + 16].astype(F32)[0:2]
    for r in range(col_count):
        turned = spots[r].T
        for c in range(2):
            wide[r, c] = jnp.broadcast_to(turned[:, c:c + 1], (sources, nodes))
    gram_ref[...] = jnp.zeros_like(gram_ref)
    chunk = 256 if sources % 256 == 0 else sources

    def vesicle(v, total):
        r = range_ref[v]
        tx = pos_ref[pl.ds(2 * v, 1), :]
        ty = pos_ref[pl.ds(2 * v + 1, 1), :]
        product = None
        for start in range(0, sources, chunk):
            dx = tx - wide[r, 0, start:start + chunk]
            dy = ty - wide[r, 1, start:start + chunk]
            spread = dx * dx + dy * dy + EPS_SQUARED
            log_part = -0.5 * jnp.log(spread)
            inverse = reciprocal(spread)
            dxr = dx * inverse
            ff = (log_part + dx * dxr).astype(BF16)
            fs = (dy * dxr).astype(BF16)
            ss = (log_part + dy * (dy * inverse)).astype(BF16)
            part = dot(basis[r, :, start:start + chunk], jnp.concatenate([ff, fs, ss], axis=1))
            product = part if product is None else product + part
        first = product[:rank, :nodes] + product[rank:, nodes:2 * nodes]
        second = product[:rank, nodes:2 * nodes] + product[rank:, 2 * nodes:]
        high_0, high_1 = first.astype(BF16), second.astype(BF16)
        low_0 = (first - high_0.astype(F32)).astype(BF16)
        low_1 = (second - high_1.astype(F32)).astype(BF16)
        high_ref[v] = jnp.concatenate([high_0, high_1], axis=0)
        low_ref[v] = jnp.concatenate([low_0, low_1], axis=0)
        both = jnp.concatenate([
            jnp.concatenate([high_0, high_1], axis=1),
            jnp.concatenate([low_0, low_1], axis=1)], axis=0)
        return total + dot(both, both, NT)

    total = lax.fori_loop(0, vesicles, vesicle, jnp.zeros((2 * rank, 2 * rank), F32))
    gram = total[:rank, :rank] + total[rank:, rank:] + (total[:rank, rank:] + total[rank:, :rank])
    gram_ref[...] = jnp.concatenate([gram[:rank // 2], gram[rank // 2:]], axis=1)


def lower_inverse(gram):
    size = gram.shape[0]
    eye = (iota((size, size), 0) == iota((size, size), 1)).astype(F32)
    rest = jnp.concatenate([gram, eye], axis=1)
    done = []
    step = 8
    for start in range(0, size, step):
        height = size - start
        columns = [jnp.broadcast_to(rest[:, start + j:start + j + 1], (height, 2 * size))
                   for j in range(step)]
        row_number = iota((height, 2 * size), 0)
        scale = jnp.zeros((step, 2 * size), F32)
        for j in range(step):
            column = columns[j]
            pivot = column[j:j + 1]
            factor = jnp.where(row_number > j, column * reciprocal(pivot), 0.0)
            for later in range(j + 1, step):
                columns[later] = columns[later] - factor * column[later:later + 1]
            rest = rest - factor * rest[j:j + 1]
            root = lax.rsqrt(pivot)
            root = root * (1.5 - 0.5 * pivot * root * root)
            scale = jnp.where(row_number[:step] == j, root, scale)
        done.append(rest[:step] * scale)
        rest = rest[step:]
    return jnp.concatenate(done, axis=0)[:, size:]


def basis_kernel(col_count, scale_factor, *refs):
    gram_refs = refs[:col_count]
    high_ref, low_ref, out_ref, weight = refs[col_count:]
    rank = high_ref.shape[1] // 2

    @pl.when(pl.program_id(0) == 0)
    def _():
        folded = gram_refs[0][...]
        for g in gram_refs[1:]:
            folded = folded + g[...]
        gram = jnp.concatenate([folded[:, :rank], folded[:, rank:]], axis=0)
        inverse = lower_inverse(gram) * scale_factor
        turn = iota((2 * rank, rank), 0) - 2 * iota((2 * rank, rank), 1)
        spread = jnp.concatenate([
            dot((turn == d).astype(F32), inverse, precision=HIGHEST) for d in range(2)], axis=1)
        high = spread.astype(BF16)
        low = (spread - high.astype(F32)).astype(BF16)
        weight[...] = jnp.concatenate([high, high, low], axis=1)

    w = weight[...]
    for v in range(high_ref.shape[0]):
        stacked = jnp.concatenate([high_ref[v], low_ref[v], high_ref[v]], axis=0)
        out_ref[v] = dot(w, stacked)


def whole_spec():
    return pl.BlockSpec(memory_space=pltpu.VMEM)


def scalar_spec():
    return pl.BlockSpec(memory_space=pltpu.SMEM)


def params(mib):
    return pltpu.CompilerParams(vmem_limit_bytes=mib * MIB)


def shifts(count, by):
    return [(i, (i + by) % count) for i in range(count)]


def per_device(positions, tension, bending, moved_order, move_destination, move_target, far_range,
               old_basis, source_nodes):
    vesicles, _, nodes = positions.shape
    rows, sources = old_basis.shape
    rank = rows // 2
    clu_count, col_count = lax.axis_size("clu"), lax.axis_size("col")
    moves = move_target.shape[0]
    slot_cap = 2 * ((moves + clu_count - 1) // clu_count)
    clu, col = lax.axis_index("clu"), lax.axis_index("col")
    core = lax.rem(clu, 2)
    flat = positions.reshape(2 * vesicles, nodes)

    half_rows = lax.dynamic_slice_in_dim(old_basis, core * rank, rank, 0)
    sent = jnp.concatenate(
        [half_rows, source_nodes, jnp.zeros((14, sources), old_basis.dtype)], axis=0)
    swap = [(i, i ^ 1) for i in range(clu_count)]
    pieces = []
    for k in range(1, col_count):
        mine = lax.ppermute(sent, "col", shifts(col_count, k))
        pieces += [mine, lax.ppermute(mine, "clu", swap)]

    deriv, table = spectral_tables(nodes)
    force_out = pl.pallas_call(
        functools.partial(force_kernel, clu_count, slot_cap),
        out_shape=[jax.ShapeDtypeStruct((2 * vesicles, nodes), F32)]
        + [jax.ShapeDtypeStruct((BLOCK, 5 * nodes), F32)] * clu_count,
        in_specs=[scalar_spec()] + [whole_spec()] * 8,
        out_specs=[whole_spec()] * (1 + clu_count),
        compiler_params=params(16),
        cost_estimate=pl.CostEstimate(flops=10**8, bytes_accessed=10**6, transcendentals=0),
    )(clu.reshape(1), flat, tension, bending.reshape(1, vesicles), moved_order,
      move_destination.reshape(1, moves), move_target.reshape(1, moves), deriv, table)
    force, packed = force_out[0], force_out[1:]
    arrived = [packed[0]] + [
        lax.ppermute(packed[k], "clu", shifts(clu_count, k)) for k in range(1, clu_count)]

    near = pl.pallas_call(
        functools.partial(near_kernel, clu_count, slot_cap),
        out_shape=jax.ShapeDtypeStruct((2 * vesicles, nodes), F32),
        in_specs=[whole_spec()] * (1 + clu_count),
        out_specs=whole_spec(),
        scratch_shapes=[pltpu.VMEM((clu_count, BLOCK, 5 * nodes), F32)]
        + [pltpu.VMEM((clu_count, BLOCK, nodes), F32)] * 4,
        compiler_params=params(16),
        cost_estimate=pl.CostEstimate(flops=10**9, bytes_accessed=10**7, transcendentals=10**6),
    )(flat, *arrived)

    high, low, gram = pl.pallas_call(
        functools.partial(far_kernel, col_count),
        out_shape=[jax.ShapeDtypeStruct((vesicles, rows, nodes), BF16)] * 2
        + [jax.ShapeDtypeStruct((rank // 2, 2 * rank), F32)],
        in_specs=[scalar_spec()] * 2 + [whole_spec()] * (3 + 2 * (col_count - 1)),
        out_specs=[whole_spec()] * 3,
        scratch_shapes=[
            pltpu.VMEM((col_count, rows, sources), BF16),
            pltpu.VMEM((col_count, 8, sources), F32),
            pltpu.VMEM((col_count, 2, sources, nodes), F32)],
        compiler_params=params(32),
        cost_estimate=pl.CostEstimate(flops=10**10, bytes_accessed=10**7, transcendentals=10**7),
    )(jnp.stack([core, col]), far_range.reshape(vesicles), flat, old_basis, source_nodes, *pieces)

    for k in range(1, clu_count):
        moved = lax.ppermute(gram, "clu", shifts(clu_count, k))
        total = moved if k == 1 else total + moved
    gram = gram + total
    grams = [gram] + [lax.ppermute(gram, "col", shifts(col_count, k)) for k in range(1, col_count)]

    scale_factor = math.sqrt(2.0 * nodes * vesicles * clu_count * col_count)
    group = 8 if vesicles % 8 == 0 else vesicles
    block = pl.BlockSpec((group, rows, nodes), lambda i: (i, 0, 0))
    new_basis = pl.pallas_call(
        functools.partial(basis_kernel, col_count, scale_factor),
        out_shape=jax.ShapeDtypeStruct((vesicles, rows, nodes), F32),
        grid=(vesicles // group,),
        in_specs=[whole_spec()] * col_count + [block] * 2,
        out_specs=block,
        scratch_shapes=[pltpu.VMEM((rows, 3 * rows), BF16)],
        compiler_params=params(16),
        cost_estimate=pl.CostEstimate(flops=10**9, bytes_accessed=10**7, transcendentals=0),
    )(*grams, high, low)

    return (force.reshape(vesicles, 2, nodes), near.reshape(vesicles, 2, nodes),
            new_basis.reshape(vesicles, rank, 2, nodes))


def solution(mesh):
    both = ("clu", "col")
    placed = (
        P(both, None, None), P(both, None), P(both), P(both, None), P(both, None), P(both),
        P(both, None), P(None, "col"), P(None, "col"),
    )
    return jax.shard_map(
        per_device,
        mesh=mesh,
        in_specs=placed,
        out_specs=(P(both, None, None), P(both, None, None), P(both, None, None, None)),
        check_vma=False,
    )
```

```python
import functools
import math

import jax
import jax.numpy as jnp
import numpy as np
from jax import lax
from jax.experimental import pallas as pl
from jax.experimental.pallas import tpu as pltpu
from jax.sharding import PartitionSpec as P

EPS_SQUARED = 0.01
F32 = jnp.float32
BF16 = jnp.bfloat16
HIGHEST = lax.Precision.HIGHEST
BLOCK = 8
MIB = 1 << 20

NT = (((1,), (1,)), ((), ()))
NN = (((1,), (0,)), ((), ()))


def spectral_tables(node_count):
    half = node_count // 2
    j = np.arange(node_count)[:, None]
    k = np.arange(half + 1)[None, :]
    phase = (j * k % node_count) * (2.0 * math.pi / node_count)
    c, s = np.cos(phase), np.sin(phase)
    k = np.arange(half + 1, dtype=np.float64)
    inside = (k > 0) & (k < half)
    u = np.where(inside, 2.0 * k / half, 0.0)
    w = np.where(inside, 2.0 * (k / half) ** 4, np.where(k == half, 1.0, 0.0))
    derivative = ((c * u) @ s.T - (s * u) @ c.T) / node_count
    bending_table = ((c * w) @ c.T + (s * w) @ s.T) / node_count
    return derivative.T.astype(np.float32), bending_table.T.astype(np.float32)


def iota(shape, axis):
    return lax.broadcasted_iota(jnp.int32, shape, axis)


def dot(a, b, dims=NN, precision=None):
    return lax.dot_general(a, b, dims, precision=precision, preferred_element_type=F32)


def reciprocal(x):
    return pl.reciprocal(x, approx=True)


def fetch(sources, targets, sems):
    copies = [pltpu.make_async_copy(s, t, sems.at[i])
              for i, (s, t) in enumerate(zip(sources, targets))]
    for copy in copies:
        copy.start()
    for copy in copies:
        copy.wait()


def force_kernel(clu_count, *refs):
    sources, targets, sems = refs[:10], refs[13:23], refs[23]
    sent_ref, force_ref, packed_ref = refs[10:13]
    fetch(sources, targets, sems)
    (own_ref, nodes_ref, pos_ref, ten_ref, bend_ref, order_ref, dest_ref, target_ref, deriv_ref,
     table_ref) = targets
    half = own_ref.shape[0] // 2
    core = lax.rem(lax.axis_index("clu"), 2)
    sent_ref[0:half] = own_ref[pl.ds(pl.multiple_of(core * half, half), half), :]
    spots = jnp.concatenate([nodes_ref[...].astype(F32)] * 8, axis=0)
    sent_ref[half:half + 16] = spots.astype(BF16)
    vesicles = ten_ref.shape[0]
    moves = target_ref.shape[1]
    x = pos_ref[pl.ds(0, vesicles, stride=2), :]
    y = pos_ref[pl.ds(1, vesicles, stride=2), :]
    rows = jnp.concatenate([x, y], axis=0)
    deriv = deriv_ref[...]
    tension = jnp.concatenate([ten_ref[...]] * 2, axis=0)
    eye = iota((vesicles, vesicles), 0) == iota((vesicles, vesicles), 1)
    bend = jnp.sum(jnp.where(eye, bend_ref[...], 0.0), axis=1, keepdims=True)
    bend = jnp.concatenate([bend] * 2, axis=0)
    slope = dot(rows, deriv, precision=HIGHEST)
    fourth = dot(rows, table_ref[...], precision=HIGHEST)
    force = dot(tension * slope, deriv, precision=HIGHEST) - bend * fourth
    force_x, force_y = force[:vesicles], force[vesicles:]
    force_ref[pl.ds(0, vesicles, stride=2), :] = force_x
    force_ref[pl.ds(1, vesicles, stride=2), :] = force_y

    slots = clu_count * BLOCK
    hot = (iota((clu_count, moves), 0) == dest_ref[...]).astype(F32)
    earlier = (iota((moves, moves), 0) < iota((moves, moves), 1)).astype(F32)
    rank = jnp.sum(dot(hot, earlier) * hot, axis=0, keepdims=True).astype(jnp.int32)
    slot = dest_ref[...] * BLOCK + rank
    pack = (iota((slots, moves), 0) == slot).astype(F32)
    pick = (iota((vesicles, moves), 0) == order_ref[:, :moves]).astype(F32)
    select = dot(pack, pick, NT)
    carried = jnp.concatenate([x, y, force_x, force_y], axis=1)
    packed = dot(select, carried, precision=HIGHEST)
    tag = jnp.sum(pack * (target_ref[...] + 1).astype(F32), axis=1, keepdims=True)
    tag = jnp.broadcast_to(tag, (slots, x.shape[1]))
    packed = jnp.concatenate([packed, tag], axis=1)
    packed_ref[...] = packed.reshape(clu_count, BLOCK, packed.shape[1])


def near_kernel(clu_count, slot_cap, pos_ref, arrived, near_ref, aim_x, aim_y, speed_x, speed_y):
    vesicles = pos_ref.shape[0] // 2
    nodes = pos_ref.shape[1]
    slots = clu_count * BLOCK
    tag = arrived[:, :, 4 * nodes:].reshape(slots, nodes)[:, :vesicles]
    hot = (tag == (iota((slots, vesicles), 1) + 1).astype(F32)).astype(F32)
    x = pos_ref[pl.ds(0, vesicles, stride=2), :]
    y = pos_ref[pl.ds(1, vesicles, stride=2), :]
    aim_x[...] = dot(hot, x, precision=HIGHEST).reshape(clu_count, BLOCK, nodes)
    aim_y[...] = dot(hot, y, precision=HIGHEST).reshape(clu_count, BLOCK, nodes)

    def piece(k, _):
        data = arrived[k]
        turned = [data[:, c * nodes:(c + 1) * nodes].T for c in range(4)]
        tx, ty = aim_x[k], aim_y[k]
        rows_x, rows_y = [], []
        for h in range(slot_cap):
            sx, sy, fx, fy = [jnp.broadcast_to(t[:, h:h + 1], (nodes, nodes)) for t in turned]
            dx = tx[h:h + 1] - sx
            dy = ty[h:h + 1] - sy
            spread = dx * dx + dy * dy + EPS_SQUARED
            log_part = -0.5 * jnp.log(spread)
            along = (dx * fx + dy * fy) * reciprocal(spread)
            rows_x.append(jnp.sum(log_part * fx + dx * along, axis=0, keepdims=True))
            rows_y.append(jnp.sum(log_part * fy + dy * along, axis=0, keepdims=True))
        rows_x += [jnp.zeros((1, nodes), F32)] * (BLOCK - slot_cap)
        rows_y += [jnp.zeros((1, nodes), F32)] * (BLOCK - slot_cap)
        speed_x[k] = jnp.concatenate(rows_x, axis=0)
        speed_y[k] = jnp.concatenate(rows_y, axis=0)
        return 0

    lax.fori_loop(0, clu_count, piece, 0)
    turned_hot = hot.T
    near_ref[pl.ds(0, vesicles, stride=2), :] = dot(
        turned_hot, speed_x[...].reshape(slots, nodes), precision=HIGHEST) / nodes
    near_ref[pl.ds(1, vesicles, stride=2), :] = dot(
        turned_hot, speed_y[...].reshape(slots, nodes), precision=HIGHEST) / nodes


def far_kernel(col_count, range_in, pos_in, own_in, nodes_in, _, *refs):
    count = 2 * (col_count - 1)
    piece_refs = refs[:count]
    (high_ref, low_ref, gram_ref, range_ref, pos_ref, own_nodes, basis, spots, wide, buffer,
     sums, sems) = refs[count:]
    vesicles = pos_ref.shape[0] // 2
    nodes = pos_ref.shape[1]
    _, rows, sources = basis.shape
    half, rank = rows // 2, rows // 2
    core, col = lax.rem(lax.axis_index("clu"), 2), lax.axis_index("col")
    fetch([range_in, pos_in, nodes_in, own_in], [range_ref, pos_ref, own_nodes, basis.at[col]], sems)
    spots[col, 0:2] = own_nodes[...].astype(F32)
    for k in range(1, col_count):
        where = origin(col, k, col_count)
        mine, other = piece_refs[2 * k - 2], piece_refs[2 * k - 1]
        basis[where, pl.ds(pl.multiple_of(core * half, half), half), :] = mine[0:half]
        basis[where, pl.ds(pl.multiple_of((1 - core) * half, half), half), :] = other[0:half]
        spots[where, 0:2] = mine[half:half + 16].astype(F32)[0:2]
    for r in range(col_count):
        turned = spots[r].T
        for c in range(2):
            wide[r, c] = jnp.broadcast_to(turned[:, c:c + 1], (sources, nodes))
    sums[...] = jnp.zeros_like(sums)
    chunk = 128 if sources % 128 == 0 else sources

    def evaluate(v, slot):
        r = range_ref[0, v]
        tx = pos_ref[pl.ds(2 * v, 1), :]
        ty = pos_ref[pl.ds(2 * v + 1, 1), :]
        for start in range(0, sources, chunk):
            dx = tx - wide[r, 0, start:start + chunk]
            dy = ty - wide[r, 1, start:start + chunk]
            spread = dx * dx + dy * dy + EPS_SQUARED
            log_part = -0.5 * jnp.log(spread)
            inverse = reciprocal(spread)
            dxr = dx * inverse
            here = slice(start, start + chunk)
            buffer[slot, here, 0:nodes] = (log_part + dx * dxr).astype(BF16)
            buffer[slot, here, nodes:2 * nodes] = (dy * dxr).astype(BF16)
            buffer[slot, here, 2 * nodes:] = (log_part + dy * (dy * inverse)).astype(BF16)

    def multiply(v, slot):
        product = dot(basis[range_ref[0, v]], buffer[slot])
        first = product[:rank, :nodes] + product[rank:, nodes:2 * nodes]
        second = product[:rank, nodes:2 * nodes] + product[rank:, 2 * nodes:]
        high_0, high_1 = first.astype(BF16), second.astype(BF16)
        low_0 = (first - high_0.astype(F32)).astype(BF16)
        low_1 = (second - high_1.astype(F32)).astype(BF16)
        high_ref[v] = jnp.concatenate([high_0, high_1], axis=0)
        low_ref[v] = jnp.concatenate([low_0, low_1], axis=0)
        both = jnp.concatenate([
            jnp.concatenate([high_0, high_1], axis=1),
            jnp.concatenate([low_0, low_1], axis=1)], axis=0)
        sums[...] += dot(both, both, NT)

    evaluate(0, 0)

    def pair(i, _):
        v = 2 * i
        evaluate(v + 1, 1)
        multiply(v, 0)
        evaluate(jnp.minimum(v + 2, vesicles - 1), 0)
        multiply(v + 1, 1)
        return 0

    lax.fori_loop(0, vesicles // 2, pair, 0)
    total = sums[...]
    gram = total[:rank, :rank] + total[rank:, rank:] + (total[:rank, rank:] + total[rank:, :rank])
    gram_ref[...] = jnp.concatenate([gram[:rank // 2], gram[rank // 2:]], axis=1)


def lower_inverse(gram):
    size = gram.shape[0]
    eye = (iota((size, size), 0) == iota((size, size), 1)).astype(F32)
    rest = jnp.concatenate([gram, eye], axis=1)
    done = []
    step = 8
    for start in range(0, size, step):
        height = size - start
        columns = [jnp.broadcast_to(rest[:, start + j:start + j + 1], (height, 2 * size))
                   for j in range(step)]
        row_number = iota((height, 2 * size), 0)
        scale = jnp.zeros((step, 2 * size), F32)
        for j in range(step):
            column = columns[j]
            pivot = column[j:j + 1]
            factor = jnp.where(row_number > j, column * reciprocal(pivot), 0.0)
            for later in range(j + 1, step):
                columns[later] = columns[later] - factor * column[later:later + 1]
            rest = rest - factor * rest[j:j + 1]
            root = lax.rsqrt(pivot)
            root = root * (1.5 - 0.5 * pivot * root * root)
            scale = jnp.where(row_number[:step] == j, root, scale)
        done.append(rest[:step] * scale)
        rest = rest[step:]
    return jnp.concatenate(done, axis=0)[:, size:]


def basis_kernel(scale_factor, *refs):
    gram_ref, high_ref, low_ref, out_ref, weight = refs
    rank = high_ref.shape[1] // 2

    @pl.when(pl.program_id(0) == 0)
    def _():
        folded = gram_ref[...]
        gram = jnp.concatenate([folded[:, :rank], folded[:, rank:]], axis=0)
        inverse = lower_inverse(gram) * scale_factor
        turn = iota((2 * rank, rank), 0) - 2 * iota((2 * rank, rank), 1)
        spread = jnp.concatenate([
            dot((turn == d).astype(F32), inverse, precision=HIGHEST) for d in range(2)], axis=1)
        high = spread.astype(BF16)
        low = (spread - high.astype(F32)).astype(BF16)
        weight[...] = jnp.concatenate([high, high, low], axis=1)

    w = weight[...]
    for v in range(high_ref.shape[0]):
        stacked = jnp.concatenate([high_ref[v], low_ref[v], high_ref[v]], axis=0)
        out_ref[v] = dot(w, stacked)


def whole_spec():
    return pl.BlockSpec(memory_space=pltpu.VMEM)


def far_off_spec():
    return pl.BlockSpec(memory_space=pltpu.HBM)


def params(mib):
    return pltpu.CompilerParams(vmem_limit_bytes=mib * MIB)


def power_of_two(count):
    return count & (count - 1) == 0


def partners(count, step):
    if power_of_two(count):
        return [(i, i ^ step) for i in range(count)]
    return [(i, (i + step) % count) for i in range(count)]


def origin(index, step, count):
    if power_of_two(count):
        return jnp.bitwise_xor(index, step)
    return lax.rem(index - step + count, count)


def sum_over(value, axis):
    count = lax.axis_size(axis)
    if power_of_two(count):
        step = 1
        while step < count:
            value = value + lax.ppermute(value, axis, partners(count, step))
            step *= 2
        return value
    moved = [lax.ppermute(value, axis, partners(count, k)) for k in range(1, count)]
    return sum(moved, value)


def per_device(positions, tension, bending, moved_order, move_destination, move_target, far_range,
               old_basis, source_nodes):
    vesicles, _, nodes = positions.shape
    rows, sources = old_basis.shape
    rank = rows // 2
    clu_count, col_count = lax.axis_size("clu"), lax.axis_size("col")
    moves = move_target.shape[0]
    slot_cap = 2 * ((moves + clu_count - 1) // clu_count)
    flat = positions.reshape(2 * vesicles, nodes)

    deriv, table = spectral_tables(nodes)
    operands = [old_basis, source_nodes, flat, tension, bending.reshape(1, vesicles), moved_order,
                move_destination.reshape(1, moves), move_target.reshape(1, moves),
                jnp.asarray(deriv), jnp.asarray(table)]
    operands = [pltpu.with_memory_space_constraint(o, pltpu.HBM) for o in operands]
    sent, force, packed = pl.pallas_call(
        functools.partial(force_kernel, clu_count),
        out_shape=[jax.ShapeDtypeStruct((rank + 16, sources), BF16),
                   jax.ShapeDtypeStruct((2 * vesicles, nodes), F32),
                   jax.ShapeDtypeStruct((clu_count, BLOCK, 5 * nodes), F32)],
        in_specs=[far_off_spec()] * len(operands),
        out_specs=[whole_spec()] * 3,
        scratch_shapes=[pltpu.VMEM(o.shape, o.dtype) for o in operands]
        + [pltpu.SemaphoreType.DMA((len(operands),))],
        compiler_params=params(16),
        cost_estimate=pl.CostEstimate(flops=10**8, bytes_accessed=10**6, transcendentals=0),
    )(*operands)

    moved_halves = [lax.ppermute(sent, "col", partners(col_count, k)) for k in range(1, col_count)]
    arrived = lax.all_to_all(packed, "clu", split_axis=0, concat_axis=0, tiled=True)
    pieces = []
    for mine in moved_halves:
        pieces += [mine, lax.ppermute(mine, "clu", [(i, i ^ 1) for i in range(clu_count)])]

    near = pl.pallas_call(
        functools.partial(near_kernel, clu_count, slot_cap),
        out_shape=jax.ShapeDtypeStruct((2 * vesicles, nodes), F32),
        in_specs=[whole_spec()] * 2,
        out_specs=whole_spec(),
        scratch_shapes=[pltpu.VMEM((clu_count, BLOCK, nodes), F32)] * 4,
        compiler_params=params(16),
        cost_estimate=pl.CostEstimate(flops=10**9, bytes_accessed=10**7, transcendentals=10**6),
    )(flat, arrived)

    high, low, gram = pl.pallas_call(
        functools.partial(far_kernel, col_count),
        out_shape=[jax.ShapeDtypeStruct((vesicles, rows, nodes), BF16)] * 2
        + [jax.ShapeDtypeStruct((rank // 2, 2 * rank), F32)],
        in_specs=[far_off_spec()] * 5 + [whole_spec()] * (2 * (col_count - 1)),
        out_specs=[whole_spec()] * 3,
        scratch_shapes=[
            pltpu.SMEM((1, vesicles), jnp.int32),
            pltpu.VMEM((2 * vesicles, nodes), F32),
            pltpu.VMEM((2, sources), BF16),
            pltpu.VMEM((col_count, rows, sources), BF16),
            pltpu.VMEM((col_count, 8, sources), F32),
            pltpu.VMEM((col_count, 2, sources, nodes), F32),
            pltpu.VMEM((2, sources, 3 * nodes), BF16),
            pltpu.VMEM((rows, rows), F32),
            pltpu.SemaphoreType.DMA((4,))],
        compiler_params=params(32),
        cost_estimate=pl.CostEstimate(flops=10**10, bytes_accessed=10**7, transcendentals=10**7),
    )(pltpu.with_memory_space_constraint(far_range.reshape(1, vesicles), pltpu.HBM), operands[2],
      operands[0], operands[1], arrived, *pieces)
    gram = sum_over(sum_over(gram, "clu"), "col")

    scale_factor = math.sqrt(2.0 * nodes * vesicles * clu_count * col_count)
    group = 8 if vesicles % 8 == 0 else vesicles
    block = pl.BlockSpec((group, rows, nodes), lambda i: (i, 0, 0))
    new_basis = pl.pallas_call(
        functools.partial(basis_kernel, scale_factor),
        out_shape=jax.ShapeDtypeStruct((vesicles, rows, nodes), F32),
        grid=(vesicles // group,),
        in_specs=[whole_spec()] + [block] * 2,
        out_specs=block,
        scratch_shapes=[pltpu.VMEM((rows, 3 * rows), BF16)],
        compiler_params=params(16),
        cost_estimate=pl.CostEstimate(flops=10**9, bytes_accessed=10**7, transcendentals=0),
    )(gram, high, low)

    return (force.reshape(vesicles, 2, nodes), near.reshape(vesicles, 2, nodes),
            new_basis.reshape(vesicles, rank, 2, nodes))


def solution(mesh):
    both = ("clu", "col")
    placed = (
        P(both, None, None), P(both, None), P(both), P(both, None), P(both, None), P(both),
        P(both, None), P(None, "col"), P(None, "col"),
    )
    return jax.shard_map(
        per_device,
        mesh=mesh,
        in_specs=placed,
        out_specs=(P(both, None, None), P(both, None, None), P(both, None, None, None)),
        check_vma=False,
    )
```

```python
import functools
import math

import jax
import jax.numpy as jnp
import numpy as np
from jax import lax
from jax.experimental import pallas as pl
from jax.experimental.pallas import tpu as pltpu
from jax.sharding import PartitionSpec as P

EPS_SQUARED = 0.01
F32 = jnp.float32
BF16 = jnp.bfloat16
HIGHEST = lax.Precision.HIGHEST
BLOCK = 8
MIB = 1 << 20

NT = (((1,), (1,)), ((), ()))
NN = (((1,), (0,)), ((), ()))


def spectral_tables(node_count):
    half = node_count // 2
    j = np.arange(node_count)[:, None]
    k = np.arange(half + 1)[None, :]
    phase = (j * k % node_count) * (2.0 * math.pi / node_count)
    c, s = np.cos(phase), np.sin(phase)
    k = np.arange(half + 1, dtype=np.float64)
    inside = (k > 0) & (k < half)
    u = np.where(inside, 2.0 * k / half, 0.0)
    w = np.where(inside, 2.0 * (k / half) ** 4, np.where(k == half, 1.0, 0.0))
    derivative = ((c * u) @ s.T - (s * u) @ c.T) / node_count
    bending_table = ((c * w) @ c.T + (s * w) @ s.T) / node_count
    return derivative.T.astype(np.float32), bending_table.T.astype(np.float32)


def iota(shape, axis):
    return lax.broadcasted_iota(jnp.int32, shape, axis)


def dot(a, b, dims=NN, precision=None):
    return lax.dot_general(a, b, dims, precision=precision, preferred_element_type=F32)


def reciprocal(x):
    return pl.reciprocal(x, approx=True)


def fetch(sources, targets, sems):
    copies = [pltpu.make_async_copy(s, t, sems.at[i])
              for i, (s, t) in enumerate(zip(sources, targets))]
    for copy in copies:
        copy.start()
    for copy in copies:
        copy.wait()


def cube_place(destination, own, count):
    relative = jnp.bitwise_xor(destination, own)
    place = jnp.zeros_like(relative)
    bit = 1
    while bit < count:
        place = 2 * place + jnp.bitwise_and(relative, bit) // bit
        bit *= 2
    return place


def cube_exchange(kept, leaving, axis):
    count = lax.axis_size(axis)
    assert power_of_two(count)
    held = [kept]
    bit = 1
    while True:
        held.append(lax.ppermute(leaving, axis, partners(count, bit)))
        bit *= 2
        if bit >= count:
            return held
        span = count // bit
        tails = []
        for h, part in enumerate(held):
            cut = part.reshape(-1, span, *part.shape[-2:])
            tails.append(cut[:, span // 2:].reshape(-1, *part.shape[-2:]))
            held[h] = cut[:, :span // 2].reshape(-1, *part.shape[-2:])
        leaving = jnp.concatenate(tails, axis=0)


def force_kernel(clu_count, *refs):
    sources, targets, sems = refs[:10], refs[14:24], refs[24]
    sent_ref, force_ref, kept_ref, leaving_ref = refs[10:14]
    fetch(sources, targets, sems)
    (own_ref, nodes_ref, pos_ref, ten_ref, bend_ref, order_ref, dest_ref, target_ref, deriv_ref,
     table_ref) = targets
    half = own_ref.shape[0] // 2
    core = lax.rem(lax.axis_index("clu"), 2)
    sent_ref[0:half] = own_ref[pl.ds(pl.multiple_of(core * half, half), half), :]
    spots = jnp.concatenate([nodes_ref[...].astype(F32)] * 8, axis=0)
    sent_ref[half:half + 16] = spots.astype(BF16)
    vesicles = ten_ref.shape[0]
    moves = target_ref.shape[1]
    x = pos_ref[pl.ds(0, vesicles, stride=2), :]
    y = pos_ref[pl.ds(1, vesicles, stride=2), :]
    rows = jnp.concatenate([x, y], axis=0)
    deriv = deriv_ref[...]
    tension = jnp.concatenate([ten_ref[...]] * 2, axis=0)
    eye = iota((vesicles, vesicles), 0) == iota((vesicles, vesicles), 1)
    bend = jnp.sum(jnp.where(eye, bend_ref[...], 0.0), axis=1, keepdims=True)
    bend = jnp.concatenate([bend] * 2, axis=0)
    slope = dot(rows, deriv, precision=HIGHEST)
    fourth = dot(rows, table_ref[...], precision=HIGHEST)
    force = dot(tension * slope, deriv, precision=HIGHEST) - bend * fourth
    force_x, force_y = force[:vesicles], force[vesicles:]
    force_ref[pl.ds(0, vesicles, stride=2), :] = force_x
    force_ref[pl.ds(1, vesicles, stride=2), :] = force_y

    slots = clu_count * BLOCK
    place = cube_place(dest_ref[...], lax.axis_index("clu"), clu_count)
    hot = (iota((clu_count, moves), 0) == place).astype(F32)
    earlier = (iota((moves, moves), 0) < iota((moves, moves), 1)).astype(F32)
    rank = jnp.sum(dot(hot, earlier) * hot, axis=0, keepdims=True).astype(jnp.int32)
    slot = place * BLOCK + rank
    pack = (iota((slots, moves), 0) == slot).astype(F32)
    pick = (iota((vesicles, moves), 0) == order_ref[:, :moves]).astype(F32)
    select = dot(pack, pick, NT)
    carried = jnp.concatenate([x, y, force_x, force_y], axis=1)
    packed = dot(select, carried, precision=HIGHEST)
    tag = jnp.sum(pack * (target_ref[...] + 1).astype(F32), axis=1, keepdims=True)
    tag = jnp.broadcast_to(tag, (slots, x.shape[1]))
    packed = jnp.concatenate([packed, tag], axis=1)
    packed = packed.reshape(clu_count, BLOCK, packed.shape[1])
    kept_ref[...] = packed[:clu_count // 2]
    leaving_ref[...] = packed[clu_count // 2:]


def near_kernel(slot_cap, piece_count, pos_ref, *refs):
    piece_refs = refs[:piece_count]
    before_ref, near_ref, arrived, aim_x, aim_y, speed_x, speed_y = refs[piece_count:]
    vesicles = pos_ref.shape[0] // 2
    nodes = pos_ref.shape[1]
    here = 0
    for ref in piece_refs:
        arrived[here:here + ref.shape[0]] = ref[...]
        here += ref.shape[0]
    pieces = arrived.shape[0]
    slots = pieces * BLOCK
    tag = arrived[:, :, 4 * nodes:].reshape(slots, nodes)[:, :vesicles]
    hot = (tag == (iota((slots, vesicles), 1) + 1).astype(F32)).astype(F32)
    x = pos_ref[pl.ds(0, vesicles, stride=2), :]
    y = pos_ref[pl.ds(1, vesicles, stride=2), :]
    aim_x[...] = dot(hot, x, precision=HIGHEST).reshape(pieces, BLOCK, nodes)
    aim_y[...] = dot(hot, y, precision=HIGHEST).reshape(pieces, BLOCK, nodes)
    chunk = 32 if nodes % 32 == 0 else nodes

    def fold(value):
        return jnp.sum(value.reshape(-1, 8, nodes), axis=0)

    def piece(k, _):
        data = arrived[k]
        turned = [data[:, c * nodes:(c + 1) * nodes].T for c in range(4)]
        tx, ty = aim_x[k], aim_y[k]
        rows_x, rows_y = [], []
        for h in range(slot_cap):
            logs_x = logs_y = pulls_x = pulls_y = jnp.zeros((8, nodes), F32)
            for start in range(0, nodes, chunk):
                sx, sy, fx, fy = [
                    jnp.broadcast_to(t[start:start + chunk, h:h + 1], (chunk, nodes))
                    for t in turned]
                dx = tx[h:h + 1] - sx
                dy = ty[h:h + 1] - sy
                spread = dx * dx + dy * dy + EPS_SQUARED
                logs = jnp.log(spread)
                along = (dx * fx + dy * fy) * reciprocal(spread)
                logs_x, logs_y = logs_x + fold(logs * fx), logs_y + fold(logs * fy)
                pulls_x, pulls_y = pulls_x + fold(dx * along), pulls_y + fold(dy * along)
            rows_x.append(jnp.sum(pulls_x - 0.5 * logs_x, axis=0, keepdims=True))
            rows_y.append(jnp.sum(pulls_y - 0.5 * logs_y, axis=0, keepdims=True))
        rows_x += [jnp.zeros((1, nodes), F32)] * (BLOCK - slot_cap)
        rows_y += [jnp.zeros((1, nodes), F32)] * (BLOCK - slot_cap)
        speed_x[k] = jnp.concatenate(rows_x, axis=0)
        speed_y[k] = jnp.concatenate(rows_y, axis=0)
        return 0

    lax.fori_loop(0, pieces, piece, 0)
    turned_hot = hot.T
    near_x = dot(turned_hot, speed_x[...].reshape(slots, nodes), precision=HIGHEST) / nodes
    near_y = dot(turned_hot, speed_y[...].reshape(slots, nodes), precision=HIGHEST) / nodes
    if before_ref is not None:
        near_x = near_x + before_ref[pl.ds(0, vesicles, stride=2), :]
        near_y = near_y + before_ref[pl.ds(1, vesicles, stride=2), :]
    near_ref[pl.ds(0, vesicles, stride=2), :] = near_x
    near_ref[pl.ds(1, vesicles, stride=2), :] = near_y


def near_start(slot_cap, piece_count, pos_ref, *refs):
    near_kernel(slot_cap, piece_count, pos_ref, *refs[:piece_count], None, *refs[piece_count:])


def near_part(flat, pieces, before, slot_cap):
    vesicles, nodes = flat.shape[0] // 2, flat.shape[1]
    count = sum(p.shape[0] for p in pieces)
    operands = [flat, *pieces] + ([] if before is None else [before])
    return pl.pallas_call(
        functools.partial(near_start if before is None else near_kernel, slot_cap, len(pieces)),
        out_shape=jax.ShapeDtypeStruct((2 * vesicles, nodes), F32),
        in_specs=[whole_spec()] * len(operands),
        out_specs=whole_spec(),
        scratch_shapes=[pltpu.VMEM((count, BLOCK, 5 * nodes), F32)]
        + [pltpu.VMEM((count, BLOCK, nodes), F32)] * 4,
        compiler_params=params(16),
        cost_estimate=pl.CostEstimate(
            flops=10**9, bytes_accessed=10**7, transcendentals=10**6),
    )(*operands)


def far_kernel(col_count, range_in, pos_in, own_in, nodes_in, *refs):
    count = 2 * (col_count - 1)
    piece_refs = refs[:count]
    (high_ref, low_ref, gram_ref, range_ref, pos_ref, own_nodes, basis, spots, wide, buffer,
     sums, sems) = refs[count:]
    vesicles = pos_ref.shape[0] // 2
    nodes = pos_ref.shape[1]
    _, rows, sources = basis.shape
    half, rank = rows // 2, rows // 2
    core, col = lax.rem(lax.axis_index("clu"), 2), lax.axis_index("col")
    fetch([range_in, pos_in, nodes_in, own_in], [range_ref, pos_ref, own_nodes, basis.at[col]], sems)
    spots[col, 0:2] = own_nodes[...].astype(F32)
    for k in range(1, col_count):
        where = origin(col, k, col_count)
        mine, other = piece_refs[2 * k - 2], piece_refs[2 * k - 1]
        basis[where, pl.ds(pl.multiple_of(core * half, half), half), :] = mine[0:half]
        basis[where, pl.ds(pl.multiple_of((1 - core) * half, half), half), :] = other[0:half]
        spots[where, 0:2] = mine[half:half + 16].astype(F32)[0:2]
    for r in range(col_count):
        turned = spots[r].T
        for c in range(2):
            wide[r, c] = jnp.broadcast_to(turned[:, c:c + 1], (sources, nodes))
    sums[...] = jnp.zeros_like(sums)
    chunk = 32 if sources % 32 == 0 else sources

    def evaluate(v, slot):
        r = range_ref[0, v]
        tx = pos_ref[pl.ds(2 * v, 1), :]
        ty = pos_ref[pl.ds(2 * v + 1, 1), :]
        for start in range(0, sources, chunk):
            dx = tx - wide[r, 0, start:start + chunk]
            dy = ty - wide[r, 1, start:start + chunk]
            spread = dx * dx + dy * dy + EPS_SQUARED
            log_part = -0.5 * jnp.log(spread)
            inverse = reciprocal(spread)
            dxr = dx * inverse
            here = slice(start, start + chunk)
            buffer[slot, here, 0:nodes] = (log_part + dx * dxr).astype(BF16)
            buffer[slot, here, nodes:2 * nodes] = (dy * dxr).astype(BF16)
            buffer[slot, here, 2 * nodes:] = (log_part + dy * (dy * inverse)).astype(BF16)

    def multiply(v, slot):
        product = dot(basis[range_ref[0, v]], buffer[slot])
        first = product[:rank, :nodes] + product[rank:, nodes:2 * nodes]
        second = product[:rank, nodes:2 * nodes] + product[rank:, 2 * nodes:]
        high_0, high_1 = first.astype(BF16), second.astype(BF16)
        low_0 = (first - high_0.astype(F32)).astype(BF16)
        low_1 = (second - high_1.astype(F32)).astype(BF16)
        high_ref[v] = jnp.concatenate([high_0, high_1], axis=0)
        low_ref[v] = jnp.concatenate([low_0, low_1], axis=0)

    def add_gram(v):
        both = jnp.concatenate([
            jnp.concatenate([ref[u, part] for u in (v, v + 1)
                             for part in (slice(0, rank), slice(rank, rows))], axis=1)
            for ref in (high_ref, low_ref)], axis=0)
        sums[...] += dot(both, both, NT)

    evaluate(0, 0)
    high_ref[0:2] = jnp.zeros((2, rows, nodes), BF16)
    low_ref[0:2] = jnp.zeros((2, rows, nodes), BF16)

    def pair(i, _):
        v = 2 * i
        add_gram(jnp.maximum(v - 2, 0))
        evaluate(v + 1, 1)
        multiply(v, 0)
        evaluate(jnp.minimum(v + 2, vesicles - 1), 0)
        multiply(v + 1, 1)
        return 0

    lax.fori_loop(0, vesicles // 2, pair, 0)
    add_gram(vesicles - 2)
    total = sums[...]
    gram = total[:rank, :rank] + total[rank:, rank:] + (total[:rank, rank:] + total[rank:, :rank])
    gram_ref[...] = jnp.concatenate([gram[:rank // 2], gram[rank // 2:]], axis=1)


def lower_inverse(gram):
    size = gram.shape[0]
    eye = (iota((size, size), 0) == iota((size, size), 1)).astype(F32)
    rest = jnp.concatenate([gram, eye], axis=1)
    done = []
    step = 8
    for start in range(0, size, step):
        height = size - start
        columns = [jnp.broadcast_to(rest[:, start + j:start + j + 1], (height, 2 * size))
                   for j in range(step)]
        row_number = iota((height, 2 * size), 0)
        scale = jnp.zeros((step, 2 * size), F32)
        for j in range(step):
            column = columns[j]
            pivot = column[j:j + 1]
            factor = jnp.where(row_number > j, column * reciprocal(pivot), 0.0)
            for later in range(j + 1, step):
                columns[later] = columns[later] - factor * column[later:later + 1]
            rest = rest - factor * rest[j:j + 1]
            root = lax.rsqrt(pivot)
            root = root * (1.5 - 0.5 * pivot * root * root)
            scale = jnp.where(row_number[:step] == j, root, scale)
        done.append(rest[:step] * scale)
        rest = rest[step:]
    return jnp.concatenate(done, axis=0)[:, size:]


def basis_kernel(scale_factor, *refs):
    gram_ref, high_ref, low_ref, out_ref, weight = refs
    rank = high_ref.shape[1] // 2

    @pl.when(pl.program_id(0) == 0)
    def _():
        folded = gram_ref[...]
        gram = jnp.concatenate([folded[:, :rank], folded[:, rank:]], axis=0)
        inverse = lower_inverse(gram) * scale_factor
        turn = iota((2 * rank, rank), 0) - 2 * iota((2 * rank, rank), 1)
        spread = jnp.concatenate([
            dot((turn == d).astype(F32), inverse, precision=HIGHEST) for d in range(2)], axis=1)
        high = spread.astype(BF16)
        low = (spread - high.astype(F32)).astype(BF16)
        weight[...] = jnp.concatenate([high, high, low], axis=1)

    w = weight[...]
    for v in range(high_ref.shape[0]):
        stacked = jnp.concatenate([high_ref[v], low_ref[v], high_ref[v]], axis=0)
        out_ref[v] = dot(w, stacked)


def whole_spec():
    return pl.BlockSpec(memory_space=pltpu.VMEM)


def far_off_spec():
    return pl.BlockSpec(memory_space=pltpu.HBM)


def params(mib):
    return pltpu.CompilerParams(vmem_limit_bytes=mib * MIB)


def power_of_two(count):
    return count & (count - 1) == 0


def partners(count, step):
    if power_of_two(count):
        return [(i, i ^ step) for i in range(count)]
    return [(i, (i + step) % count) for i in range(count)]


def origin(index, step, count):
    if power_of_two(count):
        return jnp.bitwise_xor(index, step)
    return lax.rem(index - step + count, count)


def step_groups(count, single_first):
    if not power_of_two(count):
        return [list(range(1, count))]
    groups, bit = [], 1
    if single_first and count > 1:
        groups, bit = [[1]], 2
    while bit < count:
        groups.append([bit] if 2 * bit >= count else [bit, 2 * bit, 3 * bit])
        bit *= 4
    return groups


def sum_over(value, axis, groups):
    count = lax.axis_size(axis)
    for steps in groups:
        moved = [lax.ppermute(value, axis, partners(count, k)) for k in steps]
        value = sum(moved, value)
    return value


def per_device(positions, tension, bending, moved_order, move_destination, move_target, far_range,
               old_basis, source_nodes):
    vesicles, _, nodes = positions.shape
    rows, sources = old_basis.shape
    rank = rows // 2
    clu_count, col_count = lax.axis_size("clu"), lax.axis_size("col")
    moves = move_target.shape[0]
    slot_cap = 2 * ((moves + clu_count - 1) // clu_count)
    flat = positions.reshape(2 * vesicles, nodes)

    deriv, table = spectral_tables(nodes)
    operands = [old_basis, source_nodes, flat, tension, bending.reshape(1, vesicles), moved_order,
                move_destination.reshape(1, moves), move_target.reshape(1, moves),
                jnp.asarray(deriv), jnp.asarray(table)]
    operands = [pltpu.with_memory_space_constraint(o, pltpu.HBM) for o in operands]
    sent, force, kept, leaving = pl.pallas_call(
        functools.partial(force_kernel, clu_count),
        out_shape=[jax.ShapeDtypeStruct((rank + 16, sources), BF16),
                   jax.ShapeDtypeStruct((2 * vesicles, nodes), F32),
                   *[jax.ShapeDtypeStruct((clu_count // 2, BLOCK, 5 * nodes), F32)] * 2],
        in_specs=[far_off_spec()] * len(operands),
        out_specs=[whole_spec()] * 4,
        scratch_shapes=[pltpu.VMEM(o.shape, o.dtype) for o in operands]
        + [pltpu.SemaphoreType.DMA((len(operands),))],
        compiler_params=params(16),
        cost_estimate=pl.CostEstimate(flops=10**8, bytes_accessed=10**6, transcendentals=0),
    )(*operands)

    moved_halves = [lax.ppermute(sent, "col", partners(col_count, k)) for k in range(1, col_count)]
    arrived = cube_exchange(kept, leaving, "clu")
    pieces = []
    for mine in moved_halves:
        pieces += [mine, lax.ppermute(mine, "clu", [(i, i ^ 1) for i in range(clu_count)])]

    near = near_part(flat, arrived[:-1], None, slot_cap)
    near = near_part(flat, arrived[-1:], near, slot_cap)

    high, low, gram = pl.pallas_call(
        functools.partial(far_kernel, col_count),
        out_shape=[jax.ShapeDtypeStruct((vesicles, rows, nodes), BF16)] * 2
        + [jax.ShapeDtypeStruct((rank // 2, 2 * rank), F32)],
        in_specs=[far_off_spec()] * 4 + [whole_spec()] * (2 * (col_count - 1)),
        out_specs=[whole_spec()] * 3,
        scratch_shapes=[
            pltpu.SMEM((1, vesicles), jnp.int32),
            pltpu.VMEM((2 * vesicles, nodes), F32),
            pltpu.VMEM((2, sources), BF16),
            pltpu.VMEM((col_count, rows, sources), BF16),
            pltpu.VMEM((col_count, 8, sources), F32),
            pltpu.VMEM((col_count, 2, sources, nodes), F32),
            pltpu.VMEM((2, sources, 3 * nodes), BF16),
            pltpu.VMEM((rows, rows), F32),
            pltpu.SemaphoreType.DMA((4,))],
        compiler_params=params(32),
        cost_estimate=pl.CostEstimate(flops=10**10, bytes_accessed=10**7, transcendentals=10**7),
    )(pltpu.with_memory_space_constraint(far_range.reshape(1, vesicles), pltpu.HBM), operands[2],
      operands[0], operands[1], *pieces)
    gram = sum_over(gram, "clu", step_groups(clu_count, True))
    gram = sum_over(gram, "col", step_groups(col_count, False))

    scale_factor = math.sqrt(2.0 * nodes * vesicles * clu_count * col_count)
    group = 8 if vesicles % 8 == 0 else vesicles
    block = pl.BlockSpec((group, rows, nodes), lambda i: (i, 0, 0))
    new_basis = pl.pallas_call(
        functools.partial(basis_kernel, scale_factor),
        out_shape=jax.ShapeDtypeStruct((vesicles, rows, nodes), F32),
        grid=(vesicles // group,),
        in_specs=[whole_spec()] + [block] * 2,
        out_specs=block,
        scratch_shapes=[pltpu.VMEM((rows, 3 * rows), BF16)],
        compiler_params=params(16),
        cost_estimate=pl.CostEstimate(flops=10**9, bytes_accessed=10**7, transcendentals=0),
    )(gram, high, low)

    return (force.reshape(vesicles, 2, nodes), near.reshape(vesicles, 2, nodes),
            new_basis.reshape(vesicles, rank, 2, nodes))


def solution(mesh):
    both = ("clu", "col")
    placed = (
        P(both, None, None), P(both, None), P(both), P(both, None), P(both, None), P(both),
        P(both, None), P(None, "col"), P(None, "col"),
    )
    return jax.shard_map(
        per_device,
        mesh=mesh,
        in_specs=placed,
        out_specs=(P(both, None, None), P(both, None, None), P(both, None, None, None)),
        check_vma=False,
    )
```

```python
import functools
import math

import jax
import jax.numpy as jnp
import numpy as np
from jax import lax
from jax.experimental import pallas as pl
from jax.experimental.pallas import tpu as pltpu
from jax.sharding import PartitionSpec as P

EPS_SQUARED = 0.01
F32 = jnp.float32
BF16 = jnp.bfloat16
HIGHEST = lax.Precision.HIGHEST
BLOCK = 8
MIB = 1 << 20

NT = (((1,), (1,)), ((), ()))
NN = (((1,), (0,)), ((), ()))


def spectral_tables(node_count):
    half = node_count // 2
    j = np.arange(node_count)[:, None]
    k = np.arange(half + 1)[None, :]
    phase = (j * k % node_count) * (2.0 * math.pi / node_count)
    c, s = np.cos(phase), np.sin(phase)
    k = np.arange(half + 1, dtype=np.float64)
    inside = (k > 0) & (k < half)
    u = np.where(inside, 2.0 * k / half, 0.0)
    w = np.where(inside, 2.0 * (k / half) ** 4, np.where(k == half, 1.0, 0.0))
    derivative = ((c * u) @ s.T - (s * u) @ c.T) / node_count
    bending_table = ((c * w) @ c.T + (s * w) @ s.T) / node_count
    return derivative.T.astype(np.float32), bending_table.T.astype(np.float32)


def iota(shape, axis):
    return lax.broadcasted_iota(jnp.int32, shape, axis)


def dot(a, b, dims=NN, precision=None):
    return lax.dot_general(a, b, dims, precision=precision, preferred_element_type=F32)


def reciprocal(x):
    return pl.reciprocal(x, approx=True)


def fetch(sources, targets, sems):
    copies = [pltpu.make_async_copy(s, t, sems.at[i])
              for i, (s, t) in enumerate(zip(sources, targets))]
    for copy in copies:
        copy.start()
    for copy in copies:
        copy.wait()


def force_kernel(clu_count, *refs):
    sources, targets, sems = refs[:10], refs[13:23], refs[23]
    sent_ref, force_ref, packed_ref = refs[10:13]
    fetch(sources, targets, sems)
    (own_ref, nodes_ref, pos_ref, ten_ref, bend_ref, order_ref, dest_ref, target_ref, deriv_ref,
     table_ref) = targets
    half = own_ref.shape[0] // 2
    core = lax.rem(lax.axis_index("clu"), 2)
    mine = own_ref[pl.ds(pl.multiple_of(core * half, half), half), :]
    spots = nodes_ref[...].astype(F32)
    lanes = pos_ref.shape[1]
    columns = own_ref.shape[1] // lanes
    for c in range(columns):
        sent_ref[c * half:(c + 1) * half] = mine[:, c * lanes:(c + 1) * lanes]
    spots = jnp.concatenate([spots[:, c * lanes:(c + 1) * lanes] for c in range(columns)], axis=0)
    tail = sent_ref.shape[0] - columns * half
    spots = jnp.concatenate([spots, jnp.zeros((tail - 2 * columns, lanes), F32)], axis=0)
    sent_ref[columns * half:] = spots.astype(BF16)
    vesicles = ten_ref.shape[0]
    moves = target_ref.shape[1]
    x = pos_ref[pl.ds(0, vesicles, stride=2), :]
    y = pos_ref[pl.ds(1, vesicles, stride=2), :]
    rows = jnp.concatenate([x, y], axis=0)
    deriv = deriv_ref[...]
    tension = jnp.concatenate([ten_ref[...]] * 2, axis=0)
    eye = iota((vesicles, vesicles), 0) == iota((vesicles, vesicles), 1)
    bend = jnp.sum(jnp.where(eye, bend_ref[...], 0.0), axis=1, keepdims=True)
    bend = jnp.concatenate([bend] * 2, axis=0)
    slope = dot(rows, deriv, precision=HIGHEST)
    fourth = dot(rows, table_ref[...], precision=HIGHEST)
    force = dot(tension * slope, deriv, precision=HIGHEST) - bend * fourth
    force_x, force_y = force[:vesicles], force[vesicles:]
    force_ref[pl.ds(0, vesicles, stride=2), :] = force_x
    force_ref[pl.ds(1, vesicles, stride=2), :] = force_y

    slots = clu_count * BLOCK
    hot = (iota((clu_count, moves), 0) == dest_ref[...]).astype(F32)
    earlier = (iota((moves, moves), 0) < iota((moves, moves), 1)).astype(F32)
    rank = jnp.sum(dot(hot, earlier) * hot, axis=0, keepdims=True).astype(jnp.int32)
    slot = dest_ref[...] * BLOCK + rank
    pack = (iota((slots, moves), 0) == slot).astype(F32)
    pick = (iota((vesicles, moves), 0) == order_ref[:, :moves]).astype(F32)
    select = dot(pack, pick, NT)
    carried = jnp.concatenate([x, y, force_x, force_y], axis=1)
    packed = dot(select, carried, precision=HIGHEST)
    tag = jnp.sum(pack * (target_ref[...] + 1).astype(F32), axis=1, keepdims=True)
    tag = jnp.broadcast_to(tag, (slots, x.shape[1]))
    packed = jnp.concatenate([packed, tag], axis=1)
    packed_ref[...] = packed.reshape(clu_count, BLOCK, packed.shape[1])


def near_kernel(slot_cap, span, pos_ref, all_ref, before_ref, near_ref, aim_x, aim_y, speed_x,
                speed_y):
    vesicles = pos_ref.shape[0] // 2
    nodes = pos_ref.shape[1]
    arrived = all_ref.at[span[0]:span[1]]
    pieces = span[1] - span[0]
    slots = pieces * BLOCK
    tag = arrived[:, :, 4 * nodes:].reshape(slots, nodes)[:, :vesicles]
    hot = (tag == (iota((slots, vesicles), 1) + 1).astype(F32)).astype(F32)
    x = pos_ref[pl.ds(0, vesicles, stride=2), :]
    y = pos_ref[pl.ds(1, vesicles, stride=2), :]
    aim_x[...] = dot(hot, x, precision=HIGHEST).reshape(pieces, BLOCK, nodes)
    aim_y[...] = dot(hot, y, precision=HIGHEST).reshape(pieces, BLOCK, nodes)
    chunk = 32 if nodes % 32 == 0 else nodes

    def fold(value):
        return jnp.sum(value.reshape(-1, 8, nodes), axis=0)

    def piece(k, _):
        data = arrived[k]
        turned = [data[:, c * nodes:(c + 1) * nodes].T for c in range(4)]
        tx, ty = aim_x[k], aim_y[k]
        rows_x, rows_y = [], []
        for h in range(slot_cap):
            logs_x = logs_y = pulls_x = pulls_y = jnp.zeros((8, nodes), F32)
            for start in range(0, nodes, chunk):
                sx, sy, fx, fy = [
                    jnp.broadcast_to(t[start:start + chunk, h:h + 1], (chunk, nodes))
                    for t in turned]
                dx = tx[h:h + 1] - sx
                dy = ty[h:h + 1] - sy
                spread = dx * dx + dy * dy + EPS_SQUARED
                logs = jnp.log(spread)
                along = (dx * fx + dy * fy) * reciprocal(spread)
                logs_x, logs_y = logs_x + fold(logs * fx), logs_y + fold(logs * fy)
                pulls_x, pulls_y = pulls_x + fold(dx * along), pulls_y + fold(dy * along)
            rows_x.append(jnp.sum(pulls_x - 0.5 * logs_x, axis=0, keepdims=True))
            rows_y.append(jnp.sum(pulls_y - 0.5 * logs_y, axis=0, keepdims=True))
        rows_x += [jnp.zeros((1, nodes), F32)] * (BLOCK - slot_cap)
        rows_y += [jnp.zeros((1, nodes), F32)] * (BLOCK - slot_cap)
        speed_x[k] = jnp.concatenate(rows_x, axis=0)
        speed_y[k] = jnp.concatenate(rows_y, axis=0)
        return 0

    lax.fori_loop(0, pieces, piece, 0)
    turned_hot = hot.T
    near_x = dot(turned_hot, speed_x[...].reshape(slots, nodes), precision=HIGHEST) / nodes
    near_y = dot(turned_hot, speed_y[...].reshape(slots, nodes), precision=HIGHEST) / nodes
    if before_ref is not None:
        near_x = near_x + before_ref[pl.ds(0, vesicles, stride=2), :]
        near_y = near_y + before_ref[pl.ds(1, vesicles, stride=2), :]
    near_ref[pl.ds(0, vesicles, stride=2), :] = near_x
    near_ref[pl.ds(1, vesicles, stride=2), :] = near_y


def near_start(slot_cap, span, pos_ref, all_ref, *refs):
    near_kernel(slot_cap, span, pos_ref, all_ref, None, *refs)


def near_part(flat, arrived, span, before, slot_cap):
    vesicles, nodes = flat.shape[0] // 2, flat.shape[1]
    operands = [flat, arrived] + ([] if before is None else [before])
    return pl.pallas_call(
        functools.partial(near_start if before is None else near_kernel, slot_cap, span),
        out_shape=jax.ShapeDtypeStruct((2 * vesicles, nodes), F32),
        in_specs=[whole_spec()] * len(operands),
        out_specs=whole_spec(),
        scratch_shapes=[pltpu.VMEM((span[1] - span[0], BLOCK, nodes), F32)] * 4,
        compiler_params=params(16),
        cost_estimate=pl.CostEstimate(
            flops=10**9, bytes_accessed=10**7, transcendentals=10**6),
    )(*operands)


def far_kernel(col_count, range_in, pos_in, own_in, nodes_in, *refs):
    count = 2 * (col_count - 1)
    piece_refs = refs[:count]
    (high_ref, low_ref, gram_ref, range_ref, pos_ref, own_nodes, basis, spots, wide, buffer_0,
     buffer_1, sums, sems) = refs[count:]
    vesicles = pos_ref.shape[0] // 2
    nodes = pos_ref.shape[1]
    _, rows, sources = basis.shape
    half, rank = rows // 2, rows // 2
    core, col = lax.rem(lax.axis_index("clu"), 2), lax.axis_index("col")
    fetch([range_in, pos_in, nodes_in, own_in], [range_ref, pos_ref, own_nodes, basis.at[col]], sems)
    spots[col, 0:2] = own_nodes[...].astype(F32)
    for k in range(1, col_count):
        where = origin(col, k, col_count)
        mine, other = piece_refs[2 * k - 2], piece_refs[2 * k - 1]
        columns = sources // nodes
        ends = mine[columns * half:].astype(F32)
        for c in range(columns):
            lanes = slice(c * nodes, (c + 1) * nodes)
            from_rows = slice(c * half, (c + 1) * half)
            basis[where, pl.ds(pl.multiple_of(core * half, half), half), lanes] = mine[from_rows]
            basis[where, pl.ds(pl.multiple_of((1 - core) * half, half), half), lanes] = (
                other[from_rows])
            spots[where, 0:2, lanes] = ends[2 * c:2 * c + 2]
    for r in range(col_count):
        turned = spots[r].T
        for c in range(2):
            wide[r, c] = jnp.broadcast_to(turned[:, c:c + 1], (sources, nodes))
    sums[...] = jnp.zeros_like(sums)
    chunk = 32 if sources % 32 == 0 else sources

    def evaluate(v, buffer, part, parts):
        r = range_ref[0, v]
        tx = pos_ref[pl.ds(2 * v, 1), :]
        ty = pos_ref[pl.ds(2 * v + 1, 1), :]
        for start in range(part * sources // parts, (part + 1) * sources // parts, chunk):
            dx = tx - wide[r, 0, start:start + chunk]
            dy = ty - wide[r, 1, start:start + chunk]
            spread = dx * dx + dy * dy + EPS_SQUARED
            log_part = -0.5 * jnp.log(spread)
            inverse = reciprocal(spread)
            dxr = dx * inverse
            here = slice(start, start + chunk)
            buffer[here, 0:nodes] = (log_part + dx * dxr).astype(BF16)
            buffer[here, nodes:2 * nodes] = (dy * dxr).astype(BF16)
            buffer[here, 2 * nodes:] = (log_part + dy * (dy * inverse)).astype(BF16)

    def keep(v, d, value):
        high = value.astype(BF16)
        high_ref[v, d * rank:(d + 1) * rank] = high
        low_ref[v, d * rank:(d + 1) * rank] = (value - high.astype(F32)).astype(BF16)

    def step(v, now, following):
        later = jnp.minimum(v + 1, vesicles - 1)
        rows_now = basis[range_ref[0, v]]
        product = dot(rows_now, now[:, :2 * nodes])
        evaluate(later, following, 0, 4)
        last = dot(rows_now, now[:, 2 * nodes:])
        evaluate(later, following, 1, 4)
        keep(v, 0, product[:rank, :nodes] + product[rank:, nodes:])
        evaluate(later, following, 2, 4)
        keep(v, 1, product[:rank, nodes:] + last[rank:])
        evaluate(later, following, 3, 4)

    def add_gram(v):
        both = jnp.concatenate([
            jnp.concatenate([ref[u, part] for u in (v, v + 1)
                             for part in (slice(0, rank), slice(rank, rows))], axis=1)
            for ref in (high_ref, low_ref)], axis=0)
        sums[...] += dot(both, both, NT)

    evaluate(0, buffer_0, 0, 1)
    high_ref[0:2] = jnp.zeros((2, rows, nodes), BF16)
    low_ref[0:2] = jnp.zeros((2, rows, nodes), BF16)

    def pair(i, _):
        v = 2 * i
        add_gram(jnp.maximum(v - 2, 0))
        step(v, buffer_0, buffer_1)
        step(v + 1, buffer_1, buffer_0)
        return 0

    lax.fori_loop(0, vesicles // 2, pair, 0)
    add_gram(vesicles - 2)
    total = sums[...]
    gram = total[:rank, :rank] + total[rank:, rank:] + (total[:rank, rank:] + total[rank:, :rank])
    gram_ref[...] = jnp.concatenate([gram[:rank // 2], gram[rank // 2:]], axis=1)


def lower_inverse(gram):
    size = gram.shape[0]
    eye = (iota((size, size), 0) == iota((size, size), 1)).astype(F32)
    rest = jnp.concatenate([gram, eye], axis=1)
    done = []
    step = 8
    for start in range(0, size, step):
        height = size - start
        columns = [jnp.broadcast_to(rest[:, start + j:start + j + 1], (height, 2 * size))
                   for j in range(step)]
        row_number = iota((height, 2 * size), 0)
        scale = jnp.zeros((step, 2 * size), F32)
        for j in range(step):
            column = columns[j]
            pivot = column[j:j + 1]
            factor = jnp.where(row_number > j, column * reciprocal(pivot), 0.0)
            for later in range(j + 1, step):
                columns[later] = columns[later] - factor * column[later:later + 1]
            rest = rest - factor * rest[j:j + 1]
            root = lax.rsqrt(pivot)
            root = root * (1.5 - 0.5 * pivot * root * root)
            scale = jnp.where(row_number[:step] == j, root, scale)
        done.append(rest[:step] * scale)
        rest = rest[step:]
    return jnp.concatenate(done, axis=0)[:, size:]


def basis_kernel(scale_factor, *refs):
    gram_ref, high_ref, low_ref, out_ref, weight = refs
    rank = high_ref.shape[1] // 2

    @pl.when(pl.program_id(0) == 0)
    def _():
        folded = gram_ref[...]
        gram = jnp.concatenate([folded[:, :rank], folded[:, rank:]], axis=0)
        inverse = lower_inverse(gram) * scale_factor
        turn = iota((2 * rank, rank), 0) - 2 * iota((2 * rank, rank), 1)
        spread = jnp.concatenate([
            dot((turn == d).astype(F32), inverse, precision=HIGHEST) for d in range(2)], axis=1)
        high = spread.astype(BF16)
        low = (spread - high.astype(F32)).astype(BF16)
        weight[...] = jnp.concatenate([high, high, low], axis=1)

    w = weight[...]
    for v in range(high_ref.shape[0]):
        stacked = jnp.concatenate([high_ref[v], low_ref[v], high_ref[v]], axis=0)
        out_ref[v] = dot(w, stacked)


def whole_spec():
    return pl.BlockSpec(memory_space=pltpu.VMEM)


def far_off_spec():
    return pl.BlockSpec(memory_space=pltpu.HBM)


def params(mib):
    return pltpu.CompilerParams(vmem_limit_bytes=mib * MIB)


def power_of_two(count):
    return count & (count - 1) == 0


def partners(count, step):
    if power_of_two(count):
        return [(i, i ^ step) for i in range(count)]
    return [(i, (i + step) % count) for i in range(count)]


def origin(index, step, count):
    if power_of_two(count):
        return jnp.bitwise_xor(index, step)
    return lax.rem(index - step + count, count)


def step_groups(count, single_first):
    if not power_of_two(count):
        return [list(range(1, count))]
    groups, bit = [], 1
    if single_first and count > 1:
        groups, bit = [[1]], 2
    while bit < count:
        groups.append([bit] if 2 * bit >= count else [bit, 2 * bit, 3 * bit])
        bit *= 4
    return groups


def sum_over(value, axis, groups):
    count = lax.axis_size(axis)
    for steps in groups:
        moved = [lax.ppermute(value, axis, partners(count, k)) for k in steps]
        value = sum(moved, value)
    return value


def per_device(positions, tension, bending, moved_order, move_destination, move_target, far_range,
               old_basis, source_nodes):
    vesicles, _, nodes = positions.shape
    rows, sources = old_basis.shape
    rank = rows // 2
    clu_count, col_count = lax.axis_size("clu"), lax.axis_size("col")
    moves = move_target.shape[0]
    slot_cap = 2 * ((moves + clu_count - 1) // clu_count)
    flat = positions.reshape(2 * vesicles, nodes)

    columns = sources // nodes
    sent_rows = columns * rank + (2 * columns + 15) // 16 * 16
    deriv, table = spectral_tables(nodes)
    operands = [old_basis, source_nodes, flat, tension, bending.reshape(1, vesicles), moved_order,
                move_destination.reshape(1, moves), move_target.reshape(1, moves),
                jnp.asarray(deriv), jnp.asarray(table)]
    operands = [pltpu.with_memory_space_constraint(o, pltpu.HBM) for o in operands]
    sent, force, packed = pl.pallas_call(
        functools.partial(force_kernel, clu_count),
        out_shape=[jax.ShapeDtypeStruct((sent_rows, nodes), BF16),
                   jax.ShapeDtypeStruct((2 * vesicles, nodes), F32),
                   jax.ShapeDtypeStruct((clu_count, BLOCK, 5 * nodes), F32)],
        in_specs=[far_off_spec()] * len(operands),
        out_specs=[whole_spec()] * 3,
        scratch_shapes=[pltpu.VMEM(o.shape, o.dtype) for o in operands]
        + [pltpu.SemaphoreType.DMA((len(operands),))],
        compiler_params=params(16),
        cost_estimate=pl.CostEstimate(flops=10**8, bytes_accessed=10**6, transcendentals=0),
    )(*operands)

    moved_halves = [lax.ppermute(sent, "col", partners(col_count, k)) for k in range(1, col_count)]
    arrived = lax.all_to_all(packed, "clu", split_axis=0, concat_axis=0, tiled=True)
    pieces = []
    for mine in moved_halves:
        pieces += [mine, lax.ppermute(mine, "clu", [(i, i ^ 1) for i in range(clu_count)])]

    near = near_part(flat, arrived, (0, clu_count // 2), None, slot_cap)
    near = near_part(flat, arrived, (clu_count // 2, clu_count), near, slot_cap)

    high, low, gram = pl.pallas_call(
        functools.partial(far_kernel, col_count),
        out_shape=[jax.ShapeDtypeStruct((vesicles, rows, nodes), BF16)] * 2
        + [jax.ShapeDtypeStruct((rank // 2, 2 * rank), F32)],
        in_specs=[far_off_spec()] * 4 + [whole_spec()] * (2 * (col_count - 1)),
        out_specs=[whole_spec()] * 3,
        scratch_shapes=[
            pltpu.SMEM((1, vesicles), jnp.int32),
            pltpu.VMEM((2 * vesicles, nodes), F32),
            pltpu.VMEM((2, sources), BF16),
            pltpu.VMEM((col_count, rows, sources), BF16),
            pltpu.VMEM((col_count, 8, sources), F32),
            pltpu.VMEM((col_count, 2, sources, nodes), F32),
            pltpu.VMEM((sources, 3 * nodes), BF16),
            pltpu.VMEM((sources, 3 * nodes), BF16),
            pltpu.VMEM((rows, rows), F32),
            pltpu.SemaphoreType.DMA((4,))],
        compiler_params=params(32),
        cost_estimate=pl.CostEstimate(flops=10**10, bytes_accessed=10**7, transcendentals=10**7),
    )(pltpu.with_memory_space_constraint(far_range.reshape(1, vesicles), pltpu.HBM), operands[2],
      operands[0], operands[1], *pieces)
    gram = sum_over(gram, "clu", step_groups(clu_count, True))
    gram = sum_over(gram, "col", step_groups(col_count, False))

    scale_factor = math.sqrt(2.0 * nodes * vesicles * clu_count * col_count)
    group = 8 if vesicles % 8 == 0 else vesicles
    block = pl.BlockSpec((group, rows, nodes), lambda i: (i, 0, 0))
    new_basis = pl.pallas_call(
        functools.partial(basis_kernel, scale_factor),
        out_shape=jax.ShapeDtypeStruct((vesicles, rows, nodes), F32),
        grid=(vesicles // group,),
        in_specs=[whole_spec()] + [block] * 2,
        out_specs=block,
        scratch_shapes=[pltpu.VMEM((rows, 3 * rows), BF16)],
        compiler_params=params(16),
        cost_estimate=pl.CostEstimate(flops=10**9, bytes_accessed=10**7, transcendentals=0),
    )(gram, high, low)

    return (force.reshape(vesicles, 2, nodes), near.reshape(vesicles, 2, nodes),
            new_basis.reshape(vesicles, rank, 2, nodes))


def solution(mesh):
    both = ("clu", "col")
    placed = (
        P(both, None, None), P(both, None), P(both), P(both, None), P(both, None), P(both),
        P(both, None), P(None, "col"), P(None, "col"),
    )
    return jax.shard_map(
        per_device,
        mesh=mesh,
        in_specs=placed,
        out_specs=(P(both, None, None), P(both, None, None), P(both, None, None, None)),
        check_vma=False,
    )
```

```python
import functools
import math

import jax
import jax.numpy as jnp
import numpy as np
from jax import lax
from jax.experimental import pallas as pl
from jax.experimental.pallas import tpu as pltpu
from jax.sharding import PartitionSpec as P

EPS_SQUARED = 0.01
F32 = jnp.float32
BF16 = jnp.bfloat16
HIGHEST = lax.Precision.HIGHEST
BLOCK = 8
DEPTH = 16
MIB = 1 << 20

NT = (((1,), (1,)), ((), ()))
NN = (((1,), (0,)), ((), ()))


def spectral_tables(node_count):
    half = node_count // 2
    j = np.arange(node_count)[:, None]
    k = np.arange(half + 1)[None, :]
    phase = (j * k % node_count) * (2.0 * math.pi / node_count)
    c, s = np.cos(phase), np.sin(phase)
    k = np.arange(half + 1, dtype=np.float64)
    inside = (k > 0) & (k < half)
    u = np.where(inside, 2.0 * k / half, 0.0)
    w = np.where(inside, 2.0 * (k / half) ** 4, np.where(k == half, 1.0, 0.0))
    derivative = ((c * u) @ s.T - (s * u) @ c.T) / node_count
    bending_table = ((c * w) @ c.T + (s * w) @ s.T) / node_count
    return derivative.T.astype(np.float32), bending_table.T.astype(np.float32)


def iota(shape, axis):
    return lax.broadcasted_iota(jnp.int32, shape, axis)


def dot(a, b, dims=NN, precision=None):
    return lax.dot_general(a, b, dims, precision=precision, preferred_element_type=F32)


def reciprocal(x):
    return pl.reciprocal(x, approx=True)


def fetch(sources, targets, sems):
    copies = [pltpu.make_async_copy(s, t, sems.at[i])
              for i, (s, t) in enumerate(zip(sources, targets))]
    for copy in copies:
        copy.start()
    for copy in copies:
        copy.wait()


def piece_kernel(own_in, nodes_in, sent_ref, own_ref, nodes_ref, sems):
    fetch([own_in, nodes_in], [own_ref, nodes_ref], sems)
    half = own_ref.shape[0] // 2
    core = lax.rem(lax.axis_index("clu"), 2)
    mine = own_ref[pl.ds(pl.multiple_of(core * half, half), half), :]
    spots = nodes_ref[...].astype(F32)
    lanes = sent_ref.shape[1]
    columns = own_ref.shape[1] // lanes
    for c in range(columns):
        sent_ref[c * half:(c + 1) * half] = mine[:, c * lanes:(c + 1) * lanes]
    spots = jnp.concatenate([spots[:, c * lanes:(c + 1) * lanes] for c in range(columns)], axis=0)
    tail = sent_ref.shape[0] - columns * half
    spots = jnp.concatenate([spots, jnp.zeros((tail - 2 * columns, lanes), F32)], axis=0)
    sent_ref[columns * half:] = spots.astype(BF16)


def cube_place(destination, own, count):
    relative = jnp.bitwise_xor(destination, own)
    place = jnp.zeros_like(relative)
    bit = 1
    while bit < count:
        place = 2 * place + jnp.bitwise_and(relative, bit) // bit
        bit *= 2
    return place


def cube_exchange(kept, leaving, axis):
    count = lax.axis_size(axis)
    assert power_of_two(count)
    held = [kept]
    bit = 1
    while True:
        held.append(lax.ppermute(leaving, axis, partners(count, bit)))
        bit *= 2
        if bit >= count:
            return held
        span = count // bit
        tails = []
        for h, part in enumerate(held):
            cut = part.reshape(-1, span, *part.shape[-2:])
            tails.append(cut[:, span // 2:].reshape(-1, *part.shape[-2:]))
            held[h] = cut[:, :span // 2].reshape(-1, *part.shape[-2:])
        leaving = jnp.concatenate(tails, axis=0)


def force_kernel(clu_count, *refs):
    sources, targets, sems = refs[:8], refs[11:19], refs[19]
    force_ref, kept_ref, leaving_ref = refs[8:11]
    fetch(sources, targets, sems)
    (pos_ref, ten_ref, bend_ref, order_ref, dest_ref, target_ref, deriv_ref, table_ref) = targets
    vesicles = ten_ref.shape[0]
    moves = target_ref.shape[1]
    x = pos_ref[pl.ds(0, vesicles, stride=2), :]
    y = pos_ref[pl.ds(1, vesicles, stride=2), :]
    rows = jnp.concatenate([x, y], axis=0)
    deriv = deriv_ref[...]
    tension = jnp.concatenate([ten_ref[...]] * 2, axis=0)
    eye = iota((vesicles, vesicles), 0) == iota((vesicles, vesicles), 1)
    bend = jnp.sum(jnp.where(eye, bend_ref[...], 0.0), axis=1, keepdims=True)
    bend = jnp.concatenate([bend] * 2, axis=0)
    slope = dot(rows, deriv, precision=HIGHEST)
    fourth = dot(rows, table_ref[...], precision=HIGHEST)
    force = dot(tension * slope, deriv, precision=HIGHEST) - bend * fourth
    force_x, force_y = force[:vesicles], force[vesicles:]
    force_ref[pl.ds(0, vesicles, stride=2), :] = force_x
    force_ref[pl.ds(1, vesicles, stride=2), :] = force_y

    slots = clu_count * BLOCK
    place = cube_place(dest_ref[...], lax.axis_index("clu"), clu_count)
    hot = (iota((clu_count, moves), 0) == place).astype(F32)
    earlier = (iota((moves, moves), 0) < iota((moves, moves), 1)).astype(F32)
    rank = jnp.sum(dot(hot, earlier) * hot, axis=0, keepdims=True).astype(jnp.int32)
    slot = place * BLOCK + rank
    pack = (iota((slots, moves), 0) == slot).astype(F32)
    pick = (iota((vesicles, moves), 0) == order_ref[:, :moves]).astype(F32)
    select = dot(pack, pick, NT)
    carried = jnp.concatenate([x, y, force_x, force_y], axis=1)
    packed = dot(select, carried, precision=HIGHEST)
    tag = jnp.sum(pack * (target_ref[...] + 1).astype(F32), axis=1, keepdims=True)
    tag = jnp.broadcast_to(tag, (slots, x.shape[1]))
    packed = jnp.concatenate([packed, tag], axis=1)
    packed = packed.reshape(clu_count, BLOCK, packed.shape[1])
    kept_ref[...] = packed[:clu_count // 2]
    leaving_ref[...] = packed[clu_count // 2:]


def near_kernel(slot_cap, piece_count, pos_ref, *refs):
    piece_refs = refs[:piece_count]
    near_ref, arrived, aim_x, aim_y, speed_x, speed_y = refs[piece_count:]
    vesicles = pos_ref.shape[0] // 2
    nodes = pos_ref.shape[1]
    here = 0
    for ref in piece_refs:
        arrived[here:here + ref.shape[0]] = ref[...]
        here += ref.shape[0]
    pieces = arrived.shape[0]
    slots = pieces * BLOCK
    tag = arrived[:, :, 4 * nodes:].reshape(slots, nodes)[:, :vesicles]
    hot = (tag == (iota((slots, vesicles), 1) + 1).astype(F32)).astype(F32)
    x = pos_ref[pl.ds(0, vesicles, stride=2), :]
    y = pos_ref[pl.ds(1, vesicles, stride=2), :]
    aim_x[...] = dot(hot, x, precision=HIGHEST).reshape(pieces, BLOCK, nodes)
    aim_y[...] = dot(hot, y, precision=HIGHEST).reshape(pieces, BLOCK, nodes)
    chunk = 32 if nodes % 32 == 0 else nodes

    def fold(value):
        return jnp.sum(value.reshape(-1, 8, nodes), axis=0)

    def piece(k, _):
        data = arrived[k]
        turned = [data[:, c * nodes:(c + 1) * nodes].T for c in range(4)]
        tx, ty = aim_x[k], aim_y[k]
        rows_x, rows_y = [], []
        for h in range(slot_cap):
            logs_x = logs_y = pulls_x = pulls_y = jnp.zeros((8, nodes), F32)
            for start in range(0, nodes, chunk):
                sx, sy, fx, fy = [
                    jnp.broadcast_to(t[start:start + chunk, h:h + 1], (chunk, nodes))
                    for t in turned]
                dx = tx[h:h + 1] - sx
                dy = ty[h:h + 1] - sy
                spread = dx * dx + dy * dy + EPS_SQUARED
                logs = jnp.log(spread)
                along = (dx * fx + dy * fy) * reciprocal(spread)
                logs_x, logs_y = logs_x + fold(logs * fx), logs_y + fold(logs * fy)
                pulls_x, pulls_y = pulls_x + fold(dx * along), pulls_y + fold(dy * along)
            rows_x.append(jnp.sum(pulls_x - 0.5 * logs_x, axis=0, keepdims=True))
            rows_y.append(jnp.sum(pulls_y - 0.5 * logs_y, axis=0, keepdims=True))
        rows_x += [jnp.zeros((1, nodes), F32)] * (BLOCK - slot_cap)
        rows_y += [jnp.zeros((1, nodes), F32)] * (BLOCK - slot_cap)
        speed_x[k] = jnp.concatenate(rows_x, axis=0)
        speed_y[k] = jnp.concatenate(rows_y, axis=0)
        return 0

    lax.fori_loop(0, pieces, piece, 0)
    turned_hot = hot.T
    near_x = dot(turned_hot, speed_x[...].reshape(slots, nodes), precision=HIGHEST) / nodes
    near_y = dot(turned_hot, speed_y[...].reshape(slots, nodes), precision=HIGHEST) / nodes
    near_ref[pl.ds(0, vesicles, stride=2), :] = near_x
    near_ref[pl.ds(1, vesicles, stride=2), :] = near_y


def parts_of(value, count):
    parts = []
    for _ in range(count):
        part = value.astype(BF16).astype(F32)
        parts.append(part)
        value = value - part
    return parts


def source_powers(sx, sy):
    one = jnp.ones_like(sx)
    rows = [sx] * 3 + [sy] * 3 + [one] * 3
    for value in (sx * sx, sy * sy, sx * sy):
        rows += parts_of(value, 2)
    return jnp.concatenate(rows + [jnp.zeros_like(sx)], axis=0)


def target_factors(pos_ref, factors):
    vesicles, nodes = pos_ref.shape[0] // 2, pos_ref.shape[1]
    x = pos_ref[pl.ds(0, vesicles, stride=2), :]
    y = pos_ref[pl.ds(1, vesicles, stride=2), :]
    zero = jnp.zeros_like(x)
    wanted = [
        (-2.0 * x, -2.0 * y, x * x + y * y + EPS_SQUARED, 1.0, 1.0, 0.0),
        (4.0 * x, zero, -2.0 * (x * x), -2.0, 0.0, 0.0),
        (2.0 * y, 2.0 * x, -2.0 * (x * y), 0.0, 0.0, -2.0),
        (zero, 4.0 * y, -2.0 * (y * y), 0.0, -2.0, 0.0),
    ]
    for c, entries in enumerate(wanted):
        rows = []
        for value in entries[:3]:
            rows += parts_of(value, 3)
        for value in entries[3:]:
            rows += [jnp.full_like(x, value)] * 2
        for k, row in enumerate(rows + [zero]):
            factors[c, pl.ds(k, vesicles, stride=DEPTH), :] = row


def far_kernel(col_count, range_in, pos_in, own_in, nodes_in, *refs):
    count = 2 * (col_count - 1)
    piece_refs = refs[:count]
    (high_ref, low_ref, gram_ref, range_ref, pos_ref, own_nodes, basis, spots, powers, factors,
     buffer_0, buffer_1, sums, sems) = refs[count:]
    vesicles = pos_ref.shape[0] // 2
    nodes = pos_ref.shape[1]
    _, rows, sources = basis.shape
    half, rank = rows // 2, rows // 2
    core, col = lax.rem(lax.axis_index("clu"), 2), lax.axis_index("col")
    fetch([range_in, pos_in, nodes_in, own_in], [range_ref, pos_ref, own_nodes, basis.at[col]], sems)
    spots[col, 0:2] = own_nodes[...].astype(F32)
    for k in range(1, col_count):
        where = origin(col, k, col_count)
        mine, other = piece_refs[2 * k - 2], piece_refs[2 * k - 1]
        columns = sources // nodes
        ends = mine[columns * half:].astype(F32)
        for c in range(columns):
            lanes = slice(c * nodes, (c + 1) * nodes)
            from_rows = slice(c * half, (c + 1) * half)
            basis[where, pl.ds(pl.multiple_of(core * half, half), half), lanes] = mine[from_rows]
            basis[where, pl.ds(pl.multiple_of((1 - core) * half, half), half), lanes] = (
                other[from_rows])
            spots[where, 0:2, lanes] = ends[2 * c:2 * c + 2]
    for r in range(col_count):
        powers[r] = source_powers(spots[r, 0:1], spots[r, 1:2]).T.astype(BF16)
    target_factors(pos_ref, factors)
    sums[...] = jnp.zeros_like(sums)

    def evaluate(v, buffer, part, parts):
        r = range_ref[0, v]
        rows_here = pl.ds(pl.multiple_of(v * DEPTH, DEPTH), DEPTH)
        mine = jnp.concatenate([factors[c, rows_here, :] for c in range(4)], axis=1).astype(BF16)
        size = sources // parts
        here = slice(part * size, (part + 1) * size)
        shape = dot(powers[r, here], mine)
        spread, xx, xy, yy = [shape[:, c * nodes:(c + 1) * nodes] for c in range(4)]
        log_part = jnp.log(spread)
        inverse = reciprocal(spread)
        buffer[here, 0:nodes] = (log_part + inverse * xx).astype(BF16)
        buffer[here, nodes:2 * nodes] = (inverse * xy).astype(BF16)
        buffer[here, 2 * nodes:] = (log_part + inverse * yy).astype(BF16)

    def keep(v, d, value):
        high = value.astype(BF16)
        high_ref[v, d * rank:(d + 1) * rank] = high
        low_ref[v, d * rank:(d + 1) * rank] = (value - high.astype(F32)).astype(BF16)

    def step(v, now, following):
        later = jnp.minimum(v + 1, vesicles - 1)
        rows_now = basis[range_ref[0, v]]
        product = dot(rows_now, now[:, :2 * nodes])
        evaluate(later, following, 0, 4)
        last = dot(rows_now, now[:, 2 * nodes:])
        evaluate(later, following, 1, 4)
        keep(v, 0, product[:rank, :nodes] + product[rank:, nodes:])
        evaluate(later, following, 2, 4)
        keep(v, 1, product[:rank, nodes:] + last[rank:])
        evaluate(later, following, 3, 4)

    def add_gram(v):
        both = jnp.concatenate([
            jnp.concatenate([ref[u, part] for u in (v, v + 1)
                             for part in (slice(0, rank), slice(rank, rows))], axis=1)
            for ref in (high_ref, low_ref)], axis=0)
        sums[...] += dot(both, both, NT)

    for part in range(4):
        evaluate(0, buffer_0, part, 4)
    high_ref[0:2] = jnp.zeros((2, rows, nodes), BF16)
    low_ref[0:2] = jnp.zeros((2, rows, nodes), BF16)

    def pair(i, _):
        v = 2 * i
        add_gram(jnp.maximum(v - 2, 0))
        step(v, buffer_0, buffer_1)
        step(v + 1, buffer_1, buffer_0)
        return 0

    lax.fori_loop(0, vesicles // 2, pair, 0)
    add_gram(vesicles - 2)
    total = sums[...]
    gram = total[:rank, :rank] + total[rank:, rank:] + (total[:rank, rank:] + total[rank:, :rank])
    gram_ref[...] = jnp.concatenate([gram[:rank // 2], gram[rank // 2:]], axis=1)


def lower_inverse(gram):
    size = gram.shape[0]
    eye = (iota((size, size), 0) == iota((size, size), 1)).astype(F32)
    rest = jnp.concatenate([gram, eye], axis=1)
    done = []
    step = 8
    for start in range(0, size, step):
        height = size - start
        columns = [jnp.broadcast_to(rest[:, start + j:start + j + 1], (height, 2 * size))
                   for j in range(step)]
        row_number = iota((height, 2 * size), 0)
        scale = jnp.zeros((step, 2 * size), F32)
        for j in range(step):
            column = columns[j]
            pivot = column[j:j + 1]
            factor = jnp.where(row_number > j, column * reciprocal(pivot), 0.0)
            for later in range(j + 1, step):
                columns[later] = columns[later] - factor * column[later:later + 1]
            rest = rest - factor * rest[j:j + 1]
            root = lax.rsqrt(pivot)
            root = root * (1.5 - 0.5 * pivot * root * root)
            scale = jnp.where(row_number[:step] == j, root, scale)
        done.append(rest[:step] * scale)
        rest = rest[step:]
    return jnp.concatenate(done, axis=0)[:, size:]


def basis_kernel(scale_factor, *refs):
    gram_ref, high_ref, low_ref, out_ref, weight = refs
    rank = high_ref.shape[1] // 2

    @pl.when(pl.program_id(0) == 0)
    def _():
        folded = gram_ref[...]
        gram = jnp.concatenate([folded[:, :rank], folded[:, rank:]], axis=0)
        inverse = lower_inverse(gram) * scale_factor
        turn = iota((2 * rank, rank), 0) - 2 * iota((2 * rank, rank), 1)
        spread = jnp.concatenate([
            dot((turn == d).astype(F32), inverse, precision=HIGHEST) for d in range(2)], axis=1)
        high = spread.astype(BF16)
        low = (spread - high.astype(F32)).astype(BF16)
        weight[...] = jnp.concatenate([high, high, low], axis=1)

    w = weight[...]
    for v in range(high_ref.shape[0]):
        stacked = jnp.concatenate([high_ref[v], low_ref[v], high_ref[v]], axis=0)
        out_ref[v] = dot(w, stacked)


def whole_spec():
    return pl.BlockSpec(memory_space=pltpu.VMEM)


def far_off_spec():
    return pl.BlockSpec(memory_space=pltpu.HBM)


def params(mib):
    return pltpu.CompilerParams(vmem_limit_bytes=mib * MIB)


def power_of_two(count):
    return count & (count - 1) == 0


def partners(count, step):
    if power_of_two(count):
        return [(i, i ^ step) for i in range(count)]
    return [(i, (i + step) % count) for i in range(count)]


def origin(index, step, count):
    if power_of_two(count):
        return jnp.bitwise_xor(index, step)
    return lax.rem(index - step + count, count)


def step_groups(count, single_first):
    if not power_of_two(count):
        return [list(range(1, count))]
    groups, bit = [], 1
    if single_first and count > 1:
        groups, bit = [[1]], 2
    while bit < count:
        groups.append([bit] if 2 * bit >= count else [bit, 2 * bit, 3 * bit])
        bit *= 4
    return groups


def sum_over(value, axis, groups):
    count = lax.axis_size(axis)
    for steps in groups:
        moved = [lax.ppermute(value, axis, partners(count, k)) for k in steps]
        value = sum(moved, value)
    return value


def per_device(positions, tension, bending, moved_order, move_destination, move_target, far_range,
               old_basis, source_nodes):
    vesicles, _, nodes = positions.shape
    rows, sources = old_basis.shape
    rank = rows // 2
    clu_count, col_count = lax.axis_size("clu"), lax.axis_size("col")
    moves = move_target.shape[0]
    slot_cap = 2 * ((moves + clu_count - 1) // clu_count)
    flat = positions.reshape(2 * vesicles, nodes)

    columns = sources // nodes
    sent_rows = columns * rank + (2 * columns + 15) // 16 * 16
    deriv, table = spectral_tables(nodes)
    near_by = functools.partial(pltpu.with_memory_space_constraint, memory_space=pltpu.HBM)
    basis_here, nodes_here, flat_here = near_by(old_basis), near_by(source_nodes), near_by(flat)
    sent = pl.pallas_call(
        piece_kernel,
        out_shape=jax.ShapeDtypeStruct((sent_rows, nodes), BF16),
        in_specs=[far_off_spec()] * 2,
        out_specs=whole_spec(),
        scratch_shapes=[pltpu.VMEM(old_basis.shape, BF16), pltpu.VMEM(source_nodes.shape, BF16),
                        pltpu.SemaphoreType.DMA((2,))],
        compiler_params=params(16),
        cost_estimate=pl.CostEstimate(flops=10**5, bytes_accessed=10**5, transcendentals=0),
    )(basis_here, nodes_here)

    operands = [flat, tension, bending.reshape(1, vesicles), moved_order,
                move_destination.reshape(1, moves), move_target.reshape(1, moves),
                jnp.asarray(deriv), jnp.asarray(table)]
    operands = [flat_here] + [near_by(o) for o in operands[1:]]
    force, kept, leaving = pl.pallas_call(
        functools.partial(force_kernel, clu_count),
        out_shape=[jax.ShapeDtypeStruct((2 * vesicles, nodes), F32),
                   *[jax.ShapeDtypeStruct((clu_count // 2, BLOCK, 5 * nodes), F32)] * 2],
        in_specs=[far_off_spec()] * len(operands),
        out_specs=[whole_spec()] * 3,
        scratch_shapes=[pltpu.VMEM(o.shape, o.dtype) for o in operands]
        + [pltpu.SemaphoreType.DMA((len(operands),))],
        compiler_params=params(16),
        cost_estimate=pl.CostEstimate(flops=10**8, bytes_accessed=10**6, transcendentals=0),
    )(*operands)

    moved_halves = [lax.ppermute(sent, "col", partners(col_count, k)) for k in range(1, col_count)]
    arrived = cube_exchange(kept, leaving, "clu")
    pieces = []
    for mine in moved_halves:
        pieces += [mine, lax.ppermute(mine, "clu", [(i, i ^ 1) for i in range(clu_count)])]

    near = pl.pallas_call(
        functools.partial(near_kernel, slot_cap, len(arrived)),
        out_shape=jax.ShapeDtypeStruct((2 * vesicles, nodes), F32),
        in_specs=[whole_spec()] * (1 + len(arrived)),
        out_specs=whole_spec(),
        scratch_shapes=[pltpu.VMEM((clu_count, BLOCK, 5 * nodes), F32)]
        + [pltpu.VMEM((clu_count, BLOCK, nodes), F32)] * 4,
        compiler_params=params(16),
        cost_estimate=pl.CostEstimate(
            flops=10**9, bytes_accessed=10**7, transcendentals=10**6),
    )(flat, *arrived)

    high, low, gram = pl.pallas_call(
        functools.partial(far_kernel, col_count),
        out_shape=[jax.ShapeDtypeStruct((vesicles, rows, nodes), BF16)] * 2
        + [jax.ShapeDtypeStruct((rank // 2, 2 * rank), F32)],
        in_specs=[far_off_spec()] * 4 + [whole_spec()] * (2 * (col_count - 1)),
        out_specs=[whole_spec()] * 3,
        scratch_shapes=[
            pltpu.SMEM((1, vesicles), jnp.int32),
            pltpu.VMEM((2 * vesicles, nodes), F32),
            pltpu.VMEM((2, sources), BF16),
            pltpu.VMEM((col_count, rows, sources), BF16),
            pltpu.VMEM((col_count, 8, sources), F32),
            pltpu.VMEM((col_count, sources, DEPTH), BF16),
            pltpu.VMEM((4, vesicles * DEPTH, nodes), F32),
            pltpu.VMEM((sources, 3 * nodes), BF16),
            pltpu.VMEM((sources, 3 * nodes), BF16),
            pltpu.VMEM((rows, rows), F32),
            pltpu.SemaphoreType.DMA((4,))],
        compiler_params=params(32),
        cost_estimate=pl.CostEstimate(flops=10**10, bytes_accessed=10**7, transcendentals=10**7),
    )(near_by(far_range.reshape(1, vesicles)), flat_here, basis_here, nodes_here, *pieces)
    gram = sum_over(gram, "clu", step_groups(clu_count, True))
    gram = sum_over(gram, "col", step_groups(col_count, False))

    scale_factor = -math.sqrt(2.0 * nodes * vesicles * clu_count * col_count)
    group = 8 if vesicles % 8 == 0 else vesicles
    block = pl.BlockSpec((group, rows, nodes), lambda i: (i, 0, 0))
    new_basis = pl.pallas_call(
        functools.partial(basis_kernel, scale_factor),
        out_shape=jax.ShapeDtypeStruct((vesicles, rows, nodes), F32),
        grid=(vesicles // group,),
        in_specs=[whole_spec()] + [block] * 2,
        out_specs=block,
        scratch_shapes=[pltpu.VMEM((rows, 3 * rows), BF16)],
        compiler_params=params(16),
        cost_estimate=pl.CostEstimate(flops=10**9, bytes_accessed=10**7, transcendentals=0),
    )(gram, high, low)

    return (force.reshape(vesicles, 2, nodes), near.reshape(vesicles, 2, nodes),
            new_basis.reshape(vesicles, rank, 2, nodes))


def solution(mesh):
    both = ("clu", "col")
    placed = (
        P(both, None, None), P(both, None), P(both), P(both, None), P(both, None), P(both),
        P(both, None), P(None, "col"), P(None, "col"),
    )
    return jax.shard_map(
        per_device,
        mesh=mesh,
        in_specs=placed,
        out_specs=(P(both, None, None), P(both, None, None), P(both, None, None, None)),
        check_vma=False,
    )
```

```python
import functools
import math

import jax
import jax.numpy as jnp
import numpy as np
from jax import lax
from jax.experimental import pallas as pl
from jax.experimental.pallas import tpu as pltpu
from jax.sharding import PartitionSpec as P

EPS_SQUARED = 0.01
F32 = jnp.float32
BF16 = jnp.bfloat16
HIGHEST = lax.Precision.HIGHEST
BLOCK = 8
MIB = 1 << 20

NT = (((1,), (1,)), ((), ()))
NN = (((1,), (0,)), ((), ()))


def spectral_tables(node_count):
    half = node_count // 2
    j = np.arange(node_count)[:, None]
    k = np.arange(half + 1)[None, :]
    phase = (j * k % node_count) * (2.0 * math.pi / node_count)
    c, s = np.cos(phase), np.sin(phase)
    k = np.arange(half + 1, dtype=np.float64)
    inside = (k > 0) & (k < half)
    u = np.where(inside, 2.0 * k / half, 0.0)
    w = np.where(inside, 2.0 * (k / half) ** 4, np.where(k == half, 1.0, 0.0))
    derivative = ((c * u) @ s.T - (s * u) @ c.T) / node_count
    bending_table = ((c * w) @ c.T + (s * w) @ s.T) / node_count
    return derivative.T.astype(np.float32), bending_table.T.astype(np.float32)


def iota(shape, axis):
    return lax.broadcasted_iota(jnp.int32, shape, axis)


def dot(a, b, dims=NN, precision=None):
    return lax.dot_general(a, b, dims, precision=precision, preferred_element_type=F32)


def reciprocal(x):
    return pl.reciprocal(x, approx=True)


def fetch(sources, targets, sems):
    copies = [pltpu.make_async_copy(s, t, sems.at[i])
              for i, (s, t) in enumerate(zip(sources, targets))]
    for copy in copies:
        copy.start()
    for copy in copies:
        copy.wait()


def piece_kernel(own_in, nodes_in, sent_ref, own_ref, nodes_ref, sems):
    fetch([own_in, nodes_in], [own_ref, nodes_ref], sems)
    half = own_ref.shape[0] // 2
    core = lax.rem(lax.axis_index("clu"), 2)
    mine = own_ref[pl.ds(pl.multiple_of(core * half, half), half), :]
    spots = nodes_ref[...].astype(F32)
    lanes = sent_ref.shape[1]
    columns = own_ref.shape[1] // lanes
    for c in range(columns):
        sent_ref[c * half:(c + 1) * half] = mine[:, c * lanes:(c + 1) * lanes]
    spots = jnp.concatenate([spots[:, c * lanes:(c + 1) * lanes] for c in range(columns)], axis=0)
    tail = sent_ref.shape[0] - columns * half
    spots = jnp.concatenate([spots, jnp.zeros((tail - 2 * columns, lanes), F32)], axis=0)
    sent_ref[columns * half:] = spots.astype(BF16)


def cube_place(destination, own, count):
    relative = jnp.bitwise_xor(destination, own)
    place = jnp.zeros_like(relative)
    bit = 1
    while bit < count:
        place = 2 * place + jnp.bitwise_and(relative, bit) // bit
        bit *= 2
    return place


def cube_exchange(kept, leaving, axis):
    count = lax.axis_size(axis)
    assert power_of_two(count)
    held = [kept]
    bit = 1
    while True:
        held.append(lax.ppermute(leaving, axis, partners(count, bit)))
        bit *= 2
        if bit >= count:
            return held
        span = count // bit
        tails = []
        for h, part in enumerate(held):
            cut = part.reshape(-1, span, *part.shape[-2:])
            tails.append(cut[:, span // 2:].reshape(-1, *part.shape[-2:]))
            held[h] = cut[:, :span // 2].reshape(-1, *part.shape[-2:])
        leaving = jnp.concatenate(tails, axis=0)


def force_kernel(clu_count, *refs):
    sources, targets, sems = refs[:8], refs[11:19], refs[19]
    force_ref, kept_ref, leaving_ref = refs[8:11]
    fetch(sources, targets, sems)
    (pos_ref, ten_ref, bend_ref, order_ref, dest_ref, target_ref, deriv_ref, table_ref) = targets
    vesicles = ten_ref.shape[0]
    moves = target_ref.shape[1]
    x = pos_ref[pl.ds(0, vesicles, stride=2), :]
    y = pos_ref[pl.ds(1, vesicles, stride=2), :]
    rows = jnp.concatenate([x, y], axis=0)
    deriv = deriv_ref[...]
    tension = jnp.concatenate([ten_ref[...]] * 2, axis=0)
    eye = iota((vesicles, vesicles), 0) == iota((vesicles, vesicles), 1)
    bend = jnp.sum(jnp.where(eye, bend_ref[...], 0.0), axis=1, keepdims=True)
    bend = jnp.concatenate([bend] * 2, axis=0)
    slope = dot(rows, deriv, precision=HIGHEST)
    fourth = dot(rows, table_ref[...], precision=HIGHEST)
    force = dot(tension * slope, deriv, precision=HIGHEST) - bend * fourth
    force_x, force_y = force[:vesicles], force[vesicles:]
    force_ref[pl.ds(0, vesicles, stride=2), :] = force_x
    force_ref[pl.ds(1, vesicles, stride=2), :] = force_y

    slots = clu_count * BLOCK
    place = cube_place(dest_ref[...], lax.axis_index("clu"), clu_count)
    hot = (iota((clu_count, moves), 0) == place).astype(F32)
    earlier = (iota((moves, moves), 0) < iota((moves, moves), 1)).astype(F32)
    rank = jnp.sum(dot(hot, earlier) * hot, axis=0, keepdims=True).astype(jnp.int32)
    slot = place * BLOCK + rank
    pack = (iota((slots, moves), 0) == slot).astype(F32)
    pick = (iota((vesicles, moves), 0) == order_ref[:, :moves]).astype(F32)
    select = dot(pack, pick, NT)
    carried = jnp.concatenate([x, y, force_x, force_y], axis=1)
    packed = dot(select, carried, precision=HIGHEST)
    tag = jnp.sum(pack * (target_ref[...] + 1).astype(F32), axis=1, keepdims=True)
    tag = jnp.broadcast_to(tag, (slots, x.shape[1]))
    packed = jnp.concatenate([packed, tag], axis=1)
    packed = packed.reshape(clu_count, BLOCK, packed.shape[1])
    kept_ref[...] = packed[:clu_count // 2]
    leaving_ref[...] = packed[clu_count // 2:]


def near_kernel(slot_cap, piece_count, pos_ref, *refs):
    piece_refs = refs[:piece_count]
    before_ref, near_ref, arrived, aim_x, aim_y, speed_x, speed_y = refs[piece_count:]
    vesicles = pos_ref.shape[0] // 2
    nodes = pos_ref.shape[1]
    here = 0
    for ref in piece_refs:
        arrived[here:here + ref.shape[0]] = ref[...]
        here += ref.shape[0]
    pieces = arrived.shape[0]
    slots = pieces * BLOCK
    tag = arrived[:, :, 4 * nodes:].reshape(slots, nodes)[:, :vesicles]
    hot = (tag == (iota((slots, vesicles), 1) + 1).astype(F32)).astype(F32)
    x = pos_ref[pl.ds(0, vesicles, stride=2), :]
    y = pos_ref[pl.ds(1, vesicles, stride=2), :]
    aim_x[...] = dot(hot, x, precision=HIGHEST).reshape(pieces, BLOCK, nodes)
    aim_y[...] = dot(hot, y, precision=HIGHEST).reshape(pieces, BLOCK, nodes)
    chunk = 32 if nodes % 32 == 0 else nodes

    def fold(value):
        return jnp.sum(value.reshape(-1, 8, nodes), axis=0)

    def piece(k, _):
        data = arrived[k]
        turned = [data[:, c * nodes:(c + 1) * nodes].T for c in range(4)]
        tx, ty = aim_x[k], aim_y[k]
        rows_x, rows_y = [], []
        for h in range(slot_cap):
            logs_x = logs_y = pulls_x = pulls_y = jnp.zeros((8, nodes), F32)
            for start in range(0, nodes, chunk):
                sx, sy, fx, fy = [
                    jnp.broadcast_to(t[start:start + chunk, h:h + 1], (chunk, nodes))
                    for t in turned]
                dx = tx[h:h + 1] - sx
                dy = ty[h:h + 1] - sy
                spread = dx * dx + dy * dy + EPS_SQUARED
                logs = jnp.log(spread)
                along = (dx * fx + dy * fy) * reciprocal(spread)
                logs_x, logs_y = logs_x + fold(logs * fx), logs_y + fold(logs * fy)
                pulls_x, pulls_y = pulls_x + fold(dx * along), pulls_y + fold(dy * along)
            rows_x.append(jnp.sum(pulls_x - 0.5 * logs_x, axis=0, keepdims=True))
            rows_y.append(jnp.sum(pulls_y - 0.5 * logs_y, axis=0, keepdims=True))
        rows_x += [jnp.zeros((1, nodes), F32)] * (BLOCK - slot_cap)
        rows_y += [jnp.zeros((1, nodes), F32)] * (BLOCK - slot_cap)
        speed_x[k] = jnp.concatenate(rows_x, axis=0)
        speed_y[k] = jnp.concatenate(rows_y, axis=0)
        return 0

    lax.fori_loop(0, pieces, piece, 0)
    turned_hot = hot.T
    near_x = dot(turned_hot, speed_x[...].reshape(slots, nodes), precision=HIGHEST) / nodes
    near_y = dot(turned_hot, speed_y[...].reshape(slots, nodes), precision=HIGHEST) / nodes
    if before_ref is not None:
        near_x = near_x + before_ref[pl.ds(0, vesicles, stride=2), :]
        near_y = near_y + before_ref[pl.ds(1, vesicles, stride=2), :]
    near_ref[pl.ds(0, vesicles, stride=2), :] = near_x
    near_ref[pl.ds(1, vesicles, stride=2), :] = near_y


def near_start(slot_cap, piece_count, pos_ref, *refs):
    near_kernel(slot_cap, piece_count, pos_ref, *refs[:piece_count], None, *refs[piece_count:])


def near_part(flat, pieces, before, slot_cap):
    vesicles, nodes = flat.shape[0] // 2, flat.shape[1]
    count = sum(p.shape[0] for p in pieces)
    operands = [flat, *pieces] + ([] if before is None else [before])
    return pl.pallas_call(
        functools.partial(near_start if before is None else near_kernel, slot_cap, len(pieces)),
        out_shape=jax.ShapeDtypeStruct((2 * vesicles, nodes), F32),
        in_specs=[whole_spec()] * len(operands),
        out_specs=whole_spec(),
        scratch_shapes=[pltpu.VMEM((count, BLOCK, 5 * nodes), F32)]
        + [pltpu.VMEM((count, BLOCK, nodes), F32)] * 4,
        compiler_params=params(16),
        cost_estimate=pl.CostEstimate(
            flops=10**9, bytes_accessed=10**7, transcendentals=10**6),
    )(*operands)


def far_kernel(col_count, range_in, pos_in, own_in, nodes_in, *refs):
    count = 2 * (col_count - 1)
    piece_refs = refs[:count]
    (high_ref, low_ref, gram_ref, range_ref, pos_ref, own_nodes, own_rows, basis, spots, wide,
     buffer_0, buffer_1, sums, sems) = refs[count:]
    vesicles = pos_ref.shape[0] // 2
    nodes = pos_ref.shape[1]
    rank, sources = own_rows.shape[0] // 2, own_rows.shape[1]
    rows = 2 * rank
    core, col = lax.rem(lax.axis_index("clu"), 2), lax.axis_index("col")
    fetch([range_in, pos_in, nodes_in, own_in], [range_ref, pos_ref, own_nodes, own_rows], sems)
    basis[col, :, :sources] = own_rows[:rank]
    basis[col, :, sources:] = own_rows[rank:]
    spots[col, 0:2] = own_nodes[...].astype(F32)
    for k in range(1, col_count):
        where = origin(col, k, col_count)
        mine, other = piece_refs[2 * k - 2], piece_refs[2 * k - 1]
        columns = sources // nodes
        ends = mine[columns * rank:].astype(F32)
        for c in range(columns):
            lanes = slice(c * nodes, (c + 1) * nodes)
            from_rows = slice(c * rank, (c + 1) * rank)
            for ref, part in ((mine, core), (other, 1 - core)):
                there = pl.multiple_of(part * sources + c * nodes, nodes)
                basis[where, :, pl.ds(there, nodes)] = ref[from_rows]
            spots[where, 0:2, lanes] = ends[2 * c:2 * c + 2]
    for r in range(col_count):
        turned = spots[r].T
        for c in range(2):
            wide[r, c] = jnp.broadcast_to(turned[:, c:c + 1], (sources, nodes))
    sums[...] = jnp.zeros_like(sums)

    chunk = 32 if sources % 32 == 0 else sources

    def evaluate(v, buffer, part, parts):
        r = range_ref[0, v]
        tx = pos_ref[pl.ds(2 * v, 1), :]
        ty = pos_ref[pl.ds(2 * v + 1, 1), :]
        for start in range(part * sources // parts, (part + 1) * sources // parts, chunk):
            dx = tx - wide[r, 0, start:start + chunk]
            dy = ty - wide[r, 1, start:start + chunk]
            spread = dx * dx + dy * dy + EPS_SQUARED
            log_part = -0.5 * jnp.log(spread)
            inverse = reciprocal(spread)
            dxr = dx * inverse
            upper = slice(start, start + chunk)
            lower = slice(sources + start, sources + start + chunk)
            cross = (dy * dxr).astype(BF16)
            buffer[upper, :nodes] = (log_part + dx * dxr).astype(BF16)
            buffer[upper, nodes:] = cross
            buffer[lower, :nodes] = cross
            buffer[lower, nodes:] = (log_part + dy * (dy * inverse)).astype(BF16)

    def step(v, now, following):
        later = jnp.minimum(v + 1, vesicles - 1)
        product = dot(basis[range_ref[0, v]], now[...])
        evaluate(later, following, 0, 2)
        high = product.astype(BF16)
        high_ref[v] = high
        low_ref[v] = (product - high.astype(F32)).astype(BF16)
        evaluate(later, following, 1, 2)

    def add_gram(v):
        both = jnp.concatenate([
            jnp.concatenate([ref[v], ref[v + 1]], axis=1) for ref in (high_ref, low_ref)], axis=0)
        sums[...] += dot(both, both, NT)

    evaluate(0, buffer_0, 0, 1)
    high_ref[0:2] = jnp.zeros((2, rank, 2 * nodes), BF16)
    low_ref[0:2] = jnp.zeros((2, rank, 2 * nodes), BF16)

    def pair(i, _):
        v = 2 * i
        add_gram(jnp.maximum(v - 2, 0))
        step(v, buffer_0, buffer_1)
        step(v + 1, buffer_1, buffer_0)
        return 0

    lax.fori_loop(0, vesicles // 2, pair, 0)
    add_gram(vesicles - 2)
    total = sums[...]
    gram = total[:rank, :rank] + total[rank:, rank:] + (total[:rank, rank:] + total[rank:, :rank])
    gram_ref[...] = jnp.concatenate([gram[:rank // 2], gram[rank // 2:]], axis=1)


def lower_inverse(gram):
    size = gram.shape[0]
    eye = (iota((size, size), 0) == iota((size, size), 1)).astype(F32)
    rest = jnp.concatenate([gram, eye], axis=1)
    done = []
    step = 8
    for start in range(0, size, step):
        height = size - start
        columns = [jnp.broadcast_to(rest[:, start + j:start + j + 1], (height, 2 * size))
                   for j in range(step)]
        row_number = iota((height, 2 * size), 0)
        scale = jnp.zeros((step, 2 * size), F32)
        for j in range(step):
            column = columns[j]
            pivot = column[j:j + 1]
            factor = jnp.where(row_number > j, column * reciprocal(pivot), 0.0)
            for later in range(j + 1, step):
                columns[later] = columns[later] - factor * column[later:later + 1]
            rest = rest - factor * rest[j:j + 1]
            root = lax.rsqrt(pivot)
            root = root * (1.5 - 0.5 * pivot * root * root)
            scale = jnp.where(row_number[:step] == j, root, scale)
        done.append(rest[:step] * scale)
        rest = rest[step:]
    return jnp.concatenate(done, axis=0)[:, size:]


def basis_kernel(scale_factor, gram_ref, high_ref, low_ref, _, out_ref, weight):
    rank, nodes = high_ref.shape[1], high_ref.shape[2] // 2

    @pl.when(pl.program_id(0) == 0)
    def _():
        folded = gram_ref[...]
        gram = jnp.concatenate([folded[:, :rank], folded[:, rank:]], axis=0)
        inverse = lower_inverse(gram) * scale_factor
        high = inverse.astype(BF16)
        low = (inverse - high.astype(F32)).astype(BF16)
        weight[...] = jnp.concatenate([high, high, low], axis=1)

    w = weight[...]
    for v in range(high_ref.shape[0]):
        fresh = dot(w, jnp.concatenate([high_ref[v], low_ref[v], high_ref[v]], axis=0))
        for d in range(2):
            out_ref[v, pl.ds(d, rank, stride=2), :] = fresh[:, d * nodes:(d + 1) * nodes]


def whole_spec():
    return pl.BlockSpec(memory_space=pltpu.VMEM)


def far_off_spec():
    return pl.BlockSpec(memory_space=pltpu.HBM)


def params(mib):
    return pltpu.CompilerParams(vmem_limit_bytes=mib * MIB)


def power_of_two(count):
    return count & (count - 1) == 0


def partners(count, step):
    if power_of_two(count):
        return [(i, i ^ step) for i in range(count)]
    return [(i, (i + step) % count) for i in range(count)]


def origin(index, step, count):
    if power_of_two(count):
        return jnp.bitwise_xor(index, step)
    return lax.rem(index - step + count, count)


def step_groups(count, single_first):
    if not power_of_two(count):
        return [list(range(1, count))]
    groups, bit = [], 1
    if single_first and count > 1:
        groups, bit = [[1]], 2
    while bit < count:
        groups.append([bit] if 2 * bit >= count else [bit, 2 * bit, 3 * bit])
        bit *= 4
    return groups


def add_kernel(first, *refs):
    total = first[...]
    for ref in refs[:-2]:
        total = total + ref[...]
    refs[-1][...] = total


def add_after(terms, other):
    return pl.pallas_call(
        add_kernel,
        out_shape=jax.ShapeDtypeStruct(terms[0].shape, terms[0].dtype),
        in_specs=[whole_spec()] * len(terms) + [far_off_spec()],
        out_specs=whole_spec(),
        compiler_params=params(16),
        cost_estimate=pl.CostEstimate(flops=10**4, bytes_accessed=10**5, transcendentals=0),
    )(*terms, other)


def sum_over(value, axis, groups, other=None):
    count = lax.axis_size(axis)
    for g, steps in enumerate(groups):
        terms = [value] + [lax.ppermute(value, axis, partners(count, k)) for k in steps]
        if other is not None and g == len(groups) - 1:
            value = add_after(terms, other)
        else:
            value = sum(terms[1:], value)
    return value


def per_device(positions, tension, bending, moved_order, move_destination, move_target, far_range,
               old_basis, source_nodes):
    vesicles, _, nodes = positions.shape
    rows, sources = old_basis.shape
    rank = rows // 2
    clu_count, col_count = lax.axis_size("clu"), lax.axis_size("col")
    moves = move_target.shape[0]
    slot_cap = 2 * ((moves + clu_count - 1) // clu_count)
    flat = positions.reshape(2 * vesicles, nodes)

    columns = sources // nodes
    sent_rows = columns * rank + (2 * columns + 15) // 16 * 16
    deriv, table = spectral_tables(nodes)
    near_by = functools.partial(pltpu.with_memory_space_constraint, memory_space=pltpu.HBM)
    basis_here, nodes_here, flat_here = near_by(old_basis), near_by(source_nodes), near_by(flat)
    sent = pl.pallas_call(
        piece_kernel,
        out_shape=jax.ShapeDtypeStruct((sent_rows, nodes), BF16),
        in_specs=[far_off_spec()] * 2,
        out_specs=whole_spec(),
        scratch_shapes=[pltpu.VMEM(old_basis.shape, BF16), pltpu.VMEM(source_nodes.shape, BF16),
                        pltpu.SemaphoreType.DMA((2,))],
        compiler_params=params(16),
        cost_estimate=pl.CostEstimate(flops=10**5, bytes_accessed=10**5, transcendentals=0),
    )(basis_here, nodes_here)

    operands = [flat, tension, bending.reshape(1, vesicles), moved_order,
                move_destination.reshape(1, moves), move_target.reshape(1, moves),
                jnp.asarray(deriv), jnp.asarray(table)]
    operands = [flat_here] + [near_by(o) for o in operands[1:]]
    force, kept, leaving = pl.pallas_call(
        functools.partial(force_kernel, clu_count),
        out_shape=[jax.ShapeDtypeStruct((2 * vesicles, nodes), F32),
                   *[jax.ShapeDtypeStruct((clu_count // 2, BLOCK, 5 * nodes), F32)] * 2],
        in_specs=[far_off_spec()] * len(operands),
        out_specs=[whole_spec()] * 3,
        scratch_shapes=[pltpu.VMEM(o.shape, o.dtype) for o in operands]
        + [pltpu.SemaphoreType.DMA((len(operands),))],
        compiler_params=params(16),
        cost_estimate=pl.CostEstimate(flops=10**8, bytes_accessed=10**6, transcendentals=0),
    )(*operands)

    moved_halves = [lax.ppermute(sent, "col", partners(col_count, k)) for k in range(1, col_count)]
    arrived = cube_exchange(kept, leaving, "clu")
    pieces = []
    for mine in moved_halves:
        pieces += [mine, lax.ppermute(mine, "clu", [(i, i ^ 1) for i in range(clu_count)])]

    near_first = near_part(flat, arrived[:-1], None, slot_cap)
    near = near_part(flat, arrived[-1:], near_first, slot_cap)

    high, low, gram = pl.pallas_call(
        functools.partial(far_kernel, col_count),
        out_shape=[jax.ShapeDtypeStruct((vesicles, rank, 2 * nodes), BF16)] * 2
        + [jax.ShapeDtypeStruct((rank // 2, 2 * rank), F32)],
        in_specs=[far_off_spec()] * 4 + [whole_spec()] * (2 * (col_count - 1)),
        out_specs=[whole_spec()] * 3,
        scratch_shapes=[
            pltpu.SMEM((1, vesicles), jnp.int32),
            pltpu.VMEM((2 * vesicles, nodes), F32),
            pltpu.VMEM((2, sources), BF16),
            pltpu.VMEM((rows, sources), BF16),
            pltpu.VMEM((col_count, rank, 2 * sources), BF16),
            pltpu.VMEM((col_count, 8, sources), F32),
            pltpu.VMEM((col_count, 2, sources, nodes), F32),
            pltpu.VMEM((2 * sources, 2 * nodes), BF16),
            pltpu.VMEM((2 * sources, 2 * nodes), BF16),
            pltpu.VMEM((rows, rows), F32),
            pltpu.SemaphoreType.DMA((4,))],
        compiler_params=params(32),
        cost_estimate=pl.CostEstimate(flops=10**10, bytes_accessed=10**7, transcendentals=10**7),
    )(near_by(far_range.reshape(1, vesicles)), flat_here, basis_here, nodes_here, *pieces)
    gram = sum_over(gram, "clu", step_groups(clu_count, True), near_first)
    gram = sum_over(gram, "col", step_groups(col_count, False))

    scale_factor = math.sqrt(2.0 * nodes * vesicles * clu_count * col_count)
    group = 8 if vesicles % 8 == 0 else vesicles
    block = pl.BlockSpec((group, rows, nodes), lambda i: (i, 0, 0))
    held = pl.BlockSpec((group, rank, 2 * nodes), lambda i: (i, 0, 0))
    new_basis = pl.pallas_call(
        functools.partial(basis_kernel, scale_factor),
        out_shape=jax.ShapeDtypeStruct((vesicles, rows, nodes), F32),
        grid=(vesicles // group,),
        in_specs=[whole_spec(), held, held, far_off_spec()],
        out_specs=block,
        scratch_shapes=[pltpu.VMEM((rank, 3 * rank), BF16)],
        compiler_params=params(16),
        cost_estimate=pl.CostEstimate(flops=10**9, bytes_accessed=10**7, transcendentals=0),
    )(gram, high, low, near)

    return (force.reshape(vesicles, 2, nodes), near.reshape(vesicles, 2, nodes),
            new_basis.reshape(vesicles, rank, 2, nodes))


def solution(mesh):
    both = ("clu", "col")
    placed = (
        P(both, None, None), P(both, None), P(both), P(both, None), P(both, None), P(both),
        P(both, None), P(None, "col"), P(None, "col"),
    )
    return jax.shard_map(
        per_device,
        mesh=mesh,
        in_specs=placed,
        out_specs=(P(both, None, None), P(both, None, None), P(both, None, None, None)),
        check_vma=False,
    )
```

```python
import functools
import math

import jax
import jax.numpy as jnp
import numpy as np
from jax import lax
from jax.experimental import pallas as pl
from jax.experimental.pallas import tpu as pltpu
from jax.sharding import PartitionSpec as P

EPS_SQUARED = 0.01
F32 = jnp.float32
BF16 = jnp.bfloat16
HIGHEST = lax.Precision.HIGHEST
BLOCK = 8
MIB = 1 << 20

NT = (((1,), (1,)), ((), ()))
NN = (((1,), (0,)), ((), ()))


def spectral_tables(node_count):
    half = node_count // 2
    j = np.arange(node_count)[:, None]
    k = np.arange(half + 1)[None, :]
    phase = (j * k % node_count) * (2.0 * math.pi / node_count)
    c, s = np.cos(phase), np.sin(phase)
    k = np.arange(half + 1, dtype=np.float64)
    inside = (k > 0) & (k < half)
    u = np.where(inside, 2.0 * k / half, 0.0)
    w = np.where(inside, 2.0 * (k / half) ** 4, np.where(k == half, 1.0, 0.0))
    derivative = ((c * u) @ s.T - (s * u) @ c.T) / node_count
    bending_table = ((c * w) @ c.T + (s * w) @ s.T) / node_count
    return derivative.T.astype(np.float32), bending_table.T.astype(np.float32)


def iota(shape, axis):
    return lax.broadcasted_iota(jnp.int32, shape, axis)


def dot(a, b, dims=NN, precision=None):
    return lax.dot_general(a, b, dims, precision=precision, preferred_element_type=F32)


def reciprocal(x):
    return pl.reciprocal(x, approx=True)


def fetch(sources, targets, sems):
    copies = [pltpu.make_async_copy(s, t, sems.at[i])
              for i, (s, t) in enumerate(zip(sources, targets))]
    for copy in copies:
        copy.start()
    for copy in copies:
        copy.wait()


def piece_kernel(own_in, nodes_in, sent_ref, own_ref, nodes_ref, sems):
    fetch([own_in, nodes_in], [own_ref, nodes_ref], sems)
    half = own_ref.shape[0] // 2
    core = lax.rem(lax.axis_index("clu"), 2)
    mine = own_ref[pl.ds(pl.multiple_of(core * half, half), half), :]
    spots = nodes_ref[...].astype(F32)
    lanes = sent_ref.shape[1]
    columns = own_ref.shape[1] // lanes
    for c in range(columns):
        sent_ref[c * half:(c + 1) * half] = mine[:, c * lanes:(c + 1) * lanes]
    spots = jnp.concatenate([spots[:, c * lanes:(c + 1) * lanes] for c in range(columns)], axis=0)
    tail = sent_ref.shape[0] - columns * half
    spots = jnp.concatenate([spots, jnp.zeros((tail - 2 * columns, lanes), F32)], axis=0)
    sent_ref[columns * half:] = spots.astype(BF16)


def cube_place(destination, own, count):
    relative = jnp.bitwise_xor(destination, own)
    place = jnp.zeros_like(relative)
    bit = 1
    while bit < count:
        place = 2 * place + jnp.bitwise_and(relative, bit) // bit
        bit *= 2
    return place


def cube_exchange(kept, leaving, axis):
    count = lax.axis_size(axis)
    assert power_of_two(count)
    held = [kept]
    bit = 1
    while True:
        held.append(lax.ppermute(leaving, axis, partners(count, bit)))
        bit *= 2
        if bit >= count:
            return held
        span = count // bit
        tails = []
        for h, part in enumerate(held):
            cut = part.reshape(-1, span, *part.shape[-2:])
            tails.append(cut[:, span // 2:].reshape(-1, *part.shape[-2:]))
            held[h] = cut[:, :span // 2].reshape(-1, *part.shape[-2:])
        leaving = jnp.concatenate(tails, axis=0)


def force_kernel(clu_count, *refs):
    sources, targets, sems = refs[:8], refs[11:19], refs[19]
    force_ref, kept_ref, leaving_ref = refs[8:11]
    fetch(sources, targets, sems)
    (pos_ref, ten_ref, bend_ref, order_ref, dest_ref, target_ref, deriv_ref, table_ref) = targets
    vesicles = ten_ref.shape[0]
    moves = target_ref.shape[1]
    x = pos_ref[pl.ds(0, vesicles, stride=2), :]
    y = pos_ref[pl.ds(1, vesicles, stride=2), :]
    rows = jnp.concatenate([x, y], axis=0)
    deriv = deriv_ref[...]
    tension = jnp.concatenate([ten_ref[...]] * 2, axis=0)
    eye = iota((vesicles, vesicles), 0) == iota((vesicles, vesicles), 1)
    bend = jnp.sum(jnp.where(eye, bend_ref[...], 0.0), axis=1, keepdims=True)
    bend = jnp.concatenate([bend] * 2, axis=0)
    slope = dot(rows, deriv, precision=HIGHEST)
    fourth = dot(rows, table_ref[...], precision=HIGHEST)
    force = dot(tension * slope, deriv, precision=HIGHEST) - bend * fourth
    force_x, force_y = force[:vesicles], force[vesicles:]
    force_ref[pl.ds(0, vesicles, stride=2), :] = force_x
    force_ref[pl.ds(1, vesicles, stride=2), :] = force_y

    slots = clu_count * BLOCK
    place = cube_place(dest_ref[...], lax.axis_index("clu"), clu_count)
    hot = (iota((clu_count, moves), 0) == place).astype(F32)
    earlier = (iota((moves, moves), 0) < iota((moves, moves), 1)).astype(F32)
    rank = jnp.sum(dot(hot, earlier) * hot, axis=0, keepdims=True).astype(jnp.int32)
    slot = place * BLOCK + rank
    pack = (iota((slots, moves), 0) == slot).astype(F32)
    pick = (iota((vesicles, moves), 0) == order_ref[:, :moves]).astype(F32)
    select = dot(pack, pick, NT)
    carried = jnp.concatenate([x, y, force_x, force_y], axis=1)
    packed = dot(select, carried, precision=HIGHEST)
    tag = jnp.sum(pack * (target_ref[...] + 1).astype(F32), axis=1, keepdims=True)
    tag = jnp.broadcast_to(tag, (slots, x.shape[1]))
    packed = jnp.concatenate([packed, tag], axis=1)
    packed = packed.reshape(clu_count, BLOCK, packed.shape[1])
    kept_ref[...] = packed[:clu_count // 2]
    leaving_ref[...] = packed[clu_count // 2:]


def near_kernel(slot_cap, piece_count, pos_ref, *refs):
    piece_refs = refs[:piece_count]
    before_ref, near_ref, arrived, aim_x, aim_y, speed_x, speed_y = refs[piece_count:]
    vesicles = pos_ref.shape[0] // 2
    nodes = pos_ref.shape[1]
    here = 0
    for ref in piece_refs:
        arrived[here:here + ref.shape[0]] = ref[...]
        here += ref.shape[0]
    pieces = arrived.shape[0]
    slots = pieces * BLOCK
    tag = arrived[:, :, 4 * nodes:].reshape(slots, nodes)[:, :vesicles]
    hot = (tag == (iota((slots, vesicles), 1) + 1).astype(F32)).astype(F32)
    x = pos_ref[pl.ds(0, vesicles, stride=2), :]
    y = pos_ref[pl.ds(1, vesicles, stride=2), :]
    aim_x[...] = dot(hot, x, precision=HIGHEST).reshape(pieces, BLOCK, nodes)
    aim_y[...] = dot(hot, y, precision=HIGHEST).reshape(pieces, BLOCK, nodes)
    chunk = 32 if nodes % 32 == 0 else nodes

    def fold(value):
        return jnp.sum(value.reshape(-1, 8, nodes), axis=0)

    def piece(k, _):
        data = arrived[k]
        turned = [data[:, c * nodes:(c + 1) * nodes].T for c in range(4)]
        tx, ty = aim_x[k], aim_y[k]
        rows_x, rows_y = [], []
        for h in range(slot_cap):
            logs_x = logs_y = pulls_x = pulls_y = jnp.zeros((8, nodes), F32)
            for start in range(0, nodes, chunk):
                sx, sy, fx, fy = [
                    jnp.broadcast_to(t[start:start + chunk, h:h + 1], (chunk, nodes))
                    for t in turned]
                dx = tx[h:h + 1] - sx
                dy = ty[h:h + 1] - sy
                spread = dx * dx + dy * dy + EPS_SQUARED
                logs = jnp.log(spread)
                along = (dx * fx + dy * fy) * reciprocal(spread)
                logs_x, logs_y = logs_x + fold(logs * fx), logs_y + fold(logs * fy)
                pulls_x, pulls_y = pulls_x + fold(dx * along), pulls_y + fold(dy * along)
            rows_x.append(jnp.sum(pulls_x - 0.5 * logs_x, axis=0, keepdims=True))
            rows_y.append(jnp.sum(pulls_y - 0.5 * logs_y, axis=0, keepdims=True))
        rows_x += [jnp.zeros((1, nodes), F32)] * (BLOCK - slot_cap)
        rows_y += [jnp.zeros((1, nodes), F32)] * (BLOCK - slot_cap)
        speed_x[k] = jnp.concatenate(rows_x, axis=0)
        speed_y[k] = jnp.concatenate(rows_y, axis=0)
        return 0

    lax.fori_loop(0, pieces, piece, 0)
    turned_hot = hot.T
    near_x = dot(turned_hot, speed_x[...].reshape(slots, nodes), precision=HIGHEST) / nodes
    near_y = dot(turned_hot, speed_y[...].reshape(slots, nodes), precision=HIGHEST) / nodes
    if before_ref is not None:
        near_x = near_x + before_ref[pl.ds(0, vesicles, stride=2), :]
        near_y = near_y + before_ref[pl.ds(1, vesicles, stride=2), :]
    near_ref[pl.ds(0, vesicles, stride=2), :] = near_x
    near_ref[pl.ds(1, vesicles, stride=2), :] = near_y


def near_start(slot_cap, piece_count, pos_ref, *refs):
    near_kernel(slot_cap, piece_count, pos_ref, *refs[:piece_count], None, *refs[piece_count:])


def near_part(flat, pieces, before, slot_cap):
    vesicles, nodes = flat.shape[0] // 2, flat.shape[1]
    count = sum(p.shape[0] for p in pieces)
    operands = [flat, *pieces] + ([] if before is None else [before])
    return pl.pallas_call(
        functools.partial(near_start if before is None else near_kernel, slot_cap, len(pieces)),
        out_shape=jax.ShapeDtypeStruct((2 * vesicles, nodes), F32),
        in_specs=[whole_spec()] * len(operands),
        out_specs=whole_spec(),
        scratch_shapes=[pltpu.VMEM((count, BLOCK, 5 * nodes), F32)]
        + [pltpu.VMEM((count, BLOCK, nodes), F32)] * 4,
        compiler_params=params(16),
        cost_estimate=pl.CostEstimate(
            flops=10**9, bytes_accessed=10**7, transcendentals=10**6),
    )(*operands)


def far_kernel(col_count, range_in, pos_in, own_in, nodes_in, *refs):
    count = 2 * (col_count - 1)
    piece_refs = refs[:count]
    (high_ref, low_ref, gram_ref, range_ref, pos_ref, own_nodes, own_rows, basis, spots, wide,
     sums, sems) = refs[count:]
    vesicles = pos_ref.shape[0] // 2
    nodes = pos_ref.shape[1]
    rank, sources = own_rows.shape[0] // 2, own_rows.shape[1]
    rows = 2 * rank
    core, col = lax.rem(lax.axis_index("clu"), 2), lax.axis_index("col")
    fetch([range_in, pos_in, nodes_in, own_in], [range_ref, pos_ref, own_nodes, own_rows], sems)
    basis[col, :, :sources] = own_rows[:rank]
    basis[col, :, sources:] = own_rows[rank:]
    spots[col, 0:2] = own_nodes[...].astype(F32)
    for k in range(1, col_count):
        where = origin(col, k, col_count)
        mine, other = piece_refs[2 * k - 2], piece_refs[2 * k - 1]
        columns = sources // nodes
        ends = mine[columns * rank:].astype(F32)
        for c in range(columns):
            lanes = slice(c * nodes, (c + 1) * nodes)
            from_rows = slice(c * rank, (c + 1) * rank)
            for ref, part in ((mine, core), (other, 1 - core)):
                there = pl.multiple_of(part * sources + c * nodes, nodes)
                basis[where, :, pl.ds(there, nodes)] = ref[from_rows]
            spots[where, 0:2, lanes] = ends[2 * c:2 * c + 2]
    for r in range(col_count):
        turned = spots[r].T
        for c in range(2):
            wide[r, c] = jnp.broadcast_to(turned[:, c:c + 1], (sources, nodes))
    sums[...] = jnp.zeros_like(sums)

    chunk = 32 if sources % 32 == 0 else sources
    depth = 256 if sources % 256 == 0 else sources

    def evaluate(v, start):
        r = range_ref[0, v]
        tx = pos_ref[pl.ds(2 * v, 1), :]
        ty = pos_ref[pl.ds(2 * v + 1, 1), :]
        dx = tx - wide[r, 0, start:start + chunk]
        dy = ty - wide[r, 1, start:start + chunk]
        spread = dx * dx + dy * dy + EPS_SQUARED
        log_part = -0.5 * jnp.log(spread)
        inverse = reciprocal(spread)
        dxr = dx * inverse
        return ((log_part + dx * dxr).astype(BF16), (dy * dxr).astype(BF16),
                (log_part + dy * (dy * inverse)).astype(BF16))

    def sketch(v):
        r = range_ref[0, v]
        total = None
        for start in range(0, sources, depth):
            ff, fs, ss = [jnp.concatenate(p, axis=0) for p in zip(
                *[evaluate(v, start + c) for c in range(0, depth, chunk)])]
            part = dot(basis[r, :, start:start + depth], jnp.concatenate([ff, fs], axis=1))
            part += dot(basis[r, :, sources + start:sources + start + depth],
                        jnp.concatenate([fs, ss], axis=1))
            total = part if total is None else total + part
        return total

    def pair_gram(v):
        both = jnp.concatenate([
            jnp.concatenate([ref[v], ref[v + 1]], axis=1) for ref in (high_ref, low_ref)], axis=0)
        return dot(both, both, NT)

    high_ref[0:2] = jnp.zeros((2, rank, 2 * nodes), BF16)
    low_ref[0:2] = jnp.zeros((2, rank, 2 * nodes), BF16)

    def pair(i, _):
        v = 2 * i
        before = pair_gram(jnp.maximum(v - 2, 0))
        made = [sketch(v), sketch(v + 1)]
        sums[...] += before
        for c, value in enumerate(made):
            high = value.astype(BF16)
            high_ref[v + c] = high
            low_ref[v + c] = (value - high.astype(F32)).astype(BF16)
        return 0

    lax.fori_loop(0, vesicles // 2, pair, 0)
    sums[...] += pair_gram(vesicles - 2)
    total = sums[...]
    gram = total[:rank, :rank] + total[rank:, rank:] + (total[:rank, rank:] + total[rank:, :rank])
    gram_ref[...] = jnp.concatenate([gram[:rank // 2], gram[rank // 2:]], axis=1)


def lower_inverse(gram):
    size = gram.shape[0]
    eye = (iota((size, size), 0) == iota((size, size), 1)).astype(F32)
    rest = jnp.concatenate([gram, eye], axis=1)
    done = []
    step = 8
    for start in range(0, size, step):
        height = size - start
        columns = [jnp.broadcast_to(rest[:, start + j:start + j + 1], (height, 2 * size))
                   for j in range(step)]
        row_number = iota((height, 2 * size), 0)
        scale = jnp.zeros((step, 2 * size), F32)
        for j in range(step):
            column = columns[j]
            pivot = column[j:j + 1]
            factor = jnp.where(row_number > j, column * reciprocal(pivot), 0.0)
            for later in range(j + 1, step):
                columns[later] = columns[later] - factor * column[later:later + 1]
            rest = rest - factor * rest[j:j + 1]
            root = lax.rsqrt(pivot)
            root = root * (1.5 - 0.5 * pivot * root * root)
            scale = jnp.where(row_number[:step] == j, root, scale)
        done.append(rest[:step] * scale)
        rest = rest[step:]
    return jnp.concatenate(done, axis=0)[:, size:]


def basis_kernel(scale_factor, gram_ref, high_ref, low_ref, _, out_ref, weight):
    rank, nodes = high_ref.shape[1], high_ref.shape[2] // 2

    @pl.when(pl.program_id(0) == 0)
    def _():
        folded = gram_ref[...]
        gram = jnp.concatenate([folded[:, :rank], folded[:, rank:]], axis=0)
        inverse = lower_inverse(gram) * scale_factor
        high = inverse.astype(BF16)
        low = (inverse - high.astype(F32)).astype(BF16)
        weight[...] = jnp.concatenate([high, high, low], axis=1)

    w = weight[...]
    for v in range(high_ref.shape[0]):
        fresh = dot(w, jnp.concatenate([high_ref[v], low_ref[v], high_ref[v]], axis=0))
        for d in range(2):
            out_ref[v, pl.ds(d, rank, stride=2), :] = fresh[:, d * nodes:(d + 1) * nodes]


def whole_spec():
    return pl.BlockSpec(memory_space=pltpu.VMEM)


def far_off_spec():
    return pl.BlockSpec(memory_space=pltpu.HBM)


def params(mib):
    return pltpu.CompilerParams(vmem_limit_bytes=mib * MIB)


def power_of_two(count):
    return count & (count - 1) == 0


def partners(count, step):
    if power_of_two(count):
        return [(i, i ^ step) for i in range(count)]
    return [(i, (i + step) % count) for i in range(count)]


def origin(index, step, count):
    if power_of_two(count):
        return jnp.bitwise_xor(index, step)
    return lax.rem(index - step + count, count)


def step_groups(count, single_first):
    if not power_of_two(count):
        return [list(range(1, count))]
    groups, bit = [], 1
    if single_first and count > 1:
        groups, bit = [[1]], 2
    while bit < count:
        groups.append([bit] if 2 * bit >= count else [bit, 2 * bit, 3 * bit])
        bit *= 4
    return groups


def add_kernel(first, *refs):
    total = first[...]
    for ref in refs[:-2]:
        total = total + ref[...]
    refs[-1][...] = total


def add_after(terms, other):
    return pl.pallas_call(
        add_kernel,
        out_shape=jax.ShapeDtypeStruct(terms[0].shape, terms[0].dtype),
        in_specs=[whole_spec()] * len(terms) + [far_off_spec()],
        out_specs=whole_spec(),
        compiler_params=params(16),
        cost_estimate=pl.CostEstimate(flops=10**4, bytes_accessed=10**5, transcendentals=0),
    )(*terms, other)


def sum_over(value, axis, groups, other=None):
    count = lax.axis_size(axis)
    for g, steps in enumerate(groups):
        terms = [value] + [lax.ppermute(value, axis, partners(count, k)) for k in steps]
        if other is not None and g == len(groups) - 1:
            value = add_after(terms, other)
        else:
            value = sum(terms[1:], value)
    return value


def per_device(positions, tension, bending, moved_order, move_destination, move_target, far_range,
               old_basis, source_nodes):
    vesicles, _, nodes = positions.shape
    rows, sources = old_basis.shape
    rank = rows // 2
    clu_count, col_count = lax.axis_size("clu"), lax.axis_size("col")
    moves = move_target.shape[0]
    slot_cap = 2 * ((moves + clu_count - 1) // clu_count)
    flat = positions.reshape(2 * vesicles, nodes)

    columns = sources // nodes
    sent_rows = columns * rank + (2 * columns + 15) // 16 * 16
    deriv, table = spectral_tables(nodes)
    near_by = functools.partial(pltpu.with_memory_space_constraint, memory_space=pltpu.HBM)
    basis_here, nodes_here, flat_here = near_by(old_basis), near_by(source_nodes), near_by(flat)
    sent = pl.pallas_call(
        piece_kernel,
        out_shape=jax.ShapeDtypeStruct((sent_rows, nodes), BF16),
        in_specs=[far_off_spec()] * 2,
        out_specs=whole_spec(),
        scratch_shapes=[pltpu.VMEM(old_basis.shape, BF16), pltpu.VMEM(source_nodes.shape, BF16),
                        pltpu.SemaphoreType.DMA((2,))],
        compiler_params=params(16),
        cost_estimate=pl.CostEstimate(flops=10**5, bytes_accessed=10**5, transcendentals=0),
    )(basis_here, nodes_here)

    operands = [flat, tension, bending.reshape(1, vesicles), moved_order,
                move_destination.reshape(1, moves), move_target.reshape(1, moves),
                jnp.asarray(deriv), jnp.asarray(table)]
    operands = [flat_here] + [near_by(o) for o in operands[1:]]
    force, kept, leaving = pl.pallas_call(
        functools.partial(force_kernel, clu_count),
        out_shape=[jax.ShapeDtypeStruct((2 * vesicles, nodes), F32),
                   *[jax.ShapeDtypeStruct((clu_count // 2, BLOCK, 5 * nodes), F32)] * 2],
        in_specs=[far_off_spec()] * len(operands),
        out_specs=[whole_spec()] * 3,
        scratch_shapes=[pltpu.VMEM(o.shape, o.dtype) for o in operands]
        + [pltpu.SemaphoreType.DMA((len(operands),))],
        compiler_params=params(16),
        cost_estimate=pl.CostEstimate(flops=10**8, bytes_accessed=10**6, transcendentals=0),
    )(*operands)

    moved_halves = [lax.ppermute(sent, "col", partners(col_count, k)) for k in range(1, col_count)]
    arrived = cube_exchange(kept, leaving, "clu")
    pieces = []
    for mine in moved_halves:
        pieces += [mine, lax.ppermute(mine, "clu", [(i, i ^ 1) for i in range(clu_count)])]

    near_first = near_part(flat, arrived[:-1], None, slot_cap)
    near = near_part(flat, arrived[-1:], near_first, slot_cap)

    high, low, gram = pl.pallas_call(
        functools.partial(far_kernel, col_count),
        out_shape=[jax.ShapeDtypeStruct((vesicles, rank, 2 * nodes), BF16)] * 2
        + [jax.ShapeDtypeStruct((rank // 2, 2 * rank), F32)],
        in_specs=[far_off_spec()] * 4 + [whole_spec()] * (2 * (col_count - 1)),
        out_specs=[whole_spec()] * 3,
        scratch_shapes=[
            pltpu.SMEM((1, vesicles), jnp.int32),
            pltpu.VMEM((2 * vesicles, nodes), F32),
            pltpu.VMEM((2, sources), BF16),
            pltpu.VMEM((rows, sources), BF16),
            pltpu.VMEM((col_count, rank, 2 * sources), BF16),
            pltpu.VMEM((col_count, 8, sources), F32),
            pltpu.VMEM((col_count, 2, sources, nodes), F32),
            pltpu.VMEM((rows, rows), F32),
            pltpu.SemaphoreType.DMA((4,))],
        compiler_params=params(32),
        cost_estimate=pl.CostEstimate(flops=10**10, bytes_accessed=10**7, transcendentals=10**7),
    )(near_by(far_range.reshape(1, vesicles)), flat_here, basis_here, nodes_here, *pieces)
    gram = sum_over(gram, "clu", step_groups(clu_count, True), near_first)
    gram = sum_over(gram, "col", step_groups(col_count, False))

    scale_factor = math.sqrt(2.0 * nodes * vesicles * clu_count * col_count)
    group = 8 if vesicles % 8 == 0 else vesicles
    block = pl.BlockSpec((group, rows, nodes), lambda i: (i, 0, 0))
    held = pl.BlockSpec((group, rank, 2 * nodes), lambda i: (i, 0, 0))
    new_basis = pl.pallas_call(
        functools.partial(basis_kernel, scale_factor),
        out_shape=jax.ShapeDtypeStruct((vesicles, rows, nodes), F32),
        grid=(vesicles // group,),
        in_specs=[whole_spec(), held, held, far_off_spec()],
        out_specs=block,
        scratch_shapes=[pltpu.VMEM((rank, 3 * rank), BF16)],
        compiler_params=params(16),
        cost_estimate=pl.CostEstimate(flops=10**9, bytes_accessed=10**7, transcendentals=0),
    )(gram, high, low, near_by(near))

    return (force.reshape(vesicles, 2, nodes), near.reshape(vesicles, 2, nodes),
            new_basis.reshape(vesicles, rank, 2, nodes))


def solution(mesh):
    both = ("clu", "col")
    placed = (
        P(both, None, None), P(both, None), P(both), P(both, None), P(both, None), P(both),
        P(both, None), P(None, "col"), P(None, "col"),
    )
    return jax.shard_map(
        per_device,
        mesh=mesh,
        in_specs=placed,
        out_specs=(P(both, None, None), P(both, None, None), P(both, None, None, None)),
        check_vma=False,
    )
```

```python
import functools
import math

import jax
import jax.numpy as jnp
import numpy as np
from jax import lax
from jax.experimental import pallas as pl
from jax.experimental.pallas import tpu as pltpu
from jax.sharding import PartitionSpec as P

EPS_SQUARED = 0.01
F32 = jnp.float32
BF16 = jnp.bfloat16
HIGHEST = lax.Precision.HIGHEST
BLOCK = 8
MIB = 1 << 20

NT = (((1,), (1,)), ((), ()))
NN = (((1,), (0,)), ((), ()))


def spectral_tables(node_count):
    half = node_count // 2
    j = np.arange(node_count)[:, None]
    k = np.arange(half + 1)[None, :]
    phase = (j * k % node_count) * (2.0 * math.pi / node_count)
    c, s = np.cos(phase), np.sin(phase)
    k = np.arange(half + 1, dtype=np.float64)
    inside = (k > 0) & (k < half)
    u = np.where(inside, 2.0 * k / half, 0.0)
    w = np.where(inside, 2.0 * (k / half) ** 4, np.where(k == half, 1.0, 0.0))
    derivative = ((c * u) @ s.T - (s * u) @ c.T) / node_count
    bending_table = ((c * w) @ c.T + (s * w) @ s.T) / node_count
    return derivative.T.astype(np.float32), bending_table.T.astype(np.float32)


def iota(shape, axis):
    return lax.broadcasted_iota(jnp.int32, shape, axis)


def dot(a, b, dims=NN, precision=None):
    return lax.dot_general(a, b, dims, precision=precision, preferred_element_type=F32)


def reciprocal(x):
    return pl.reciprocal(x, approx=True)


def fetch(sources, targets, sems):
    copies = [pltpu.make_async_copy(s, t, sems.at[i])
              for i, (s, t) in enumerate(zip(sources, targets))]
    for copy in copies:
        copy.start()
    for copy in copies:
        copy.wait()


def piece_kernel(own_in, nodes_in, sent_ref, own_ref, nodes_ref, sems):
    fetch([own_in, nodes_in], [own_ref, nodes_ref], sems)
    half = own_ref.shape[0] // 2
    core = lax.rem(lax.axis_index("clu"), 2)
    mine = own_ref[pl.ds(pl.multiple_of(core * half, half), half), :]
    spots = nodes_ref[...].astype(F32)
    lanes = sent_ref.shape[1]
    columns = own_ref.shape[1] // lanes
    for c in range(columns):
        sent_ref[c * half:(c + 1) * half] = mine[:, c * lanes:(c + 1) * lanes]
    spots = jnp.concatenate([spots[:, c * lanes:(c + 1) * lanes] for c in range(columns)], axis=0)
    tail = sent_ref.shape[0] - columns * half
    spots = jnp.concatenate([spots, jnp.zeros((tail - 2 * columns, lanes), F32)], axis=0)
    sent_ref[columns * half:] = spots.astype(BF16)


def cube_place(destination, own, count):
    relative = jnp.bitwise_xor(destination, own)
    place = jnp.zeros_like(relative)
    bit = 1
    while bit < count:
        place = 2 * place + jnp.bitwise_and(relative, bit) // bit
        bit *= 2
    return place


def cube_exchange(kept, leaving, axis):
    count = lax.axis_size(axis)
    assert power_of_two(count)
    held = [kept]
    bit = 1
    while True:
        held.append(lax.ppermute(leaving, axis, partners(count, bit)))
        bit *= 2
        if bit >= count:
            return held
        span = count // bit
        tails = []
        for h, part in enumerate(held):
            cut = part.reshape(-1, span, *part.shape[-2:])
            tails.append(cut[:, span // 2:].reshape(-1, *part.shape[-2:]))
            held[h] = cut[:, :span // 2].reshape(-1, *part.shape[-2:])
        leaving = jnp.concatenate(tails, axis=0)


def force_kernel(clu_count, *refs):
    sources, targets, sems = refs[:8], refs[11:19], refs[19]
    force_ref, kept_ref, leaving_ref = refs[8:11]
    fetch(sources, targets, sems)
    (pos_ref, ten_ref, bend_ref, order_ref, dest_ref, target_ref, deriv_ref, table_ref) = targets
    vesicles = ten_ref.shape[0]
    moves = target_ref.shape[1]
    x = pos_ref[pl.ds(0, vesicles, stride=2), :]
    y = pos_ref[pl.ds(1, vesicles, stride=2), :]
    rows = jnp.concatenate([x, y], axis=0)
    deriv = deriv_ref[...]
    tension = jnp.concatenate([ten_ref[...]] * 2, axis=0)
    eye = iota((vesicles, vesicles), 0) == iota((vesicles, vesicles), 1)
    bend = jnp.sum(jnp.where(eye, bend_ref[...], 0.0), axis=1, keepdims=True)
    bend = jnp.concatenate([bend] * 2, axis=0)
    slope = dot(rows, deriv, precision=HIGHEST)
    fourth = dot(rows, table_ref[...], precision=HIGHEST)
    force = dot(tension * slope, deriv, precision=HIGHEST) - bend * fourth
    force_x, force_y = force[:vesicles], force[vesicles:]
    force_ref[pl.ds(0, vesicles, stride=2), :] = force_x
    force_ref[pl.ds(1, vesicles, stride=2), :] = force_y

    slots = clu_count * BLOCK
    place = cube_place(dest_ref[...], lax.axis_index("clu"), clu_count)
    hot = (iota((clu_count, moves), 0) == place).astype(F32)
    earlier = (iota((moves, moves), 0) < iota((moves, moves), 1)).astype(F32)
    rank = jnp.sum(dot(hot, earlier) * hot, axis=0, keepdims=True).astype(jnp.int32)
    slot = place * BLOCK + rank
    pack = (iota((slots, moves), 0) == slot).astype(F32)
    pick = (iota((vesicles, moves), 0) == order_ref[:, :moves]).astype(F32)
    select = dot(pack, pick, NT)
    carried = jnp.concatenate([x, y, force_x, force_y], axis=1)
    packed = dot(select, carried, precision=HIGHEST)
    tag = jnp.sum(pack * (target_ref[...] + 1).astype(F32), axis=1, keepdims=True)
    tag = jnp.broadcast_to(tag, (slots, x.shape[1]))
    packed = jnp.concatenate([packed, tag], axis=1)
    packed = packed.reshape(clu_count, BLOCK, packed.shape[1])
    kept_ref[...] = packed[:clu_count // 2]
    leaving_ref[...] = packed[clu_count // 2:]


def near_piece(data, tx, ty, slot_cap):
    nodes = tx.shape[1]
    chunk = 32 if nodes % 32 == 0 else nodes
    turned = [data[:, c * nodes:(c + 1) * nodes].T for c in range(4)]

    def fold(value):
        return jnp.sum(value.reshape(-1, 8, nodes), axis=0)

    rows_x, rows_y = [], []
    for h in range(slot_cap):
        logs_x = logs_y = pulls_x = pulls_y = jnp.zeros((8, nodes), F32)
        for start in range(0, nodes, chunk):
            sx, sy, fx, fy = [
                jnp.broadcast_to(t[start:start + chunk, h:h + 1], (chunk, nodes)) for t in turned]
            dx = tx[h:h + 1] - sx
            dy = ty[h:h + 1] - sy
            spread = dx * dx + dy * dy + EPS_SQUARED
            logs = jnp.log(spread)
            along = (dx * fx + dy * fy) * reciprocal(spread)
            logs_x, logs_y = logs_x + fold(logs * fx), logs_y + fold(logs * fy)
            pulls_x, pulls_y = pulls_x + fold(dx * along), pulls_y + fold(dy * along)
        rows_x.append(jnp.sum(pulls_x - 0.5 * logs_x, axis=0, keepdims=True))
        rows_y.append(jnp.sum(pulls_y - 0.5 * logs_y, axis=0, keepdims=True))
    rest = [jnp.zeros((BLOCK - slot_cap, nodes), F32)] if slot_cap < BLOCK else []
    return jnp.concatenate(rows_x + rest, axis=0), jnp.concatenate(rows_y + rest, axis=0)


def target_table(tag, vesicles):
    tag = tag.reshape(-1, tag.shape[-1])[:, :vesicles]
    return (tag == (iota(tag.shape, 1) + 1).astype(F32)).astype(F32)


def axis_rows(vesicles, axis):
    return pl.ds(axis, vesicles, stride=2)


def near_kernel(slot_cap, piece_count, pos_ref, *refs):
    piece_refs = refs[:piece_count]
    near_ref, arrived, aim_x, aim_y, speed_x, speed_y = refs[piece_count:]
    vesicles, nodes = pos_ref.shape[0] // 2, pos_ref.shape[1]
    here = 0
    for ref in piece_refs:
        arrived[here:here + ref.shape[0]] = ref[...]
        here += ref.shape[0]
    pieces = arrived.shape[0]
    hot = target_table(arrived[:, :, 4 * nodes:], vesicles)
    for axis, aim in enumerate((aim_x, aim_y)):
        aim[...] = dot(hot, pos_ref[axis_rows(vesicles, axis), :], precision=HIGHEST).reshape(
            pieces, BLOCK, nodes)
    many = 2 if pieces % 2 == 0 else 1

    def group(i, _):
        speeds = [near_piece(arrived[i * many + c], aim_x[i * many + c], aim_y[i * many + c],
                             slot_cap) for c in range(many)]
        for c, (value_x, value_y) in enumerate(speeds):
            speed_x[i * many + c] = value_x
            speed_y[i * many + c] = value_y
        return 0

    lax.fori_loop(0, pieces // many, group, 0)
    turned_hot = hot.T
    for axis, speed in enumerate((speed_x, speed_y)):
        near_ref[axis_rows(vesicles, axis), :] = dot(
            turned_hot, speed[...].reshape(-1, nodes), precision=HIGHEST) / nodes


def near_part(flat, pieces, slot_cap):
    vesicles, nodes = flat.shape[0] // 2, flat.shape[1]
    count = sum(p.shape[0] for p in pieces)
    return pl.pallas_call(
        functools.partial(near_kernel, slot_cap, len(pieces)),
        out_shape=jax.ShapeDtypeStruct((2 * vesicles, nodes), F32),
        in_specs=[whole_spec()] * (1 + len(pieces)),
        out_specs=whole_spec(),
        scratch_shapes=[pltpu.VMEM((count, BLOCK, 5 * nodes), F32)]
        + [pltpu.VMEM((count, BLOCK, nodes), F32)] * 4,
        compiler_params=params(16),
        cost_estimate=pl.CostEstimate(
            flops=10**9, bytes_accessed=10**7, transcendentals=10**6),
    )(flat, *pieces)


def near_rest(slot_cap, pos_ref, piece_ref, before_ref, near_ref):
    vesicles, nodes = pos_ref.shape[0] // 2, pos_ref.shape[1]
    hot = target_table(piece_ref[:, :, 4 * nodes:], vesicles)
    aims = [dot(hot, pos_ref[axis_rows(vesicles, axis), :], precision=HIGHEST)
            for axis in range(2)]
    speeds = [near_piece(piece_ref[k], *[aim[k * BLOCK:(k + 1) * BLOCK] for aim in aims], slot_cap)
              for k in range(piece_ref.shape[0])]
    turned_hot = hot.T
    for axis in range(2):
        rows = axis_rows(vesicles, axis)
        speed = jnp.concatenate([pieces[axis] for pieces in speeds], axis=0)
        near_ref[rows, :] = before_ref[rows, :] + dot(turned_hot, speed, precision=HIGHEST) / nodes


def far_kernel(col_count, range_in, pos_in, own_in, nodes_in, *refs):
    count = 2 * (col_count - 1)
    piece_refs = refs[:count]
    (high_ref, low_ref, gram_ref, range_ref, pos_ref, own_nodes, own_rows, basis, spots, wide,
     sums, sems) = refs[count:]
    vesicles = pos_ref.shape[0] // 2
    nodes = pos_ref.shape[1]
    rank, sources = own_rows.shape[0] // 2, own_rows.shape[1]
    rows = 2 * rank
    core, col = lax.rem(lax.axis_index("clu"), 2), lax.axis_index("col")
    fetch([range_in, pos_in, nodes_in, own_in], [range_ref, pos_ref, own_nodes, own_rows], sems)
    basis[col, :, :sources] = own_rows[:rank]
    basis[col, :, sources:] = own_rows[rank:]
    spots[col, 0:2] = own_nodes[...].astype(F32)
    for k in range(1, col_count):
        where = origin(col, k, col_count)
        mine, other = piece_refs[2 * k - 2], piece_refs[2 * k - 1]
        columns = sources // nodes
        ends = mine[columns * rank:].astype(F32)
        for c in range(columns):
            lanes = slice(c * nodes, (c + 1) * nodes)
            from_rows = slice(c * rank, (c + 1) * rank)
            for ref, part in ((mine, core), (other, 1 - core)):
                there = pl.multiple_of(part * sources + c * nodes, nodes)
                basis[where, :, pl.ds(there, nodes)] = ref[from_rows]
            spots[where, 0:2, lanes] = ends[2 * c:2 * c + 2]
    for r in range(col_count):
        turned = spots[r].T
        for c in range(2):
            wide[r, c] = jnp.broadcast_to(turned[:, c:c + 1], (sources, nodes))
    sums[...] = jnp.zeros_like(sums)

    chunk = 32 if sources % 32 == 0 else sources
    depth = 256 if sources % 256 == 0 else sources

    def evaluate(v, start):
        r = range_ref[0, v]
        tx = pos_ref[pl.ds(2 * v, 1), :]
        ty = pos_ref[pl.ds(2 * v + 1, 1), :]
        dx = tx - wide[r, 0, start:start + chunk]
        dy = ty - wide[r, 1, start:start + chunk]
        xx, yy = dx * dx, dy * dy
        spread = xx + yy + EPS_SQUARED
        log_part = -0.5 * jnp.log(spread)
        inverse = reciprocal(spread)
        return ((log_part + xx * inverse).astype(BF16), (dx * dy * inverse).astype(BF16),
                (log_part + yy * inverse).astype(BF16))

    def sketch(v):
        r = range_ref[0, v]
        total = None
        for start in range(0, sources, depth):
            ff, fs, ss = [jnp.concatenate(p, axis=0) for p in zip(
                *[evaluate(v, start + c) for c in range(0, depth, chunk)])]
            part = dot(basis[r, :, start:start + depth], jnp.concatenate([ff, fs], axis=1))
            part += dot(basis[r, :, sources + start:sources + start + depth],
                        jnp.concatenate([fs, ss], axis=1))
            total = part if total is None else total + part
        return total

    many = math.gcd(vesicles, 4)

    def group_gram(v):
        both = jnp.concatenate([
            jnp.concatenate([ref[v + c] for c in range(many)], axis=1)
            for ref in (high_ref, low_ref)], axis=0)
        return dot(both, both, NT)

    high_ref[0:many] = jnp.zeros((many, rank, 2 * nodes), BF16)
    low_ref[0:many] = jnp.zeros((many, rank, 2 * nodes), BF16)

    def group(i, _):
        v = many * i
        before = group_gram(jnp.maximum(v - many, 0))
        made = [sketch(v + c) for c in range(many)]
        sums[...] += before
        for c, value in enumerate(made):
            high = value.astype(BF16)
            high_ref[v + c] = high
            low_ref[v + c] = (value - high.astype(F32)).astype(BF16)
        return 0

    lax.fori_loop(0, vesicles // many, group, 0)
    sums[...] += group_gram(vesicles - many)
    total = sums[...]
    gram = total[:rank, :rank] + total[rank:, rank:] + (total[:rank, rank:] + total[rank:, :rank])
    gram_ref[...] = jnp.concatenate([gram[:rank // 2], gram[rank // 2:]], axis=1)


def lower_inverse(gram):
    size = gram.shape[0]
    eye = (iota((size, size), 0) == iota((size, size), 1)).astype(F32)
    rest = jnp.concatenate([gram, eye], axis=1)
    done = []
    step = 8
    for start in range(0, size, step):
        height = size - start
        columns = [jnp.broadcast_to(rest[:, start + j:start + j + 1], (height, 2 * size))
                   for j in range(step)]
        row_number = iota((height, 2 * size), 0)
        scale = jnp.zeros((step, 2 * size), F32)
        for j in range(step):
            column = columns[j]
            pivot = column[j:j + 1]
            factor = jnp.where(row_number > j, column * reciprocal(pivot), 0.0)
            for later in range(j + 1, step):
                columns[later] = columns[later] - factor * column[later:later + 1]
            rest = rest - factor * rest[j:j + 1]
            root = lax.rsqrt(pivot)
            root = root * (1.5 - 0.5 * pivot * root * root)
            scale = jnp.where(row_number[:step] == j, root, scale)
        done.append(rest[:step] * scale)
        rest = rest[step:]
    return jnp.concatenate(done, axis=0)[:, size:]


def basis_kernel(scale_factor, slot_cap, gram_ref, high_ref, low_ref, pos_ref, piece_ref,
                 before_ref, out_ref, near_ref, weight):
    rank, nodes = high_ref.shape[1], high_ref.shape[2] // 2

    @pl.when(pl.program_id(0) == 0)
    def _():
        near_rest(slot_cap, pos_ref, piece_ref, before_ref, near_ref)
        folded = gram_ref[...]
        gram = jnp.concatenate([folded[:, :rank], folded[:, rank:]], axis=0)
        inverse = lower_inverse(gram) * scale_factor
        high = inverse.astype(BF16)
        low = (inverse - high.astype(F32)).astype(BF16)
        weight[...] = jnp.concatenate([high, high, low], axis=1)

    w = weight[...]
    for v in range(high_ref.shape[0]):
        fresh = dot(w, jnp.concatenate([high_ref[v], low_ref[v], high_ref[v]], axis=0))
        for d in range(2):
            out_ref[v, pl.ds(d, rank, stride=2), :] = fresh[:, d * nodes:(d + 1) * nodes]


def whole_spec():
    return pl.BlockSpec(memory_space=pltpu.VMEM)


def far_off_spec():
    return pl.BlockSpec(memory_space=pltpu.HBM)


def params(mib):
    return pltpu.CompilerParams(vmem_limit_bytes=mib * MIB)


def power_of_two(count):
    return count & (count - 1) == 0


def partners(count, step):
    if power_of_two(count):
        return [(i, i ^ step) for i in range(count)]
    return [(i, (i + step) % count) for i in range(count)]


def origin(index, step, count):
    if power_of_two(count):
        return jnp.bitwise_xor(index, step)
    return lax.rem(index - step + count, count)


def step_groups(count, single_first):
    if not power_of_two(count):
        return [list(range(1, count))]
    groups, bit = [], 1
    if single_first and count > 1:
        groups, bit = [[1]], 2
    while bit < count:
        groups.append([bit] if 2 * bit >= count else [bit, 2 * bit, 3 * bit])
        bit *= 4
    return groups


def add_kernel(count, *refs):
    total = refs[0][...]
    for ref in refs[1:count]:
        total = total + ref[...]
    refs[-1][...] = total


def add_after(terms, others):
    return pl.pallas_call(
        functools.partial(add_kernel, len(terms)),
        out_shape=jax.ShapeDtypeStruct(terms[0].shape, terms[0].dtype),
        in_specs=[whole_spec()] * len(terms) + [far_off_spec()] * len(others),
        out_specs=whole_spec(),
        compiler_params=params(16),
        cost_estimate=pl.CostEstimate(flops=10**4, bytes_accessed=10**5, transcendentals=0),
    )(*terms, *others)


def sum_over(value, axis, groups, others=None):
    count = lax.axis_size(axis)
    for g, steps in enumerate(groups):
        terms = [value] + [lax.ppermute(value, axis, partners(count, k)) for k in steps]
        if others is not None and g == len(groups) - 1:
            value = add_after(terms, others)
        else:
            value = sum(terms[1:], value)
    return value


def per_device(positions, tension, bending, moved_order, move_destination, move_target, far_range,
               old_basis, source_nodes):
    vesicles, _, nodes = positions.shape
    rows, sources = old_basis.shape
    rank = rows // 2
    clu_count, col_count = lax.axis_size("clu"), lax.axis_size("col")
    moves = move_target.shape[0]
    slot_cap = 2 * ((moves + clu_count - 1) // clu_count)
    flat = positions.reshape(2 * vesicles, nodes)

    columns = sources // nodes
    sent_rows = columns * rank + (2 * columns + 15) // 16 * 16
    deriv, table = spectral_tables(nodes)
    near_by = functools.partial(pltpu.with_memory_space_constraint, memory_space=pltpu.HBM)
    basis_here, nodes_here, flat_here = near_by(old_basis), near_by(source_nodes), near_by(flat)
    sent = pl.pallas_call(
        piece_kernel,
        out_shape=jax.ShapeDtypeStruct((sent_rows, nodes), BF16),
        in_specs=[far_off_spec()] * 2,
        out_specs=whole_spec(),
        scratch_shapes=[pltpu.VMEM(old_basis.shape, BF16), pltpu.VMEM(source_nodes.shape, BF16),
                        pltpu.SemaphoreType.DMA((2,))],
        compiler_params=params(16),
        cost_estimate=pl.CostEstimate(flops=10**5, bytes_accessed=10**5, transcendentals=0),
    )(basis_here, nodes_here)

    operands = [flat, tension, bending.reshape(1, vesicles), moved_order,
                move_destination.reshape(1, moves), move_target.reshape(1, moves),
                jnp.asarray(deriv), jnp.asarray(table)]
    operands = [flat_here] + [near_by(o) for o in operands[1:]]
    force, kept, leaving = pl.pallas_call(
        functools.partial(force_kernel, clu_count),
        out_shape=[jax.ShapeDtypeStruct((2 * vesicles, nodes), F32),
                   *[jax.ShapeDtypeStruct((clu_count // 2, BLOCK, 5 * nodes), F32)] * 2],
        in_specs=[far_off_spec()] * len(operands),
        out_specs=[whole_spec()] * 3,
        scratch_shapes=[pltpu.VMEM(o.shape, o.dtype) for o in operands]
        + [pltpu.SemaphoreType.DMA((len(operands),))],
        compiler_params=params(16),
        cost_estimate=pl.CostEstimate(flops=10**8, bytes_accessed=10**6, transcendentals=0),
    )(*operands)

    moved_halves = [lax.ppermute(sent, "col", partners(col_count, k)) for k in range(1, col_count)]
    arrived = cube_exchange(kept, leaving, "clu")
    pieces = []
    for mine in moved_halves:
        pieces += [mine, lax.ppermute(mine, "clu", [(i, i ^ 1) for i in range(clu_count)])]

    near_first = near_part(flat, arrived[:-1], slot_cap)

    high, low, gram = pl.pallas_call(
        functools.partial(far_kernel, col_count),
        out_shape=[jax.ShapeDtypeStruct((vesicles, rank, 2 * nodes), BF16)] * 2
        + [jax.ShapeDtypeStruct((rank // 2, 2 * rank), F32)],
        in_specs=[far_off_spec()] * 4 + [whole_spec()] * (2 * (col_count - 1)),
        out_specs=[whole_spec()] * 3,
        scratch_shapes=[
            pltpu.SMEM((1, vesicles), jnp.int32),
            pltpu.VMEM((2 * vesicles, nodes), F32),
            pltpu.VMEM((2, sources), BF16),
            pltpu.VMEM((rows, sources), BF16),
            pltpu.VMEM((col_count, rank, 2 * sources), BF16),
            pltpu.VMEM((col_count, 8, sources), F32),
            pltpu.VMEM((col_count, 2, sources, nodes), F32),
            pltpu.VMEM((rows, rows), F32),
            pltpu.SemaphoreType.DMA((4,))],
        compiler_params=params(32),
        cost_estimate=pl.CostEstimate(flops=10**10, bytes_accessed=10**7, transcendentals=10**7),
    )(near_by(far_range.reshape(1, vesicles)), flat_here, basis_here, nodes_here, *pieces)
    gram = sum_over(gram, "clu", step_groups(clu_count, True), [near_first, arrived[-1]])
    gram = sum_over(gram, "col", step_groups(col_count, False))

    scale_factor = math.sqrt(2.0 * nodes * vesicles * clu_count * col_count)
    group = 8 if vesicles % 8 == 0 else vesicles
    block = pl.BlockSpec((group, rows, nodes), lambda i: (i, 0, 0))
    held = pl.BlockSpec((group, rank, 2 * nodes), lambda i: (i, 0, 0))
    new_basis, near = pl.pallas_call(
        functools.partial(basis_kernel, scale_factor, slot_cap),
        out_shape=[jax.ShapeDtypeStruct((vesicles, rows, nodes), F32),
                   jax.ShapeDtypeStruct((2 * vesicles, nodes), F32)],
        grid=(vesicles // group,),
        in_specs=[whole_spec(), held, held] + [whole_spec()] * 3,
        out_specs=[block, whole_spec()],
        scratch_shapes=[pltpu.VMEM((rank, 3 * rank), BF16)],
        compiler_params=params(16),
        cost_estimate=pl.CostEstimate(flops=10**9, bytes_accessed=10**7, transcendentals=0),
    )(gram, high, low, flat, arrived[-1], near_first)

    return (force.reshape(vesicles, 2, nodes), near.reshape(vesicles, 2, nodes),
            new_basis.reshape(vesicles, rank, 2, nodes))


def solution(mesh):
    both = ("clu", "col")
    placed = (
        P(both, None, None), P(both, None), P(both), P(both, None), P(both, None), P(both),
        P(both, None), P(None, "col"), P(None, "col"),
    )
    return jax.shard_map(
        per_device,
        mesh=mesh,
        in_specs=placed,
        out_specs=(P(both, None, None), P(both, None, None), P(both, None, None, None)),
        check_vma=False,
    )
```

```python
import functools
import math

import jax
import jax.numpy as jnp
import numpy as np
from jax import lax
from jax.experimental import pallas as pl
from jax.experimental.pallas import tpu as pltpu
from jax.sharding import PartitionSpec as P

EPS_SQUARED = 0.01
F32 = jnp.float32
BF16 = jnp.bfloat16
HIGHEST = lax.Precision.HIGHEST
BLOCK = 8
MIB = 1 << 20

NT = (((1,), (1,)), ((), ()))
NN = (((1,), (0,)), ((), ()))


def spectral_tables(node_count):
    half = node_count // 2
    j = np.arange(node_count)[:, None]
    k = np.arange(half + 1)[None, :]
    phase = (j * k % node_count) * (2.0 * math.pi / node_count)
    c, s = np.cos(phase), np.sin(phase)
    k = np.arange(half + 1, dtype=np.float64)
    inside = (k > 0) & (k < half)
    u = np.where(inside, 2.0 * k / half, 0.0)
    w = np.where(inside, 2.0 * (k / half) ** 4, np.where(k == half, 1.0, 0.0))
    derivative = ((c * u) @ s.T - (s * u) @ c.T) / node_count
    bending_table = ((c * w) @ c.T + (s * w) @ s.T) / node_count
    return derivative.T.astype(np.float32), bending_table.T.astype(np.float32)


def iota(shape, axis):
    return lax.broadcasted_iota(jnp.int32, shape, axis)


def dot(a, b, dims=NN, precision=None):
    return lax.dot_general(a, b, dims, precision=precision, preferred_element_type=F32)


def reciprocal(x):
    return pl.reciprocal(x, approx=True)


def fetch(sources, targets, sems, meanwhile=None):
    copies = [pltpu.make_async_copy(s, t, sems.at[i])
              for i, (s, t) in enumerate(zip(sources, targets))]
    for copy in copies:
        copy.start()
    if meanwhile is not None:
        meanwhile()
    for copy in copies:
        copy.wait()


def piece_kernel(own_in, nodes_in, sent_ref, own_ref, nodes_ref, sems):
    fetch([own_in, nodes_in], [own_ref, nodes_ref], sems)
    half = own_ref.shape[0] // 2
    core = lax.rem(lax.axis_index("clu"), 2)
    mine = own_ref[pl.ds(pl.multiple_of(core * half, half), half), :]
    spots = nodes_ref[...].astype(F32)
    lanes = sent_ref.shape[1]
    columns = own_ref.shape[1] // lanes
    for c in range(columns):
        sent_ref[c * half:(c + 1) * half] = mine[:, c * lanes:(c + 1) * lanes]
    spots = jnp.concatenate([spots[:, c * lanes:(c + 1) * lanes] for c in range(columns)], axis=0)
    tail = sent_ref.shape[0] - columns * half
    spots = jnp.concatenate([spots, jnp.zeros((tail - 2 * columns, lanes), F32)], axis=0)
    sent_ref[columns * half:] = spots.astype(BF16)


def cube_place(destination, own, count):
    relative = jnp.bitwise_xor(destination, own)
    place = jnp.zeros_like(relative)
    bit = 1
    while bit < count:
        place = 2 * place + jnp.bitwise_and(relative, bit) // bit
        bit *= 2
    return place


def cube_exchange(kept, leaving, axis):
    count = lax.axis_size(axis)
    assert power_of_two(count)
    held = [kept]
    bit = 1
    while True:
        held.append(lax.ppermute(leaving, axis, partners(count, bit)))
        bit *= 2
        if bit >= count:
            return held
        span = count // bit
        tails = []
        for h, part in enumerate(held):
            cut = part.reshape(-1, span, *part.shape[-2:])
            tails.append(cut[:, span // 2:].reshape(-1, *part.shape[-2:]))
            held[h] = cut[:, :span // 2].reshape(-1, *part.shape[-2:])
        leaving = jnp.concatenate(tails, axis=0)


def force_kernel(clu_count, *refs):
    sources, targets, sems = refs[:8], refs[11:19], refs[19]
    force_ref, kept_ref, leaving_ref = refs[8:11]
    fetch(sources, targets, sems)
    (pos_ref, ten_ref, bend_ref, order_ref, dest_ref, target_ref, deriv_ref, table_ref) = targets
    vesicles = ten_ref.shape[0]
    moves = target_ref.shape[1]
    x = pos_ref[pl.ds(0, vesicles, stride=2), :]
    y = pos_ref[pl.ds(1, vesicles, stride=2), :]
    rows = jnp.concatenate([x, y], axis=0)
    deriv = deriv_ref[...]
    tension = jnp.concatenate([ten_ref[...]] * 2, axis=0)
    eye = iota((vesicles, vesicles), 0) == iota((vesicles, vesicles), 1)
    bend = jnp.sum(jnp.where(eye, bend_ref[...], 0.0), axis=1, keepdims=True)
    bend = jnp.concatenate([bend] * 2, axis=0)
    slope = dot(rows, deriv, precision=HIGHEST)
    fourth = dot(rows, table_ref[...], precision=HIGHEST)
    force = dot(tension * slope, deriv, precision=HIGHEST) - bend * fourth
    force_x, force_y = force[:vesicles], force[vesicles:]
    force_ref[pl.ds(0, vesicles, stride=2), :] = force_x
    force_ref[pl.ds(1, vesicles, stride=2), :] = force_y

    slots = clu_count * BLOCK
    place = cube_place(dest_ref[...], lax.axis_index("clu"), clu_count)
    hot = (iota((clu_count, moves), 0) == place).astype(F32)
    earlier = (iota((moves, moves), 0) < iota((moves, moves), 1)).astype(F32)
    rank = jnp.sum(dot(hot, earlier) * hot, axis=0, keepdims=True).astype(jnp.int32)
    slot = place * BLOCK + rank
    pack = (iota((slots, moves), 0) == slot).astype(F32)
    pick = (iota((vesicles, moves), 0) == order_ref[:, :moves]).astype(F32)
    select = dot(pack, pick, NT)
    carried = jnp.concatenate([x, y, force_x, force_y], axis=1)
    packed = dot(select, carried, precision=HIGHEST)
    tag = jnp.sum(pack * (target_ref[...] + 1).astype(F32), axis=1, keepdims=True)
    tag = jnp.broadcast_to(tag, (slots, x.shape[1]))
    packed = jnp.concatenate([packed, tag], axis=1)
    packed = packed.reshape(clu_count, BLOCK, packed.shape[1])
    kept_ref[...] = packed[:clu_count // 2]
    leaving_ref[...] = packed[clu_count // 2:]


def near_slot(turned, tx, ty):
    nodes = tx.shape[1]
    chunk = 32 if nodes % 32 == 0 else nodes

    def fold(value):
        return jnp.sum(value.reshape(-1, 8, nodes), axis=0)

    logs_x = logs_y = pulls_x = pulls_y = jnp.zeros((8, nodes), F32)
    for start in range(0, nodes, chunk):
        sx, sy, fx, fy = [
            jnp.broadcast_to(t[start:start + chunk], (chunk, nodes)) for t in turned]
        dx = tx - sx
        dy = ty - sy
        spread = dx * dx + dy * dy + EPS_SQUARED
        logs = jnp.log(spread)
        along = (dx * fx + dy * fy) * reciprocal(spread)
        logs_x, logs_y = logs_x + fold(logs * fx), logs_y + fold(logs * fy)
        pulls_x, pulls_y = pulls_x + fold(dx * along), pulls_y + fold(dy * along)
    return (jnp.sum(pulls_x - 0.5 * logs_x, axis=0, keepdims=True),
            jnp.sum(pulls_y - 0.5 * logs_y, axis=0, keepdims=True))


def near_piece(data, tx, ty, slot_cap):
    nodes = tx.shape[1]
    turned = [data[:, c * nodes:(c + 1) * nodes].T for c in range(4)]
    return [functools.partial(near_slot, [t[:, h:h + 1] for t in turned], tx[h:h + 1], ty[h:h + 1])
            for h in range(slot_cap)]


def gather_rows(slots, axis):
    nodes = slots[0][axis].shape[1]
    rest = [jnp.zeros((BLOCK - len(slots), nodes), F32)] if len(slots) < BLOCK else []
    return jnp.concatenate([slot[axis] for slot in slots] + rest, axis=0)


def target_table(tag, vesicles):
    tag = tag.reshape(-1, tag.shape[-1])[:, :vesicles]
    return (tag == (iota(tag.shape, 1) + 1).astype(F32)).astype(F32)


def axis_rows(vesicles, axis):
    return pl.ds(axis, vesicles, stride=2)


def near_kernel(slot_cap, piece_count, pos_ref, *refs):
    piece_refs = refs[:piece_count]
    near_ref, arrived, aim_x, aim_y, speed_x, speed_y = refs[piece_count:]
    vesicles, nodes = pos_ref.shape[0] // 2, pos_ref.shape[1]
    here = 0
    for ref in piece_refs:
        arrived[here:here + ref.shape[0]] = ref[...]
        here += ref.shape[0]
    pieces = arrived.shape[0]
    hot = target_table(arrived[:, :, 4 * nodes:], vesicles)
    for axis, aim in enumerate((aim_x, aim_y)):
        aim[...] = dot(hot, pos_ref[axis_rows(vesicles, axis), :], precision=HIGHEST).reshape(
            pieces, BLOCK, nodes)
    many = math.gcd(pieces, 4)

    def group(i, _):
        calls = [near_piece(arrived[i * many + c], aim_x[i * many + c], aim_y[i * many + c],
                            slot_cap) for c in range(many)]
        slots = [[call() for call in piece] for piece in calls]
        for c, piece in enumerate(slots):
            speed_x[i * many + c] = gather_rows(piece, 0)
            speed_y[i * many + c] = gather_rows(piece, 1)
        return 0

    lax.fori_loop(0, pieces // many, group, 0)
    turned_hot = hot.T
    for axis, speed in enumerate((speed_x, speed_y)):
        near_ref[axis_rows(vesicles, axis), :] = dot(
            turned_hot, speed[...].reshape(-1, nodes), precision=HIGHEST) / nodes


def near_part(flat, pieces, slot_cap):
    vesicles, nodes = flat.shape[0] // 2, flat.shape[1]
    count = sum(p.shape[0] for p in pieces)
    return pl.pallas_call(
        functools.partial(near_kernel, slot_cap, len(pieces)),
        out_shape=jax.ShapeDtypeStruct((2 * vesicles, nodes), F32),
        in_specs=[whole_spec()] * (1 + len(pieces)),
        out_specs=whole_spec(),
        scratch_shapes=[pltpu.VMEM((count, BLOCK, 5 * nodes), F32)]
        + [pltpu.VMEM((count, BLOCK, nodes), F32)] * 4,
        compiler_params=params(16),
        cost_estimate=pl.CostEstimate(
            flops=10**9, bytes_accessed=10**7, transcendentals=10**6),
    )(flat, *pieces)


def near_rest(slot_cap, pos_ref, piece_ref, before_ref):
    vesicles, nodes = pos_ref.shape[0] // 2, pos_ref.shape[1]
    hot = target_table(piece_ref[:, :, 4 * nodes:], vesicles)
    aims = [dot(hot, pos_ref[axis_rows(vesicles, axis), :], precision=HIGHEST)
            for axis in range(2)]
    before = [before_ref[axis_rows(vesicles, axis), :] for axis in range(2)]
    calls = [call for k in range(piece_ref.shape[0]) for call in near_piece(
        piece_ref[k], *[aim[k * BLOCK:(k + 1) * BLOCK] for aim in aims], slot_cap)]
    turned_hot = hot.T

    def finish(slots):
        pieces = [slots[k:k + slot_cap] for k in range(0, len(slots), slot_cap)]
        speeds = [jnp.concatenate([gather_rows(piece, axis) for piece in pieces], axis=0)
                  for axis in range(2)]
        return [b + dot(turned_hot, speed, precision=HIGHEST) / nodes
                for b, speed in zip(before, speeds)]

    return calls, finish


def far_kernel(col_count, range_in, pos_in, own_in, nodes_in, *refs):
    count = 2 * (col_count - 1)
    piece_refs = refs[:count]
    (high_ref, low_ref, gram_ref, range_ref, pos_ref, own_nodes, own_rows, basis, spots, wide,
     sums, sems) = refs[count:]
    vesicles = pos_ref.shape[0] // 2
    nodes = pos_ref.shape[1]
    rank, sources = own_rows.shape[0] // 2, own_rows.shape[1]
    rows = 2 * rank
    core, col = lax.rem(lax.axis_index("clu"), 2), lax.axis_index("col")
    columns = sources // nodes

    def widen(r):
        turned = spots[r].T
        for c in range(2):
            wide[r, c] = jnp.broadcast_to(turned[:, c:c + 1], (sources, nodes))

    def lay_out_received():
        for k in range(1, col_count):
            where = origin(col, k, col_count)
            mine, other = piece_refs[2 * k - 2], piece_refs[2 * k - 1]
            ends = mine[columns * rank:].astype(F32)
            for c in range(columns):
                lanes = slice(c * nodes, (c + 1) * nodes)
                from_rows = slice(c * rank, (c + 1) * rank)
                for ref, part in ((mine, core), (other, 1 - core)):
                    there = pl.multiple_of(part * sources + c * nodes, nodes)
                    basis[where, :, pl.ds(there, nodes)] = ref[from_rows]
                spots[where, 0:2, lanes] = ends[2 * c:2 * c + 2]
            widen(where)

    fetch([range_in, pos_in, nodes_in, own_in], [range_ref, pos_ref, own_nodes, own_rows], sems,
          lay_out_received)
    basis[col, :, :sources] = own_rows[:rank]
    basis[col, :, sources:] = own_rows[rank:]
    spots[col, 0:2] = own_nodes[...].astype(F32)
    widen(col)
    sums[...] = jnp.zeros_like(sums)

    chunk = 32 if sources % 32 == 0 else sources
    depth = 256 if sources % 256 == 0 else sources

    def evaluate(v, start):
        r = range_ref[0, v]
        tx = pos_ref[pl.ds(2 * v, 1), :]
        ty = pos_ref[pl.ds(2 * v + 1, 1), :]
        dx = tx - wide[r, 0, start:start + chunk]
        dy = ty - wide[r, 1, start:start + chunk]
        xx, yy = dx * dx, dy * dy
        spread = xx + yy + EPS_SQUARED
        log_part = -0.5 * jnp.log(spread)
        inverse = reciprocal(spread)
        return ((log_part + xx * inverse).astype(BF16), (dx * dy * inverse).astype(BF16),
                (log_part + yy * inverse).astype(BF16))

    def sketch(v):
        r = range_ref[0, v]
        total = None
        for start in range(0, sources, depth):
            ff, fs, ss = [jnp.concatenate(p, axis=0) for p in zip(
                *[evaluate(v, start + c) for c in range(0, depth, chunk)])]
            part = dot(basis[r, :, start:start + depth], jnp.concatenate([ff, fs], axis=1))
            part += dot(basis[r, :, sources + start:sources + start + depth],
                        jnp.concatenate([fs, ss], axis=1))
            total = part if total is None else total + part
        return total

    many = math.gcd(vesicles, 8)

    def group_gram(v):
        both = jnp.concatenate([
            jnp.concatenate([ref[v + c] for c in range(many)], axis=1)
            for ref in (high_ref, low_ref)], axis=0)
        return dot(both, both, NT)

    high_ref[0:many] = jnp.zeros((many, rank, 2 * nodes), BF16)
    low_ref[0:many] = jnp.zeros((many, rank, 2 * nodes), BF16)

    def group(i, _):
        v = many * i
        before = group_gram(jnp.maximum(v - many, 0))
        made = [sketch(v + c) for c in range(many)]
        sums[...] += before
        for c, value in enumerate(made):
            high = value.astype(BF16)
            high_ref[v + c] = high
            low_ref[v + c] = (value - high.astype(F32)).astype(BF16)
        return 0

    lax.fori_loop(0, vesicles // many, group, 0)
    sums[...] += group_gram(vesicles - many)
    total = sums[...]
    gram = total[:rank, :rank] + total[rank:, rank:] + (total[:rank, rank:] + total[rank:, :rank])
    gram_ref[...] = jnp.concatenate([gram[:rank // 2], gram[rank // 2:]], axis=1)


def lower_inverse(gram, beside):
    size = gram.shape[0]
    eye = (iota((size, size), 0) == iota((size, size), 1)).astype(F32)
    rest = jnp.concatenate([gram, eye], axis=1)
    done = []
    step = 8
    for start in range(0, size, step):
        height = size - start
        beside(start // step, size // step)
        columns = [jnp.broadcast_to(rest[:, start + j:start + j + 1], (height, 2 * size))
                   for j in range(step)]
        row_number = iota((height, 2 * size), 0)
        scale = jnp.zeros((step, 2 * size), F32)
        for j in range(step):
            column = columns[j]
            pivot = column[j:j + 1]
            factor = jnp.where(row_number > j, column * reciprocal(pivot), 0.0)
            for later in range(j + 1, step):
                columns[later] = columns[later] - factor * column[later:later + 1]
            rest = rest - factor * rest[j:j + 1]
            root = lax.rsqrt(pivot)
            root = root * (1.5 - 0.5 * pivot * root * root)
            scale = jnp.where(row_number[:step] == j, root, scale)
        done.append(rest[:step] * scale)
        rest = rest[step:]
    return jnp.concatenate(done, axis=0)[:, size:]


def basis_kernel(scale_factor, slot_cap, gram_ref, high_ref, low_ref, pos_ref, piece_ref,
                 before_ref, out_ref, near_ref, weight):
    rank, nodes = high_ref.shape[1], high_ref.shape[2] // 2

    @pl.when(pl.program_id(0) == 0)
    def _():
        folded = gram_ref[...]
        calls, finish = near_rest(slot_cap, pos_ref, piece_ref, before_ref)
        slots = []

        def beside(i, n):
            slots.extend(call() for call in calls[len(calls) * i // n:len(calls) * (i + 1) // n])

        gram = jnp.concatenate([folded[:, :rank], folded[:, rank:]], axis=0)
        inverse = lower_inverse(gram, beside) * scale_factor
        near = finish(slots)
        high = inverse.astype(BF16)
        low = (inverse - high.astype(F32)).astype(BF16)
        weight[...] = jnp.concatenate([high, high, low], axis=1)
        for axis in range(2):
            near_ref[axis_rows(near[axis].shape[0], axis), :] = near[axis]

    w = weight[...]
    many = math.gcd(high_ref.shape[0], 2)
    for v in range(0, high_ref.shape[0], many):
        fresh = [dot(w, jnp.concatenate([high_ref[u], low_ref[u], high_ref[u]], axis=0))
                 for u in range(v, v + many)]
        for u, value in enumerate(fresh):
            for d in range(2):
                out_ref[v + u, pl.ds(d, rank, stride=2), :] = value[:, d * nodes:(d + 1) * nodes]


def whole_spec():
    return pl.BlockSpec(memory_space=pltpu.VMEM)


def far_off_spec():
    return pl.BlockSpec(memory_space=pltpu.HBM)


def params(mib):
    return pltpu.CompilerParams(vmem_limit_bytes=mib * MIB)


def power_of_two(count):
    return count & (count - 1) == 0


def partners(count, step):
    if power_of_two(count):
        return [(i, i ^ step) for i in range(count)]
    return [(i, (i + step) % count) for i in range(count)]


def origin(index, step, count):
    if power_of_two(count):
        return jnp.bitwise_xor(index, step)
    return lax.rem(index - step + count, count)


def step_groups(count, single_first):
    if not power_of_two(count):
        return [list(range(1, count))]
    groups, bit = [], 1
    if single_first and count > 1:
        groups, bit = [[1]], 2
    while bit < count:
        groups.append([bit] if 2 * bit >= count else [bit, 2 * bit, 3 * bit])
        bit *= 4
    return groups


def add_kernel(count, *refs):
    total = refs[0][...]
    for ref in refs[1:count]:
        total = total + ref[...]
    refs[-1][...] = total


def add_after(terms, others):
    return pl.pallas_call(
        functools.partial(add_kernel, len(terms)),
        out_shape=jax.ShapeDtypeStruct(terms[0].shape, terms[0].dtype),
        in_specs=[whole_spec()] * len(terms) + [far_off_spec()] * len(others),
        out_specs=whole_spec(),
        compiler_params=params(16),
        cost_estimate=pl.CostEstimate(flops=10**4, bytes_accessed=10**5, transcendentals=0),
    )(*terms, *others)


def sum_over(value, axis, groups, others=None):
    count = lax.axis_size(axis)
    for g, steps in enumerate(groups):
        terms = [value] + [lax.ppermute(value, axis, partners(count, k)) for k in steps]
        if others is not None and g == len(groups) - 1:
            value = add_after(terms, others)
        else:
            value = sum(terms[1:], value)
    return value


def per_device(positions, tension, bending, moved_order, move_destination, move_target, far_range,
               old_basis, source_nodes):
    vesicles, _, nodes = positions.shape
    rows, sources = old_basis.shape
    rank = rows // 2
    clu_count, col_count = lax.axis_size("clu"), lax.axis_size("col")
    moves = move_target.shape[0]
    slot_cap = 2 * ((moves + clu_count - 1) // clu_count)
    flat = positions.reshape(2 * vesicles, nodes)

    columns = sources // nodes
    sent_rows = columns * rank + (2 * columns + 15) // 16 * 16
    deriv, table = spectral_tables(nodes)
    near_by = functools.partial(pltpu.with_memory_space_constraint, memory_space=pltpu.HBM)
    basis_here, nodes_here, flat_here = near_by(old_basis), near_by(source_nodes), near_by(flat)
    sent = pl.pallas_call(
        piece_kernel,
        out_shape=jax.ShapeDtypeStruct((sent_rows, nodes), BF16),
        in_specs=[far_off_spec()] * 2,
        out_specs=whole_spec(),
        scratch_shapes=[pltpu.VMEM(old_basis.shape, BF16), pltpu.VMEM(source_nodes.shape, BF16),
                        pltpu.SemaphoreType.DMA((2,))],
        compiler_params=params(16),
        cost_estimate=pl.CostEstimate(flops=10**5, bytes_accessed=10**5, transcendentals=0),
    )(basis_here, nodes_here)

    operands = [flat, tension, bending.reshape(1, vesicles), moved_order,
                move_destination.reshape(1, moves), move_target.reshape(1, moves),
                jnp.asarray(deriv), jnp.asarray(table)]
    operands = [flat_here] + [near_by(o) for o in operands[1:]]
    force, kept, leaving = pl.pallas_call(
        functools.partial(force_kernel, clu_count),
        out_shape=[jax.ShapeDtypeStruct((2 * vesicles, nodes), F32),
                   *[jax.ShapeDtypeStruct((clu_count // 2, BLOCK, 5 * nodes), F32)] * 2],
        in_specs=[far_off_spec()] * len(operands),
        out_specs=[whole_spec()] * 3,
        scratch_shapes=[pltpu.VMEM(o.shape, o.dtype) for o in operands]
        + [pltpu.SemaphoreType.DMA((len(operands),))],
        compiler_params=params(16),
        cost_estimate=pl.CostEstimate(flops=10**8, bytes_accessed=10**6, transcendentals=0),
    )(*operands)

    moved_halves = [lax.ppermute(sent, "col", partners(col_count, k)) for k in range(1, col_count)]
    arrived = cube_exchange(kept, leaving, "clu")
    pieces = []
    for mine in moved_halves:
        pieces += [mine, lax.ppermute(mine, "clu", [(i, i ^ 1) for i in range(clu_count)])]

    near_first = near_part(flat, arrived[:-1], slot_cap)

    high, low, gram = pl.pallas_call(
        functools.partial(far_kernel, col_count),
        out_shape=[jax.ShapeDtypeStruct((vesicles, rank, 2 * nodes), BF16)] * 2
        + [jax.ShapeDtypeStruct((rank // 2, 2 * rank), F32)],
        in_specs=[far_off_spec()] * 4 + [whole_spec()] * (2 * (col_count - 1)),
        out_specs=[whole_spec()] * 3,
        scratch_shapes=[
            pltpu.SMEM((1, vesicles), jnp.int32),
            pltpu.VMEM((2 * vesicles, nodes), F32),
            pltpu.VMEM((2, sources), BF16),
            pltpu.VMEM((rows, sources), BF16),
            pltpu.VMEM((col_count, rank, 2 * sources), BF16),
            pltpu.VMEM((col_count, 8, sources), F32),
            pltpu.VMEM((col_count, 2, sources, nodes), F32),
            pltpu.VMEM((rows, rows), F32),
            pltpu.SemaphoreType.DMA((4,))],
        compiler_params=params(32),
        cost_estimate=pl.CostEstimate(flops=10**10, bytes_accessed=10**7, transcendentals=10**7),
    )(near_by(far_range.reshape(1, vesicles)), flat_here, basis_here, nodes_here, *pieces)
    gram = sum_over(gram, "clu", step_groups(clu_count, True), [near_first, arrived[-1]])
    gram = sum_over(gram, "col", step_groups(col_count, False))

    scale_factor = math.sqrt(2.0 * nodes * vesicles * clu_count * col_count)
    group = 8 if vesicles % 8 == 0 else vesicles
    block = pl.BlockSpec((group, rows, nodes), lambda i: (i, 0, 0))
    held = pl.BlockSpec((group, rank, 2 * nodes), lambda i: (i, 0, 0))
    new_basis, near = pl.pallas_call(
        functools.partial(basis_kernel, scale_factor, slot_cap),
        out_shape=[jax.ShapeDtypeStruct((vesicles, rows, nodes), F32),
                   jax.ShapeDtypeStruct((2 * vesicles, nodes), F32)],
        grid=(vesicles // group,),
        in_specs=[whole_spec(), held, held] + [whole_spec()] * 3,
        out_specs=[block, whole_spec()],
        scratch_shapes=[pltpu.VMEM((rank, 3 * rank), BF16)],
        compiler_params=params(16),
        cost_estimate=pl.CostEstimate(flops=10**9, bytes_accessed=10**7, transcendentals=0),
    )(gram, high, low, flat, arrived[-1], near_first)

    return (force.reshape(vesicles, 2, nodes), near.reshape(vesicles, 2, nodes),
            new_basis.reshape(vesicles, rank, 2, nodes))


def solution(mesh):
    both = ("clu", "col")
    placed = (
        P(both, None, None), P(both, None), P(both), P(both, None), P(both, None), P(both),
        P(both, None), P(None, "col"), P(None, "col"),
    )
    return jax.shard_map(
        per_device,
        mesh=mesh,
        in_specs=placed,
        out_specs=(P(both, None, None), P(both, None, None), P(both, None, None, None)),
        check_vma=False,
    )
```

```python
import functools
import math

import jax
import jax.numpy as jnp
import numpy as np
from jax import lax
from jax.experimental import pallas as pl
from jax.experimental.pallas import tpu as pltpu
from jax.sharding import PartitionSpec as P

EPS_SQUARED = 0.01
F32 = jnp.float32
BF16 = jnp.bfloat16
HIGHEST = lax.Precision.HIGHEST
BLOCK = 8
MIB = 1 << 20

NT = (((1,), (1,)), ((), ()))
NN = (((1,), (0,)), ((), ()))


def spectral_tables(node_count):
    half = node_count // 2
    j = np.arange(node_count)[:, None]
    k = np.arange(half + 1)[None, :]
    phase = (j * k % node_count) * (2.0 * math.pi / node_count)
    c, s = np.cos(phase), np.sin(phase)
    k = np.arange(half + 1, dtype=np.float64)
    inside = (k > 0) & (k < half)
    u = np.where(inside, 2.0 * k / half, 0.0)
    w = np.where(inside, 2.0 * (k / half) ** 4, np.where(k == half, 1.0, 0.0))
    derivative = ((c * u) @ s.T - (s * u) @ c.T) / node_count
    bending_table = ((c * w) @ c.T + (s * w) @ s.T) / node_count
    return derivative.T.astype(np.float32), bending_table.T.astype(np.float32)


def iota(shape, axis):
    return lax.broadcasted_iota(jnp.int32, shape, axis)


def dot(a, b, dims=NN, precision=None):
    return lax.dot_general(a, b, dims, precision=precision, preferred_element_type=F32)


def reciprocal(x):
    return pl.reciprocal(x, approx=True)


def fetch(sources, targets, sems, meanwhile=None):
    copies = [pltpu.make_async_copy(s, t, sems.at[i])
              for i, (s, t) in enumerate(zip(sources, targets))]
    for copy in copies:
        copy.start()
    if meanwhile is not None:
        meanwhile()
    for copy in copies:
        copy.wait()


def piece_kernel(own_in, nodes_in, sent_ref, own_ref, nodes_ref, sems):
    fetch([own_in, nodes_in], [own_ref, nodes_ref], sems)
    half = own_ref.shape[0] // 2
    core = lax.rem(lax.axis_index("clu"), 2)
    mine = own_ref[pl.ds(pl.multiple_of(core * half, half), half), :]
    spots = nodes_ref[...].astype(F32)
    lanes = sent_ref.shape[1]
    columns = own_ref.shape[1] // lanes
    for c in range(columns):
        sent_ref[c * half:(c + 1) * half] = mine[:, c * lanes:(c + 1) * lanes]
    spots = jnp.concatenate([spots[:, c * lanes:(c + 1) * lanes] for c in range(columns)], axis=0)
    tail = sent_ref.shape[0] - columns * half
    spots = jnp.concatenate([spots, jnp.zeros((tail - 2 * columns, lanes), F32)], axis=0)
    sent_ref[columns * half:] = spots.astype(BF16)


def cube_place(destination, own, count):
    relative = jnp.bitwise_xor(destination, own)
    place = jnp.zeros_like(relative)
    bit = 1
    while bit < count:
        place = 2 * place + jnp.bitwise_and(relative, bit) // bit
        bit *= 2
    return place


def cube_exchange(kept, leaving, axis):
    count = lax.axis_size(axis)
    assert power_of_two(count)
    held = [kept]
    bit = 1
    while True:
        held.append(lax.ppermute(leaving, axis, partners(count, bit)))
        bit *= 2
        if bit >= count:
            return held
        span = count // bit
        tails = []
        for h, part in enumerate(held):
            cut = part.reshape(-1, span, *part.shape[-2:])
            tails.append(cut[:, span // 2:].reshape(-1, *part.shape[-2:]))
            held[h] = cut[:, :span // 2].reshape(-1, *part.shape[-2:])
        leaving = jnp.concatenate(tails, axis=0)


def force_kernel(clu_count, *refs):
    sources, targets, sems = refs[:8], refs[11:19], refs[19]
    force_ref, kept_ref, leaving_ref = refs[8:11]
    fetch(sources, targets, sems)
    (pos_ref, ten_ref, bend_ref, order_ref, dest_ref, target_ref, deriv_ref, table_ref) = targets
    vesicles = ten_ref.shape[0]
    moves = target_ref.shape[1]
    x = pos_ref[pl.ds(0, vesicles, stride=2), :]
    y = pos_ref[pl.ds(1, vesicles, stride=2), :]
    rows = jnp.concatenate([x, y], axis=0)
    deriv = deriv_ref[...]
    tension = jnp.concatenate([ten_ref[...]] * 2, axis=0)
    eye = iota((vesicles, vesicles), 0) == iota((vesicles, vesicles), 1)
    bend = jnp.sum(jnp.where(eye, bend_ref[...], 0.0), axis=1, keepdims=True)
    bend = jnp.concatenate([bend] * 2, axis=0)
    slope = dot(rows, deriv, precision=HIGHEST)
    fourth = dot(rows, table_ref[...], precision=HIGHEST)
    force = dot(tension * slope, deriv, precision=HIGHEST) - bend * fourth
    force_x, force_y = force[:vesicles], force[vesicles:]
    force_ref[pl.ds(0, vesicles, stride=2), :] = force_x
    force_ref[pl.ds(1, vesicles, stride=2), :] = force_y

    slots = clu_count * BLOCK
    place = cube_place(dest_ref[...], lax.axis_index("clu"), clu_count)
    hot = (iota((clu_count, moves), 0) == place).astype(F32)
    earlier = (iota((moves, moves), 0) < iota((moves, moves), 1)).astype(F32)
    rank = jnp.sum(dot(hot, earlier) * hot, axis=0, keepdims=True).astype(jnp.int32)
    slot = place * BLOCK + rank
    pack = (iota((slots, moves), 0) == slot).astype(F32)
    pick = (iota((vesicles, moves), 0) == order_ref[:, :moves]).astype(F32)
    select = dot(pack, pick, NT)
    carried = jnp.concatenate([x, y, force_x, force_y], axis=1)
    packed = dot(select, carried, precision=HIGHEST)
    tag = jnp.sum(pack * (target_ref[...] + 1).astype(F32), axis=1, keepdims=True)
    tag = jnp.broadcast_to(tag, (slots, x.shape[1]))
    packed = jnp.concatenate([packed, tag], axis=1)
    packed = packed.reshape(clu_count, BLOCK, packed.shape[1])
    kept_ref[...] = packed[:clu_count // 2]
    leaving_ref[...] = packed[clu_count // 2:]


def near_slot(turned, tx, ty):
    nodes = tx.shape[1]
    chunk = 32 if nodes % 32 == 0 else nodes

    def fold(value):
        return jnp.sum(value.reshape(-1, 8, nodes), axis=0)

    logs_x = logs_y = pulls_x = pulls_y = jnp.zeros((8, nodes), F32)
    for start in range(0, nodes, chunk):
        sx, sy, fx, fy = [
            jnp.broadcast_to(t[start:start + chunk], (chunk, nodes)) for t in turned]
        dx = tx - sx
        dy = ty - sy
        spread = dx * dx + dy * dy + EPS_SQUARED
        logs = jnp.log(spread)
        along = (dx * fx + dy * fy) * reciprocal(spread)
        logs_x, logs_y = logs_x + fold(logs * fx), logs_y + fold(logs * fy)
        pulls_x, pulls_y = pulls_x + fold(dx * along), pulls_y + fold(dy * along)
    return (jnp.sum(pulls_x - 0.5 * logs_x, axis=0, keepdims=True),
            jnp.sum(pulls_y - 0.5 * logs_y, axis=0, keepdims=True))


def near_piece(data, tx, ty, slot_cap):
    nodes = tx.shape[1]
    turned = [data[:, c * nodes:(c + 1) * nodes].T for c in range(4)]
    return [functools.partial(near_slot, [t[:, h:h + 1] for t in turned], tx[h:h + 1], ty[h:h + 1])
            for h in range(slot_cap)]


def gather_rows(slots, axis):
    nodes = slots[0][axis].shape[1]
    rest = [jnp.zeros((BLOCK - len(slots), nodes), F32)] if len(slots) < BLOCK else []
    return jnp.concatenate([slot[axis] for slot in slots] + rest, axis=0)


def target_table(tag, vesicles):
    tag = tag.reshape(-1, tag.shape[-1])[:, :vesicles]
    return (tag == (iota(tag.shape, 1) + 1).astype(F32)).astype(F32)


def axis_rows(vesicles, axis):
    return pl.ds(axis, vesicles, stride=2)


def near_kernel(slot_cap, piece_count, pos_ref, *refs):
    piece_refs, before_refs = refs[:piece_count], refs[piece_count:-6]
    near_ref, arrived, aim_x, aim_y, speed_x, speed_y = refs[-6:]
    vesicles, nodes = pos_ref.shape[0] // 2, pos_ref.shape[1]
    here = 0
    for ref in piece_refs:
        arrived[here:here + ref.shape[0]] = ref[...]
        here += ref.shape[0]
    pieces = arrived.shape[0]
    hot = target_table(arrived[:, :, 4 * nodes:], vesicles)
    for axis, aim in enumerate((aim_x, aim_y)):
        aim[...] = dot(hot, pos_ref[axis_rows(vesicles, axis), :], precision=HIGHEST).reshape(
            pieces, BLOCK, nodes)
    many = math.gcd(pieces, 4)

    def group(i, _):
        calls = [near_piece(arrived[i * many + c], aim_x[i * many + c], aim_y[i * many + c],
                            slot_cap) for c in range(many)]
        slots = [[call() for call in piece] for piece in calls]
        for c, piece in enumerate(slots):
            speed_x[i * many + c] = gather_rows(piece, 0)
            speed_y[i * many + c] = gather_rows(piece, 1)
        return 0

    lax.fori_loop(0, pieces // many, group, 0)
    turned_hot = hot.T
    for axis, speed in enumerate((speed_x, speed_y)):
        rows = axis_rows(vesicles, axis)
        near = dot(turned_hot, speed[...].reshape(-1, nodes), precision=HIGHEST) / nodes
        for before_ref in before_refs:
            near = near + before_ref[rows, :]
        near_ref[rows, :] = near


def near_part(flat, pieces, before, slot_cap):
    vesicles, nodes = flat.shape[0] // 2, flat.shape[1]
    count = sum(p.shape[0] for p in pieces)
    return pl.pallas_call(
        functools.partial(near_kernel, slot_cap, len(pieces)),
        out_shape=jax.ShapeDtypeStruct((2 * vesicles, nodes), F32),
        in_specs=[whole_spec()] * (1 + len(pieces) + len(before)),
        out_specs=whole_spec(),
        scratch_shapes=[pltpu.VMEM((count, BLOCK, 5 * nodes), F32)]
        + [pltpu.VMEM((count, BLOCK, nodes), F32)] * 4,
        compiler_params=params(16),
        cost_estimate=pl.CostEstimate(
            flops=10**9, bytes_accessed=10**7, transcendentals=10**6),
    )(flat, *pieces, *before)


def far_kernel(col_count, range_in, pos_in, own_in, nodes_in, *refs):
    count = 2 * (col_count - 1)
    piece_refs = refs[:count]
    (high_ref, low_ref, gram_ref, range_ref, pos_ref, own_nodes, own_rows, basis, spots, wide,
     sums, sems) = refs[count:]
    vesicles = pos_ref.shape[0] // 2
    nodes = pos_ref.shape[1]
    rank, sources = own_rows.shape[0] // 2, own_rows.shape[1]
    rows = 2 * rank
    core, col = lax.rem(lax.axis_index("clu"), 2), lax.axis_index("col")
    columns = sources // nodes

    def widen(r):
        turned = spots[r].T
        for c in range(2):
            wide[r, c] = jnp.broadcast_to(turned[:, c:c + 1], (sources, nodes))

    def lay_out_received():
        for k in range(1, col_count):
            where = origin(col, k, col_count)
            mine, other = piece_refs[2 * k - 2], piece_refs[2 * k - 1]
            ends = mine[columns * rank:].astype(F32)
            for c in range(columns):
                lanes = slice(c * nodes, (c + 1) * nodes)
                from_rows = slice(c * rank, (c + 1) * rank)
                for ref, part in ((mine, core), (other, 1 - core)):
                    there = pl.multiple_of(part * sources + c * nodes, nodes)
                    basis[where, :, pl.ds(there, nodes)] = ref[from_rows]
                spots[where, 0:2, lanes] = ends[2 * c:2 * c + 2]
            widen(where)

    fetch([range_in, pos_in, nodes_in, own_in], [range_ref, pos_ref, own_nodes, own_rows], sems,
          lay_out_received)
    basis[col, :, :sources] = own_rows[:rank]
    basis[col, :, sources:] = own_rows[rank:]
    spots[col, 0:2] = own_nodes[...].astype(F32)
    widen(col)
    sums[...] = jnp.zeros_like(sums)

    chunk = 32 if sources % 32 == 0 else sources
    depth = 256 if sources % 256 == 0 else sources

    def evaluate(v, start):
        r = range_ref[0, v]
        tx = pos_ref[pl.ds(2 * v, 1), :]
        ty = pos_ref[pl.ds(2 * v + 1, 1), :]
        dx = tx - wide[r, 0, start:start + chunk]
        dy = ty - wide[r, 1, start:start + chunk]
        xx, yy = dx * dx, dy * dy
        spread = xx + yy + EPS_SQUARED
        log_part = -0.5 * jnp.log(spread)
        inverse = reciprocal(spread)
        return ((log_part + xx * inverse).astype(BF16), (dx * dy * inverse).astype(BF16),
                (log_part + yy * inverse).astype(BF16))

    def sketch(v):
        r = range_ref[0, v]
        total = None
        for start in range(0, sources, depth):
            ff, fs, ss = [jnp.concatenate(p, axis=0) for p in zip(
                *[evaluate(v, start + c) for c in range(0, depth, chunk)])]
            part = dot(basis[r, :, start:start + depth], jnp.concatenate([ff, fs], axis=1))
            part += dot(basis[r, :, sources + start:sources + start + depth],
                        jnp.concatenate([fs, ss], axis=1))
            total = part if total is None else total + part
        return total

    many = math.gcd(vesicles, 8)

    def group_gram(v):
        both = jnp.concatenate([
            jnp.concatenate([ref[v + c] for c in range(many)], axis=1)
            for ref in (high_ref, low_ref)], axis=0)
        return dot(both, both, NT)

    high_ref[0:many] = jnp.zeros((many, rank, 2 * nodes), BF16)
    low_ref[0:many] = jnp.zeros((many, rank, 2 * nodes), BF16)

    def group(i, _):
        v = many * i
        before = group_gram(jnp.maximum(v - many, 0))
        made = [sketch(v + c) for c in range(many)]
        sums[...] += before
        for c, value in enumerate(made):
            high = value.astype(BF16)
            high_ref[v + c] = high
            low_ref[v + c] = (value - high.astype(F32)).astype(BF16)
        return 0

    lax.fori_loop(0, vesicles // many, group, 0)
    sums[...] += group_gram(vesicles - many)
    total = sums[...]
    gram = total[:rank, :rank] + total[rank:, rank:] + (total[:rank, rank:] + total[rank:, :rank])
    gram_ref[...] = jnp.concatenate([gram[:rank // 2], gram[rank // 2:]], axis=1)


def lower_inverse(gram):
    size = gram.shape[0]
    eye = (iota((size, size), 0) == iota((size, size), 1)).astype(F32)
    rest = jnp.concatenate([gram, eye], axis=1)
    done = []
    step = 8
    for start in range(0, size, step):
        height = size - start
        columns = [jnp.broadcast_to(rest[:, start + j:start + j + 1], (height, 2 * size))
                   for j in range(step)]
        row_number = iota((height, 2 * size), 0)
        scale = jnp.zeros((step, 2 * size), F32)
        for j in range(step):
            column = columns[j]
            pivot = column[j:j + 1]
            factor = jnp.where(row_number > j, column * reciprocal(pivot), 0.0)
            for later in range(j + 1, step):
                columns[later] = columns[later] - factor * column[later:later + 1]
            rest = rest - factor * rest[j:j + 1]
            root = lax.rsqrt(pivot)
            root = root * (1.5 - 0.5 * pivot * root * root)
            scale = jnp.where(row_number[:step] == j, root, scale)
        done.append(rest[:step] * scale)
        rest = rest[step:]
    return jnp.concatenate(done, axis=0)[:, size:]


def basis_kernel(scale_factor, groups, gram_ref, high_ref, low_ref, _, out_ref, made, sems):
    vesicles, rank, nodes = high_ref.shape[0], high_ref.shape[1], high_ref.shape[2] // 2
    folded = gram_ref[...]
    gram = jnp.concatenate([folded[:, :rank], folded[:, rank:]], axis=0)
    inverse = lower_inverse(gram) * scale_factor
    high = inverse.astype(BF16)
    low = (inverse - high.astype(F32)).astype(BF16)
    weight = jnp.concatenate([high, high, low], axis=1)
    size = vesicles // groups
    many = math.gcd(size, 4)
    copies = []
    for g in range(groups):
        for v in range(g * size, (g + 1) * size, many):
            fresh = [dot(weight, jnp.concatenate([high_ref[u], low_ref[u], high_ref[u]], axis=0))
                     for u in range(v, v + many)]
            for u, value in enumerate(fresh):
                for d in range(2):
                    made[v + u, pl.ds(d, rank, stride=2), :] = value[:, d * nodes:(d + 1) * nodes]
        here = slice(g * size, (g + 1) * size)
        copies.append(pltpu.make_async_copy(made.at[here], out_ref.at[here], sems.at[g]))
        copies[-1].start()
    for copy in copies:
        copy.wait()


def whole_spec():
    return pl.BlockSpec(memory_space=pltpu.VMEM)


def far_off_spec():
    return pl.BlockSpec(memory_space=pltpu.HBM)


def params(mib):
    return pltpu.CompilerParams(vmem_limit_bytes=mib * MIB)


def power_of_two(count):
    return count & (count - 1) == 0


def partners(count, step):
    if power_of_two(count):
        return [(i, i ^ step) for i in range(count)]
    return [(i, (i + step) % count) for i in range(count)]


def origin(index, step, count):
    if power_of_two(count):
        return jnp.bitwise_xor(index, step)
    return lax.rem(index - step + count, count)


def step_groups(count, single_first):
    if not power_of_two(count):
        return [list(range(1, count))]
    groups, bit = [], 1
    if single_first and count > 1:
        groups, bit = [[1]], 2
    while bit < count:
        groups.append([bit] if 2 * bit >= count else [bit, 2 * bit, 3 * bit])
        bit *= 4
    return groups


def add_kernel(count, *refs):
    total = refs[0][...]
    for ref in refs[1:count]:
        total = total + ref[...]
    refs[-1][...] = total


def add_after(terms, others):
    return pl.pallas_call(
        functools.partial(add_kernel, len(terms)),
        out_shape=jax.ShapeDtypeStruct(terms[0].shape, terms[0].dtype),
        in_specs=[whole_spec()] * len(terms) + [far_off_spec()] * len(others),
        out_specs=whole_spec(),
        compiler_params=params(16),
        cost_estimate=pl.CostEstimate(flops=10**4, bytes_accessed=10**5, transcendentals=0),
    )(*terms, *others)


def sum_over(value, axis, groups, others=None):
    count = lax.axis_size(axis)
    for g, steps in enumerate(groups):
        terms = [value] + [lax.ppermute(value, axis, partners(count, k)) for k in steps]
        if others is not None and g == len(groups) - 1:
            value = add_after(terms, others)
        else:
            value = sum(terms[1:], value)
    return value


def per_device(positions, tension, bending, moved_order, move_destination, move_target, far_range,
               old_basis, source_nodes):
    vesicles, _, nodes = positions.shape
    rows, sources = old_basis.shape
    rank = rows // 2
    clu_count, col_count = lax.axis_size("clu"), lax.axis_size("col")
    moves = move_target.shape[0]
    slot_cap = 2 * ((moves + clu_count - 1) // clu_count)
    flat = positions.reshape(2 * vesicles, nodes)

    columns = sources // nodes
    sent_rows = columns * rank + (2 * columns + 15) // 16 * 16
    deriv, table = spectral_tables(nodes)
    near_by = functools.partial(pltpu.with_memory_space_constraint, memory_space=pltpu.HBM)
    basis_here, nodes_here, flat_here = near_by(old_basis), near_by(source_nodes), near_by(flat)
    sent = pl.pallas_call(
        piece_kernel,
        out_shape=jax.ShapeDtypeStruct((sent_rows, nodes), BF16),
        in_specs=[far_off_spec()] * 2,
        out_specs=whole_spec(),
        scratch_shapes=[pltpu.VMEM(old_basis.shape, BF16), pltpu.VMEM(source_nodes.shape, BF16),
                        pltpu.SemaphoreType.DMA((2,))],
        compiler_params=params(16),
        cost_estimate=pl.CostEstimate(flops=10**5, bytes_accessed=10**5, transcendentals=0),
    )(basis_here, nodes_here)

    operands = [flat, tension, bending.reshape(1, vesicles), moved_order,
                move_destination.reshape(1, moves), move_target.reshape(1, moves),
                jnp.asarray(deriv), jnp.asarray(table)]
    operands = [flat_here] + [near_by(o) for o in operands[1:]]
    force, kept, leaving = pl.pallas_call(
        functools.partial(force_kernel, clu_count),
        out_shape=[jax.ShapeDtypeStruct((2 * vesicles, nodes), F32),
                   *[jax.ShapeDtypeStruct((clu_count // 2, BLOCK, 5 * nodes), F32)] * 2],
        in_specs=[far_off_spec()] * len(operands),
        out_specs=[whole_spec()] * 3,
        scratch_shapes=[pltpu.VMEM(o.shape, o.dtype) for o in operands]
        + [pltpu.SemaphoreType.DMA((len(operands),))],
        compiler_params=params(16),
        cost_estimate=pl.CostEstimate(flops=10**8, bytes_accessed=10**6, transcendentals=0),
    )(*operands)

    moved_halves = [lax.ppermute(sent, "col", partners(col_count, k)) for k in range(1, col_count)]
    arrived = cube_exchange(kept, leaving, "clu")
    pieces = []
    for mine in moved_halves:
        pieces += [mine, lax.ppermute(mine, "clu", [(i, i ^ 1) for i in range(clu_count)])]

    near_first = near_part(flat, arrived[:-1], [], slot_cap)
    near = near_part(flat, arrived[-1:], [near_first], slot_cap)

    high, low, gram = pl.pallas_call(
        functools.partial(far_kernel, col_count),
        out_shape=[jax.ShapeDtypeStruct((vesicles, rank, 2 * nodes), BF16)] * 2
        + [jax.ShapeDtypeStruct((rank // 2, 2 * rank), F32)],
        in_specs=[far_off_spec()] * 4 + [whole_spec()] * (2 * (col_count - 1)),
        out_specs=[whole_spec()] * 3,
        scratch_shapes=[
            pltpu.SMEM((1, vesicles), jnp.int32),
            pltpu.VMEM((2 * vesicles, nodes), F32),
            pltpu.VMEM((2, sources), BF16),
            pltpu.VMEM((rows, sources), BF16),
            pltpu.VMEM((col_count, rank, 2 * sources), BF16),
            pltpu.VMEM((col_count, 8, sources), F32),
            pltpu.VMEM((col_count, 2, sources, nodes), F32),
            pltpu.VMEM((rows, rows), F32),
            pltpu.SemaphoreType.DMA((4,))],
        compiler_params=params(32),
        cost_estimate=pl.CostEstimate(flops=10**10, bytes_accessed=10**7, transcendentals=10**7),
    )(near_by(far_range.reshape(1, vesicles)), flat_here, basis_here, nodes_here, *pieces)
    gram = sum_over(gram, "clu", step_groups(clu_count, True), [near_first, arrived[-1]])
    gram = sum_over(gram, "col", step_groups(col_count, False))

    scale_factor = math.sqrt(2.0 * nodes * vesicles * clu_count * col_count)
    groups = math.gcd(vesicles, 8)
    new_basis = pl.pallas_call(
        functools.partial(basis_kernel, scale_factor, groups),
        out_shape=jax.ShapeDtypeStruct((vesicles, rows, nodes), F32),
        in_specs=[whole_spec()] * 3 + [far_off_spec()],
        out_specs=far_off_spec(),
        scratch_shapes=[pltpu.VMEM((vesicles, rows, nodes), F32),
                        pltpu.SemaphoreType.DMA((groups,))],
        compiler_params=params(16),
        cost_estimate=pl.CostEstimate(flops=10**9, bytes_accessed=10**7, transcendentals=0),
    )(gram, high, low, near_by(near))

    return (force.reshape(vesicles, 2, nodes), near.reshape(vesicles, 2, nodes),
            new_basis.reshape(vesicles, rank, 2, nodes))


def solution(mesh):
    both = ("clu", "col")
    placed = (
        P(both, None, None), P(both, None), P(both), P(both, None), P(both, None), P(both),
        P(both, None), P(None, "col"), P(None, "col"),
    )
    return jax.shard_map(
        per_device,
        mesh=mesh,
        in_specs=placed,
        out_specs=(P(both, None, None), P(both, None, None), P(both, None, None, None)),
        check_vma=False,
    )
```

```python
import functools
import math

import jax
import jax.numpy as jnp
import numpy as np
from jax import lax
from jax.experimental import pallas as pl
from jax.experimental.pallas import tpu as pltpu
from jax.sharding import PartitionSpec as P

EPS_SQUARED = 0.01
F32 = jnp.float32
BF16 = jnp.bfloat16
HIGHEST = lax.Precision.HIGHEST
BLOCK = 8
MIB = 1 << 20

NT = (((1,), (1,)), ((), ()))
NN = (((1,), (0,)), ((), ()))


def spectral_tables(node_count):
    half = node_count // 2
    j = np.arange(node_count)[:, None]
    k = np.arange(half + 1)[None, :]
    phase = (j * k % node_count) * (2.0 * math.pi / node_count)
    c, s = np.cos(phase), np.sin(phase)
    k = np.arange(half + 1, dtype=np.float64)
    inside = (k > 0) & (k < half)
    u = np.where(inside, 2.0 * k / half, 0.0)
    w = np.where(inside, 2.0 * (k / half) ** 4, np.where(k == half, 1.0, 0.0))
    derivative = ((c * u) @ s.T - (s * u) @ c.T) / node_count
    bending_table = ((c * w) @ c.T + (s * w) @ s.T) / node_count
    return derivative.T.astype(np.float32), bending_table.T.astype(np.float32)


def iota(shape, axis):
    return lax.broadcasted_iota(jnp.int32, shape, axis)


def dot(a, b, dims=NN, precision=None):
    return lax.dot_general(a, b, dims, precision=precision, preferred_element_type=F32)


def reciprocal(x):
    return pl.reciprocal(x, approx=True)


def fetch(sources, targets, sems, meanwhile=None):
    copies = [pltpu.make_async_copy(s, t, sems.at[i])
              for i, (s, t) in enumerate(zip(sources, targets))]
    for copy in copies:
        copy.start()
    if meanwhile is not None:
        meanwhile()
    for copy in copies:
        copy.wait()


def piece_kernel(own_in, nodes_in, sent_ref, own_ref, nodes_ref, sems):
    fetch([own_in, nodes_in], [own_ref, nodes_ref], sems)
    half = own_ref.shape[0] // 2
    core = lax.rem(lax.axis_index("clu"), 2)
    mine = own_ref[pl.ds(pl.multiple_of(core * half, half), half), :]
    spots = nodes_ref[...].astype(F32)
    lanes = sent_ref.shape[1]
    columns = own_ref.shape[1] // lanes
    for c in range(columns):
        sent_ref[c * half:(c + 1) * half] = mine[:, c * lanes:(c + 1) * lanes]
    spots = jnp.concatenate([spots[:, c * lanes:(c + 1) * lanes] for c in range(columns)], axis=0)
    tail = sent_ref.shape[0] - columns * half
    spots = jnp.concatenate([spots, jnp.zeros((tail - 2 * columns, lanes), F32)], axis=0)
    sent_ref[columns * half:] = spots.astype(BF16)


def cube_place(destination, own, count):
    relative = jnp.bitwise_xor(destination, own)
    place = jnp.zeros_like(relative)
    bit = 1
    while bit < count:
        place = 2 * place + jnp.bitwise_and(relative, bit) // bit
        bit *= 2
    return place


def cube_exchange(kept, leaving, axis):
    count = lax.axis_size(axis)
    assert power_of_two(count)
    held = [kept]
    bit = 1
    while True:
        held.append(lax.ppermute(leaving, axis, partners(count, bit)))
        bit *= 2
        if bit >= count:
            return held
        span = count // bit
        tails = []
        for h, part in enumerate(held):
            cut = part.reshape(-1, span, *part.shape[-2:])
            tails.append(cut[:, span // 2:].reshape(-1, *part.shape[-2:]))
            held[h] = cut[:, :span // 2].reshape(-1, *part.shape[-2:])
        leaving = jnp.concatenate(tails, axis=0)


def force_kernel(clu_count, *refs):
    sources, targets, sems = refs[:8], refs[11:19], refs[19]
    force_ref, kept_ref, leaving_ref = refs[8:11]
    fetch(sources, targets, sems)
    (pos_ref, ten_ref, bend_ref, order_ref, dest_ref, target_ref, deriv_ref, table_ref) = targets
    vesicles = ten_ref.shape[0]
    moves = target_ref.shape[1]
    x = pos_ref[pl.ds(0, vesicles, stride=2), :]
    y = pos_ref[pl.ds(1, vesicles, stride=2), :]
    rows = jnp.concatenate([x, y], axis=0)
    deriv = deriv_ref[...]
    tension = jnp.concatenate([ten_ref[...]] * 2, axis=0)
    eye = iota((vesicles, vesicles), 0) == iota((vesicles, vesicles), 1)
    bend = jnp.sum(jnp.where(eye, bend_ref[...], 0.0), axis=1, keepdims=True)
    bend = jnp.concatenate([bend] * 2, axis=0)
    both = dot(rows, jnp.concatenate([deriv, table_ref[...]], axis=1), precision=HIGHEST)
    slope, fourth = both[:, :rows.shape[1]], both[:, rows.shape[1]:]
    force = dot(tension * slope, deriv, precision=HIGHEST) - bend * fourth
    force_x, force_y = force[:vesicles], force[vesicles:]
    force_ref[pl.ds(0, vesicles, stride=2), :] = force_x
    force_ref[pl.ds(1, vesicles, stride=2), :] = force_y

    slots = clu_count * BLOCK
    place = cube_place(dest_ref[...], lax.axis_index("clu"), clu_count)
    hot = (iota((clu_count, moves), 0) == place).astype(F32)
    earlier = (iota((moves, moves), 0) < iota((moves, moves), 1)).astype(F32)
    rank = jnp.sum(dot(hot, earlier) * hot, axis=0, keepdims=True).astype(jnp.int32)
    slot = place * BLOCK + rank
    pack = (iota((slots, moves), 0) == slot).astype(F32)
    pick = (iota((vesicles, moves), 0) == order_ref[:, :moves]).astype(F32)
    select = dot(pack, pick, NT)
    carried = jnp.concatenate([x, y, force_x, force_y], axis=1)
    packed = dot(select, carried, precision=HIGHEST)
    tag = jnp.sum(pack * (target_ref[...] + 1).astype(F32), axis=1, keepdims=True)
    tag = jnp.broadcast_to(tag, (slots, x.shape[1]))
    packed = jnp.concatenate([packed, tag], axis=1)
    packed = packed.reshape(clu_count, BLOCK, packed.shape[1])
    kept_ref[...] = packed[:clu_count // 2]
    leaving_ref[...] = packed[clu_count // 2:]


def near_slot(turned, tx, ty):
    nodes = tx.shape[1]
    chunk = 32 if nodes % 32 == 0 else nodes

    def fold(value):
        return jnp.sum(value.reshape(-1, 8, nodes), axis=0)

    logs_x = logs_y = pulls_x = pulls_y = jnp.zeros((8, nodes), F32)
    for start in range(0, nodes, chunk):
        sx, sy, fx, fy = [
            jnp.broadcast_to(t[start:start + chunk], (chunk, nodes)) for t in turned]
        dx = tx - sx
        dy = ty - sy
        spread = dx * dx + dy * dy + EPS_SQUARED
        logs = jnp.log(spread)
        along = (dx * fx + dy * fy) * reciprocal(spread)
        logs_x, logs_y = logs_x + fold(logs * fx), logs_y + fold(logs * fy)
        pulls_x, pulls_y = pulls_x + fold(dx * along), pulls_y + fold(dy * along)
    return (jnp.sum(pulls_x - 0.5 * logs_x, axis=0, keepdims=True),
            jnp.sum(pulls_y - 0.5 * logs_y, axis=0, keepdims=True))


def near_piece(data, tx, ty, slot_cap):
    nodes = tx.shape[1]
    turned = [data[:, c * nodes:(c + 1) * nodes].T for c in range(4)]
    return [functools.partial(near_slot, [t[:, h:h + 1] for t in turned], tx[h:h + 1], ty[h:h + 1])
            for h in range(slot_cap)]


def gather_rows(slots, axis):
    nodes = slots[0][axis].shape[1]
    rest = [jnp.zeros((BLOCK - len(slots), nodes), F32)] if len(slots) < BLOCK else []
    return jnp.concatenate([slot[axis] for slot in slots] + rest, axis=0)


def target_table(tag, vesicles):
    tag = tag.reshape(-1, tag.shape[-1])[:, :vesicles]
    return (tag == (iota(tag.shape, 1) + 1).astype(F32)).astype(F32)


def axis_rows(vesicles, axis):
    return pl.ds(axis, vesicles, stride=2)


def near_kernel(slot_cap, piece_count, pos_ref, *refs):
    piece_refs, before_refs = refs[:piece_count], refs[piece_count:-6]
    near_ref, arrived, aim_x, aim_y, speed_x, speed_y = refs[-6:]
    vesicles, nodes = pos_ref.shape[0] // 2, pos_ref.shape[1]
    here = 0
    for ref in piece_refs:
        arrived[here:here + ref.shape[0]] = ref[...]
        here += ref.shape[0]
    pieces = arrived.shape[0]
    hot = target_table(arrived[:, :, 4 * nodes:], vesicles)
    for axis, aim in enumerate((aim_x, aim_y)):
        aim[...] = dot(hot, pos_ref[axis_rows(vesicles, axis), :], precision=HIGHEST).reshape(
            pieces, BLOCK, nodes)
    many = math.gcd(pieces, 4)

    def group(i, _):
        calls = [near_piece(arrived[i * many + c], aim_x[i * many + c], aim_y[i * many + c],
                            slot_cap) for c in range(many)]
        slots = [[call() for call in piece] for piece in calls]
        for c, piece in enumerate(slots):
            speed_x[i * many + c] = gather_rows(piece, 0)
            speed_y[i * many + c] = gather_rows(piece, 1)
        return 0

    lax.fori_loop(0, pieces // many, group, 0)
    turned_hot = hot.T
    for axis, speed in enumerate((speed_x, speed_y)):
        rows = axis_rows(vesicles, axis)
        near = dot(turned_hot, speed[...].reshape(-1, nodes), precision=HIGHEST) / nodes
        for before_ref in before_refs:
            near = near + before_ref[rows, :]
        near_ref[rows, :] = near


def near_part(flat, pieces, before, slot_cap):
    vesicles, nodes = flat.shape[0] // 2, flat.shape[1]
    count = sum(p.shape[0] for p in pieces)
    return pl.pallas_call(
        functools.partial(near_kernel, slot_cap, len(pieces)),
        out_shape=jax.ShapeDtypeStruct((2 * vesicles, nodes), F32),
        in_specs=[whole_spec()] * (1 + len(pieces) + len(before)),
        out_specs=whole_spec(),
        scratch_shapes=[pltpu.VMEM((count, BLOCK, 5 * nodes), F32)]
        + [pltpu.VMEM((count, BLOCK, nodes), F32)] * 4,
        compiler_params=params(16),
        cost_estimate=pl.CostEstimate(
            flops=10**9, bytes_accessed=10**7, transcendentals=10**6),
    )(flat, *pieces, *before)


def far_kernel(col_count, range_in, pos_in, own_in, nodes_in, *refs):
    count = 2 * (col_count - 1)
    piece_refs = refs[:count]
    (high_ref, low_ref, gram_ref, range_ref, pos_ref, own_nodes, own_rows, basis, spots, wide,
     sums, sems) = refs[count:]
    vesicles = pos_ref.shape[0] // 2
    nodes = pos_ref.shape[1]
    rank, sources = own_rows.shape[0] // 2, own_rows.shape[1]
    rows = 2 * rank
    core, col = lax.rem(lax.axis_index("clu"), 2), lax.axis_index("col")
    columns = sources // nodes

    def widen(r):
        turned = spots[r].T
        for c in range(2):
            wide[r, c] = jnp.broadcast_to(turned[:, c:c + 1], (sources, nodes))

    def lay_out_received():
        for k in range(1, col_count):
            where = origin(col, k, col_count)
            mine, other = piece_refs[2 * k - 2], piece_refs[2 * k - 1]
            ends = mine[columns * rank:].astype(F32)
            for c in range(columns):
                lanes = slice(c * nodes, (c + 1) * nodes)
                from_rows = slice(c * rank, (c + 1) * rank)
                for ref, part in ((mine, core), (other, 1 - core)):
                    there = pl.multiple_of(part * sources + c * nodes, nodes)
                    basis[where, :, pl.ds(there, nodes)] = ref[from_rows]
                spots[where, 0:2, lanes] = ends[2 * c:2 * c + 2]
            widen(where)

    fetch([range_in, pos_in, nodes_in, own_in], [range_ref, pos_ref, own_nodes, own_rows], sems,
          lay_out_received)
    basis[col, :, :sources] = own_rows[:rank]
    basis[col, :, sources:] = own_rows[rank:]
    spots[col, 0:2] = own_nodes[...].astype(F32)
    widen(col)
    sums[...] = jnp.zeros_like(sums)

    chunk = 32 if sources % 32 == 0 else sources
    depth = 256 if sources % 256 == 0 else sources

    def evaluate(v, start):
        r = range_ref[0, v]
        tx = pos_ref[pl.ds(2 * v, 1), :]
        ty = pos_ref[pl.ds(2 * v + 1, 1), :]
        dx = tx - wide[r, 0, start:start + chunk]
        dy = ty - wide[r, 1, start:start + chunk]
        xx, yy = dx * dx, dy * dy
        spread = xx + yy + EPS_SQUARED
        log_part = -0.5 * jnp.log(spread)
        inverse = reciprocal(spread)
        return ((log_part + xx * inverse).astype(BF16), (dx * dy * inverse).astype(BF16),
                (log_part + yy * inverse).astype(BF16))

    def sketch(v):
        r = range_ref[0, v]
        total = None
        for start in range(0, sources, depth):
            ff, fs, ss = [jnp.concatenate(p, axis=0) for p in zip(
                *[evaluate(v, start + c) for c in range(0, depth, chunk)])]
            part = dot(basis[r, :, start:start + depth], jnp.concatenate([ff, fs], axis=1))
            part += dot(basis[r, :, sources + start:sources + start + depth],
                        jnp.concatenate([fs, ss], axis=1))
            total = part if total is None else total + part
        return total

    many = math.gcd(vesicles, 16)

    def group_gram(v):
        both = jnp.concatenate([
            jnp.concatenate([ref[v + c] for c in range(many)], axis=1)
            for ref in (high_ref, low_ref)], axis=0)
        return dot(both, both, NT)

    high_ref[0:many] = jnp.zeros((many, rank, 2 * nodes), BF16)
    low_ref[0:many] = jnp.zeros((many, rank, 2 * nodes), BF16)

    def group(i, _):
        v = many * i
        before = group_gram(jnp.maximum(v - many, 0))
        made = [sketch(v + c) for c in range(many)]
        sums[...] += before
        for c, value in enumerate(made):
            high = value.astype(BF16)
            high_ref[v + c] = high
            low_ref[v + c] = (value - high.astype(F32)).astype(BF16)
        return 0

    lax.fori_loop(0, vesicles // many, group, 0)
    sums[...] += group_gram(vesicles - many)
    total = sums[...]
    gram = total[:rank, :rank] + total[rank:, rank:] + (total[:rank, rank:] + total[rank:, :rank])
    gram_ref[...] = jnp.concatenate([gram[:rank // 2], gram[rank // 2:]], axis=1)


def lower_inverse(gram):
    size = gram.shape[0]
    eye = (iota((size, size), 0) == iota((size, size), 1)).astype(F32)
    rest = jnp.concatenate([gram, eye], axis=1)
    done = []
    step = 8
    for start in range(0, size, step):
        height = size - start
        columns = [jnp.broadcast_to(rest[:, start + j:start + j + 1], (height, 2 * size))
                   for j in range(step)]
        row_number = iota((height, 2 * size), 0)
        scale = jnp.zeros((step, 2 * size), F32)
        for j in range(step):
            column = columns[j]
            pivot = column[j:j + 1]
            factor = jnp.where(row_number > j, column * reciprocal(pivot), 0.0)
            for later in range(j + 1, step):
                columns[later] = columns[later] - factor * column[later:later + 1]
            rest = rest - factor * rest[j:j + 1]
            root = lax.rsqrt(pivot)
            root = root * (1.5 - 0.5 * pivot * root * root)
            scale = jnp.where(row_number[:step] == j, root, scale)
        done.append(rest[:step] * scale)
        rest = rest[step:]
    return jnp.concatenate(done, axis=0)[:, size:]


def basis_kernel(scale_factor, groups, gram_ref, high_ref, low_ref, _, out_ref, made, sems):
    vesicles, rank, nodes = high_ref.shape[0], high_ref.shape[1], high_ref.shape[2] // 2
    folded = gram_ref[...]
    gram = jnp.concatenate([folded[:, :rank], folded[:, rank:]], axis=0)
    inverse = lower_inverse(gram) * scale_factor
    high = inverse.astype(BF16)
    low = (inverse - high.astype(F32)).astype(BF16)
    weight = jnp.concatenate([high, high, low], axis=1)
    size = vesicles // groups
    many = math.gcd(size, 4)
    copies = []
    for g in range(groups):
        for v in range(g * size, (g + 1) * size, many):
            fresh = [dot(weight, jnp.concatenate([high_ref[u], low_ref[u], high_ref[u]], axis=0))
                     for u in range(v, v + many)]
            for u, value in enumerate(fresh):
                for d in range(2):
                    made[v + u, pl.ds(d, rank, stride=2), :] = value[:, d * nodes:(d + 1) * nodes]
        here = slice(g * size, (g + 1) * size)
        copies.append(pltpu.make_async_copy(made.at[here], out_ref.at[here], sems.at[g]))
        copies[-1].start()
    for copy in copies:
        copy.wait()


def whole_spec():
    return pl.BlockSpec(memory_space=pltpu.VMEM)


def far_off_spec():
    return pl.BlockSpec(memory_space=pltpu.HBM)


def params(mib):
    return pltpu.CompilerParams(vmem_limit_bytes=mib * MIB)


def power_of_two(count):
    return count & (count - 1) == 0


def partners(count, step):
    if power_of_two(count):
        return [(i, i ^ step) for i in range(count)]
    return [(i, (i + step) % count) for i in range(count)]


def origin(index, step, count):
    if power_of_two(count):
        return jnp.bitwise_xor(index, step)
    return lax.rem(index - step + count, count)


def step_groups(count, single_first):
    if not power_of_two(count):
        return [list(range(1, count))]
    groups, bit = [], 1
    if single_first and count > 1:
        groups, bit = [[1]], 2
    while bit < count:
        groups.append([bit] if 2 * bit >= count else [bit, 2 * bit, 3 * bit])
        bit *= 4
    return groups


def add_kernel(count, *refs):
    total = refs[0][...]
    for ref in refs[1:count]:
        total = total + ref[...]
    refs[-1][...] = total


def add_after(terms, others):
    return pl.pallas_call(
        functools.partial(add_kernel, len(terms)),
        out_shape=jax.ShapeDtypeStruct(terms[0].shape, terms[0].dtype),
        in_specs=[whole_spec()] * len(terms) + [far_off_spec()] * len(others),
        out_specs=whole_spec(),
        compiler_params=params(16),
        cost_estimate=pl.CostEstimate(flops=10**4, bytes_accessed=10**5, transcendentals=0),
    )(*terms, *others)


def sum_over(value, axis, groups, others=None):
    count = lax.axis_size(axis)
    for g, steps in enumerate(groups):
        terms = [value] + [lax.ppermute(value, axis, partners(count, k)) for k in steps]
        if others is not None and g == len(groups) - 1:
            value = add_after(terms, others)
        else:
            value = sum(terms[1:], value)
    return value


def per_device(positions, tension, bending, moved_order, move_destination, move_target, far_range,
               old_basis, source_nodes):
    vesicles, _, nodes = positions.shape
    rows, sources = old_basis.shape
    rank = rows // 2
    clu_count, col_count = lax.axis_size("clu"), lax.axis_size("col")
    moves = move_target.shape[0]
    slot_cap = 2 * ((moves + clu_count - 1) // clu_count)
    flat = positions.reshape(2 * vesicles, nodes)

    columns = sources // nodes
    sent_rows = columns * rank + (2 * columns + 15) // 16 * 16
    deriv, table = spectral_tables(nodes)
    near_by = functools.partial(pltpu.with_memory_space_constraint, memory_space=pltpu.HBM)
    basis_here, nodes_here, flat_here = near_by(old_basis), near_by(source_nodes), near_by(flat)
    sent = pl.pallas_call(
        piece_kernel,
        out_shape=jax.ShapeDtypeStruct((sent_rows, nodes), BF16),
        in_specs=[far_off_spec()] * 2,
        out_specs=whole_spec(),
        scratch_shapes=[pltpu.VMEM(old_basis.shape, BF16), pltpu.VMEM(source_nodes.shape, BF16),
                        pltpu.SemaphoreType.DMA((2,))],
        compiler_params=params(16),
        cost_estimate=pl.CostEstimate(flops=10**5, bytes_accessed=10**5, transcendentals=0),
    )(basis_here, nodes_here)

    operands = [flat, tension, bending.reshape(1, vesicles), moved_order,
                move_destination.reshape(1, moves), move_target.reshape(1, moves),
                jnp.asarray(deriv), jnp.asarray(table)]
    operands = [flat_here] + [near_by(o) for o in operands[1:]]
    force, kept, leaving = pl.pallas_call(
        functools.partial(force_kernel, clu_count),
        out_shape=[jax.ShapeDtypeStruct((2 * vesicles, nodes), F32),
                   *[jax.ShapeDtypeStruct((clu_count // 2, BLOCK, 5 * nodes), F32)] * 2],
        in_specs=[far_off_spec()] * len(operands),
        out_specs=[whole_spec()] * 3,
        scratch_shapes=[pltpu.VMEM(o.shape, o.dtype) for o in operands]
        + [pltpu.SemaphoreType.DMA((len(operands),))],
        compiler_params=params(16),
        cost_estimate=pl.CostEstimate(flops=10**8, bytes_accessed=10**6, transcendentals=0),
    )(*operands)

    moved_halves = [lax.ppermute(sent, "col", partners(col_count, k)) for k in range(1, col_count)]
    arrived = cube_exchange(kept, leaving, "clu")
    pieces = []
    for mine in moved_halves:
        pieces += [mine, lax.ppermute(mine, "clu", [(i, i ^ 1) for i in range(clu_count)])]

    near_first = near_part(flat, arrived[:-1], [], slot_cap)
    near = near_part(flat, arrived[-1:], [near_first], slot_cap)

    high, low, gram = pl.pallas_call(
        functools.partial(far_kernel, col_count),
        out_shape=[jax.ShapeDtypeStruct((vesicles, rank, 2 * nodes), BF16)] * 2
        + [jax.ShapeDtypeStruct((rank // 2, 2 * rank), F32)],
        in_specs=[far_off_spec()] * 4 + [whole_spec()] * (2 * (col_count - 1)),
        out_specs=[whole_spec()] * 3,
        scratch_shapes=[
            pltpu.SMEM((1, vesicles), jnp.int32),
            pltpu.VMEM((2 * vesicles, nodes), F32),
            pltpu.VMEM((2, sources), BF16),
            pltpu.VMEM((rows, sources), BF16),
            pltpu.VMEM((col_count, rank, 2 * sources), BF16),
            pltpu.VMEM((col_count, 8, sources), F32),
            pltpu.VMEM((col_count, 2, sources, nodes), F32),
            pltpu.VMEM((rows, rows), F32),
            pltpu.SemaphoreType.DMA((4,))],
        compiler_params=params(32),
        cost_estimate=pl.CostEstimate(flops=10**10, bytes_accessed=10**7, transcendentals=10**7),
    )(near_by(far_range.reshape(1, vesicles)), flat_here, basis_here, nodes_here, *pieces)
    gram = sum_over(gram, "clu", step_groups(clu_count, True), [near_first, arrived[-1]])
    gram = sum_over(gram, "col", step_groups(col_count, False))

    scale_factor = math.sqrt(2.0 * nodes * vesicles * clu_count * col_count)
    groups = math.gcd(vesicles, 8)
    new_basis = pl.pallas_call(
        functools.partial(basis_kernel, scale_factor, groups),
        out_shape=jax.ShapeDtypeStruct((vesicles, rows, nodes), F32),
        in_specs=[whole_spec()] * 3 + [far_off_spec()],
        out_specs=far_off_spec(),
        scratch_shapes=[pltpu.VMEM((vesicles, rows, nodes), F32),
                        pltpu.SemaphoreType.DMA((groups,))],
        compiler_params=params(16),
        cost_estimate=pl.CostEstimate(flops=10**9, bytes_accessed=10**7, transcendentals=0),
    )(gram, high, low, near_by(near))

    return (force.reshape(vesicles, 2, nodes), near.reshape(vesicles, 2, nodes),
            new_basis.reshape(vesicles, rank, 2, nodes))


def solution(mesh):
    both = ("clu", "col")
    placed = (
        P(both, None, None), P(both, None), P(both), P(both, None), P(both, None), P(both),
        P(both, None), P(None, "col"), P(None, "col"),
    )
    return jax.shard_map(
        per_device,
        mesh=mesh,
        in_specs=placed,
        out_specs=(P(both, None, None), P(both, None, None), P(both, None, None, None)),
        check_vma=False,
    )
```

```python
import functools
import math

import jax
import jax.numpy as jnp
import numpy as np
from jax import lax
from jax.experimental import pallas as pl
from jax.experimental.pallas import tpu as pltpu
from jax.sharding import PartitionSpec as P

EPS_SQUARED = 0.01
F32 = jnp.float32
BF16 = jnp.bfloat16
HIGHEST = lax.Precision.HIGHEST
BLOCK = 8
DEPTH = 16
MIB = 1 << 20

NT = (((1,), (1,)), ((), ()))
NN = (((1,), (0,)), ((), ()))


def spectral_tables(node_count):
    half = node_count // 2
    j = np.arange(node_count)[:, None]
    k = np.arange(half + 1)[None, :]
    phase = (j * k % node_count) * (2.0 * math.pi / node_count)
    c, s = np.cos(phase), np.sin(phase)
    k = np.arange(half + 1, dtype=np.float64)
    inside = (k > 0) & (k < half)
    u = np.where(inside, 2.0 * k / half, 0.0)
    w = np.where(inside, 2.0 * (k / half) ** 4, np.where(k == half, 1.0, 0.0))
    derivative = ((c * u) @ s.T - (s * u) @ c.T) / node_count
    bending_table = ((c * w) @ c.T + (s * w) @ s.T) / node_count
    return derivative.T.astype(np.float32), bending_table.T.astype(np.float32)


def iota(shape, axis):
    return lax.broadcasted_iota(jnp.int32, shape, axis)


def dot(a, b, dims=NN, precision=None):
    return lax.dot_general(a, b, dims, precision=precision, preferred_element_type=F32)


def reciprocal(x):
    return pl.reciprocal(x, approx=True)


def fetch(sources, targets, sems, meanwhile=None):
    copies = [pltpu.make_async_copy(s, t, sems.at[i])
              for i, (s, t) in enumerate(zip(sources, targets))]
    for copy in copies:
        copy.start()
    if meanwhile is not None:
        meanwhile()
    for copy in copies:
        copy.wait()


def piece_kernel(own_in, nodes_in, sent_ref, own_ref, nodes_ref, sems):
    fetch([own_in, nodes_in], [own_ref, nodes_ref], sems)
    half = own_ref.shape[0] // 2
    core = lax.rem(lax.axis_index("clu"), 2)
    mine = own_ref[pl.ds(pl.multiple_of(core * half, half), half), :]
    spots = nodes_ref[...].astype(F32)
    lanes = sent_ref.shape[1]
    columns = own_ref.shape[1] // lanes
    for c in range(columns):
        sent_ref[c * half:(c + 1) * half] = mine[:, c * lanes:(c + 1) * lanes]
    spots = jnp.concatenate([spots[:, c * lanes:(c + 1) * lanes] for c in range(columns)], axis=0)
    tail = sent_ref.shape[0] - columns * half
    spots = jnp.concatenate([spots, jnp.zeros((tail - 2 * columns, lanes), F32)], axis=0)
    sent_ref[columns * half:] = spots.astype(BF16)


def cube_place(destination, own, count):
    relative = jnp.bitwise_xor(destination, own)
    place = jnp.zeros_like(relative)
    bit = 1
    while bit < count:
        place = 2 * place + jnp.bitwise_and(relative, bit) // bit
        bit *= 2
    return place


def cube_exchange(kept, leaving, axis):
    count = lax.axis_size(axis)
    assert power_of_two(count)
    held = [kept]
    bit = 1
    while True:
        held.append(lax.ppermute(leaving, axis, partners(count, bit)))
        bit *= 2
        if bit >= count:
            return held
        span = count // bit
        tails = []
        for h, part in enumerate(held):
            cut = part.reshape(-1, span, *part.shape[-2:])
            tails.append(cut[:, span // 2:].reshape(-1, *part.shape[-2:]))
            held[h] = cut[:, :span // 2].reshape(-1, *part.shape[-2:])
        leaving = jnp.concatenate(tails, axis=0)


def force_kernel(clu_count, *refs):
    sources, targets, sems = refs[:8], refs[11:19], refs[19]
    force_ref, kept_ref, leaving_ref = refs[8:11]
    fetch(sources, targets, sems)
    (pos_ref, ten_ref, bend_ref, order_ref, dest_ref, target_ref, deriv_ref, table_ref) = targets
    vesicles = ten_ref.shape[0]
    moves = target_ref.shape[1]
    x = pos_ref[pl.ds(0, vesicles, stride=2), :]
    y = pos_ref[pl.ds(1, vesicles, stride=2), :]
    rows = jnp.concatenate([x, y], axis=0)
    deriv = deriv_ref[...]
    tension = jnp.concatenate([ten_ref[...]] * 2, axis=0)
    eye = iota((vesicles, vesicles), 0) == iota((vesicles, vesicles), 1)
    bend = jnp.sum(jnp.where(eye, bend_ref[...], 0.0), axis=1, keepdims=True)
    bend = jnp.concatenate([bend] * 2, axis=0)
    slope = dot(rows, deriv, precision=HIGHEST)
    fourth = dot(rows, table_ref[...], precision=HIGHEST)
    force = dot(tension * slope, deriv, precision=HIGHEST) - bend * fourth
    force_x, force_y = force[:vesicles], force[vesicles:]
    force_ref[pl.ds(0, vesicles, stride=2), :] = force_x
    force_ref[pl.ds(1, vesicles, stride=2), :] = force_y

    slots = clu_count * BLOCK
    place = cube_place(dest_ref[...], lax.axis_index("clu"), clu_count)
    hot = (iota((clu_count, moves), 0) == place).astype(F32)
    earlier = (iota((moves, moves), 0) < iota((moves, moves), 1)).astype(F32)
    rank = jnp.sum(dot(hot, earlier) * hot, axis=0, keepdims=True).astype(jnp.int32)
    slot = place * BLOCK + rank
    pack = (iota((slots, moves), 0) == slot).astype(F32)
    pick = (iota((vesicles, moves), 0) == order_ref[:, :moves]).astype(F32)
    select = dot(pack, pick, NT)
    carried = jnp.concatenate([x, y, force_x, force_y], axis=1)
    packed = dot(select, carried, precision=HIGHEST)
    tag = jnp.sum(pack * (target_ref[...] + 1).astype(F32), axis=1, keepdims=True)
    tag = jnp.broadcast_to(tag, (slots, x.shape[1]))
    packed = jnp.concatenate([packed, tag], axis=1)
    packed = packed.reshape(clu_count, BLOCK, packed.shape[1])
    kept_ref[...] = packed[:clu_count // 2]
    leaving_ref[...] = packed[clu_count // 2:]


def near_slot(turned, tx, ty):
    nodes = tx.shape[1]
    chunk = 32 if nodes % 32 == 0 else nodes

    def fold(value):
        return jnp.sum(value.reshape(-1, 8, nodes), axis=0)

    logs_x = logs_y = pulls_x = pulls_y = jnp.zeros((8, nodes), F32)
    for start in range(0, nodes, chunk):
        sx, sy, fx, fy = [
            jnp.broadcast_to(t[start:start + chunk], (chunk, nodes)) for t in turned]
        dx = tx - sx
        dy = ty - sy
        spread = dx * dx + dy * dy + EPS_SQUARED
        logs = jnp.log(spread)
        along = (dx * fx + dy * fy) * reciprocal(spread)
        logs_x, logs_y = logs_x + fold(logs * fx), logs_y + fold(logs * fy)
        pulls_x, pulls_y = pulls_x + fold(dx * along), pulls_y + fold(dy * along)
    return (jnp.sum(pulls_x - 0.5 * logs_x, axis=0, keepdims=True),
            jnp.sum(pulls_y - 0.5 * logs_y, axis=0, keepdims=True))


def near_piece(data, tx, ty, slot_cap):
    nodes = tx.shape[1]
    turned = [data[:, c * nodes:(c + 1) * nodes].T for c in range(4)]
    return [functools.partial(near_slot, [t[:, h:h + 1] for t in turned], tx[h:h + 1], ty[h:h + 1])
            for h in range(slot_cap)]


def gather_rows(slots, axis):
    nodes = slots[0][axis].shape[1]
    rest = [jnp.zeros((BLOCK - len(slots), nodes), F32)] if len(slots) < BLOCK else []
    return jnp.concatenate([slot[axis] for slot in slots] + rest, axis=0)


def target_table(tag, vesicles):
    tag = tag.reshape(-1, tag.shape[-1])[:, :vesicles]
    return (tag == (iota(tag.shape, 1) + 1).astype(F32)).astype(F32)


def axis_rows(vesicles, axis):
    return pl.ds(axis, vesicles, stride=2)


def near_kernel(slot_cap, piece_count, pos_ref, *refs):
    piece_refs, before_refs = refs[:piece_count], refs[piece_count:-6]
    near_ref, arrived, aim_x, aim_y, speed_x, speed_y = refs[-6:]
    vesicles, nodes = pos_ref.shape[0] // 2, pos_ref.shape[1]
    here = 0
    for ref in piece_refs:
        arrived[here:here + ref.shape[0]] = ref[...]
        here += ref.shape[0]
    pieces = arrived.shape[0]
    hot = target_table(arrived[:, :, 4 * nodes:], vesicles)
    for axis, aim in enumerate((aim_x, aim_y)):
        aim[...] = dot(hot, pos_ref[axis_rows(vesicles, axis), :], precision=HIGHEST).reshape(
            pieces, BLOCK, nodes)
    many = math.gcd(pieces, 4)

    def group(i, _):
        calls = [near_piece(arrived[i * many + c], aim_x[i * many + c], aim_y[i * many + c],
                            slot_cap) for c in range(many)]
        slots = [[call() for call in piece] for piece in calls]
        for c, piece in enumerate(slots):
            speed_x[i * many + c] = gather_rows(piece, 0)
            speed_y[i * many + c] = gather_rows(piece, 1)
        return 0

    lax.fori_loop(0, pieces // many, group, 0)
    turned_hot = hot.T
    for axis, speed in enumerate((speed_x, speed_y)):
        rows = axis_rows(vesicles, axis)
        near = dot(turned_hot, speed[...].reshape(-1, nodes), precision=HIGHEST) / nodes
        for before_ref in before_refs:
            near = near + before_ref[rows, :]
        near_ref[rows, :] = near


def near_part(flat, pieces, before, slot_cap):
    vesicles, nodes = flat.shape[0] // 2, flat.shape[1]
    count = sum(p.shape[0] for p in pieces)
    return pl.pallas_call(
        functools.partial(near_kernel, slot_cap, len(pieces)),
        out_shape=jax.ShapeDtypeStruct((2 * vesicles, nodes), F32),
        in_specs=[whole_spec()] * (1 + len(pieces) + len(before)),
        out_specs=whole_spec(),
        scratch_shapes=[pltpu.VMEM((count, BLOCK, 5 * nodes), F32)]
        + [pltpu.VMEM((count, BLOCK, nodes), F32)] * 4,
        compiler_params=params(16),
        cost_estimate=pl.CostEstimate(
            flops=10**9, bytes_accessed=10**7, transcendentals=10**6),
    )(flat, *pieces, *before)


def parts_of(value, count):
    parts = []
    for _ in range(count):
        part = value.astype(BF16).astype(F32)
        parts.append(part)
        value = value - part
    return parts


def source_powers(sx, sy):
    one = jnp.ones_like(sx)
    rows = [sx] * 3 + [sy] * 3 + [one] * 3
    for value in (sx * sx, sy * sy, sx * sy):
        rows += parts_of(value, 2)
    return jnp.concatenate(rows + [jnp.zeros_like(sx)], axis=0)


def target_factors(pos_ref, factors):
    vesicles, nodes = pos_ref.shape[0] // 2, pos_ref.shape[1]
    x = pos_ref[pl.ds(0, vesicles, stride=2), :]
    y = pos_ref[pl.ds(1, vesicles, stride=2), :]
    zero = jnp.zeros_like(x)
    wanted = [
        (-2.0 * x, -2.0 * y, x * x + y * y + EPS_SQUARED, 1.0, 1.0, 0.0),
        (4.0 * x, zero, -2.0 * (x * x), -2.0, 0.0, 0.0),
        (2.0 * y, 2.0 * x, -2.0 * (x * y), 0.0, 0.0, -2.0),
        (zero, 4.0 * y, -2.0 * (y * y), 0.0, -2.0, 0.0),
    ]
    for c, entries in enumerate(wanted):
        rows = []
        for value in entries[:3]:
            rows += parts_of(value, 3)
        for value in entries[3:]:
            rows += [jnp.full_like(x, value)] * 2
        for k, row in enumerate(rows + [zero]):
            factors[c, pl.ds(k, vesicles, stride=DEPTH), :] = row


def far_kernel(col_count, range_in, pos_in, own_in, nodes_in, *refs):
    count = 2 * (col_count - 1)
    piece_refs = refs[:count]
    (high_ref, low_ref, gram_ref, range_ref, pos_ref, own_nodes, own_rows, basis, spots, powers,
     factors, sums, sems) = refs[count:]
    vesicles = pos_ref.shape[0] // 2
    nodes = pos_ref.shape[1]
    rank, sources = own_rows.shape[0] // 2, own_rows.shape[1]
    rows = 2 * rank
    core, col = lax.rem(lax.axis_index("clu"), 2), lax.axis_index("col")
    columns = sources // nodes

    def widen(r):
        powers[r] = source_powers(spots[r, 0:1], spots[r, 1:2]).T.astype(BF16)

    def lay_out_received():
        for k in range(1, col_count):
            where = origin(col, k, col_count)
            mine, other = piece_refs[2 * k - 2], piece_refs[2 * k - 1]
            ends = mine[columns * rank:].astype(F32)
            for c in range(columns):
                lanes = slice(c * nodes, (c + 1) * nodes)
                from_rows = slice(c * rank, (c + 1) * rank)
                for ref, part in ((mine, core), (other, 1 - core)):
                    there = pl.multiple_of(part * sources + c * nodes, nodes)
                    basis[where, :, pl.ds(there, nodes)] = ref[from_rows]
                spots[where, 0:2, lanes] = ends[2 * c:2 * c + 2]
            widen(where)

    fetch([range_in, pos_in, nodes_in, own_in], [range_ref, pos_ref, own_nodes, own_rows], sems,
          lay_out_received)
    basis[col, :, :sources] = own_rows[:rank]
    basis[col, :, sources:] = own_rows[rank:]
    spots[col, 0:2] = own_nodes[...].astype(F32)
    widen(col)
    target_factors(pos_ref, factors)
    sums[...] = jnp.zeros_like(sums)

    chunk = 64 if sources % 64 == 0 else sources
    depth = 256 if sources % 256 == 0 else sources

    def evaluate(v, start):
        rows_here = pl.ds(pl.multiple_of(v * DEPTH, DEPTH), DEPTH)
        mine = jnp.concatenate([factors[c, rows_here, :] for c in range(4)], axis=1).astype(BF16)
        shape = dot(powers[range_ref[0, v], start:start + chunk], mine)
        spread, xx, xy, yy = [shape[:, c * nodes:(c + 1) * nodes] for c in range(4)]
        log_part = jnp.log(spread)
        inverse = reciprocal(spread)
        return ((log_part + inverse * xx).astype(BF16), (inverse * xy).astype(BF16),
                (log_part + inverse * yy).astype(BF16))

    def sketch(v):
        r = range_ref[0, v]
        total = None
        for start in range(0, sources, depth):
            ff, fs, ss = [jnp.concatenate(p, axis=0) for p in zip(
                *[evaluate(v, start + c) for c in range(0, depth, chunk)])]
            part = dot(basis[r, :, start:start + depth], jnp.concatenate([ff, fs], axis=1))
            part += dot(basis[r, :, sources + start:sources + start + depth],
                        jnp.concatenate([fs, ss], axis=1))
            total = part if total is None else total + part
        return total

    many = math.gcd(vesicles, 8)

    def group_gram(v):
        both = jnp.concatenate([
            jnp.concatenate([ref[v + c] for c in range(many)], axis=1)
            for ref in (high_ref, low_ref)], axis=0)
        return dot(both, both, NT)

    high_ref[0:many] = jnp.zeros((many, rank, 2 * nodes), BF16)
    low_ref[0:many] = jnp.zeros((many, rank, 2 * nodes), BF16)

    def group(i, _):
        v = many * i
        before = group_gram(jnp.maximum(v - many, 0))
        made = [sketch(v + c) for c in range(many)]
        sums[...] += before
        for c, value in enumerate(made):
            high = value.astype(BF16)
            high_ref[v + c] = high
            low_ref[v + c] = (value - high.astype(F32)).astype(BF16)
        return 0

    lax.fori_loop(0, vesicles // many, group, 0)
    sums[...] += group_gram(vesicles - many)
    total = sums[...]
    gram = total[:rank, :rank] + total[rank:, rank:] + (total[:rank, rank:] + total[rank:, :rank])
    gram_ref[...] = jnp.concatenate([gram[:rank // 2], gram[rank // 2:]], axis=1)


def lower_inverse(gram):
    size = gram.shape[0]
    eye = (iota((size, size), 0) == iota((size, size), 1)).astype(F32)
    rest = jnp.concatenate([gram, eye], axis=1)
    done = []
    step = 8
    for start in range(0, size, step):
        height = size - start
        columns = [jnp.broadcast_to(rest[:, start + j:start + j + 1], (height, 2 * size))
                   for j in range(step)]
        row_number = iota((height, 2 * size), 0)
        scale = jnp.zeros((step, 2 * size), F32)
        for j in range(step):
            column = columns[j]
            pivot = column[j:j + 1]
            factor = jnp.where(row_number > j, column * reciprocal(pivot), 0.0)
            for later in range(j + 1, step):
                columns[later] = columns[later] - factor * column[later:later + 1]
            rest = rest - factor * rest[j:j + 1]
            root = lax.rsqrt(pivot)
            root = root * (1.5 - 0.5 * pivot * root * root)
            scale = jnp.where(row_number[:step] == j, root, scale)
        done.append(rest[:step] * scale)
        rest = rest[step:]
    return jnp.concatenate(done, axis=0)[:, size:]


def basis_kernel(scale_factor, groups, gram_ref, high_ref, low_ref, _, out_ref, made, sems):
    vesicles, rank, nodes = high_ref.shape[0], high_ref.shape[1], high_ref.shape[2] // 2
    folded = gram_ref[...]
    gram = jnp.concatenate([folded[:, :rank], folded[:, rank:]], axis=0)
    inverse = lower_inverse(gram) * scale_factor
    high = inverse.astype(BF16)
    low = (inverse - high.astype(F32)).astype(BF16)
    weight = jnp.concatenate([high, high, low], axis=1)
    size = vesicles // groups
    many = math.gcd(size, 4)
    copies = []
    for g in range(groups):
        for v in range(g * size, (g + 1) * size, many):
            fresh = [dot(weight, jnp.concatenate([high_ref[u], low_ref[u], high_ref[u]], axis=0))
                     for u in range(v, v + many)]
            for u, value in enumerate(fresh):
                for d in range(2):
                    made[v + u, pl.ds(d, rank, stride=2), :] = value[:, d * nodes:(d + 1) * nodes]
        here = slice(g * size, (g + 1) * size)
        copies.append(pltpu.make_async_copy(made.at[here], out_ref.at[here], sems.at[g]))
        copies[-1].start()
    for copy in copies:
        copy.wait()


def whole_spec():
    return pl.BlockSpec(memory_space=pltpu.VMEM)


def far_off_spec():
    return pl.BlockSpec(memory_space=pltpu.HBM)


def params(mib):
    return pltpu.CompilerParams(vmem_limit_bytes=mib * MIB)


def power_of_two(count):
    return count & (count - 1) == 0


def partners(count, step):
    if power_of_two(count):
        return [(i, i ^ step) for i in range(count)]
    return [(i, (i + step) % count) for i in range(count)]


def origin(index, step, count):
    if power_of_two(count):
        return jnp.bitwise_xor(index, step)
    return lax.rem(index - step + count, count)


def step_groups(count, single_first):
    if not power_of_two(count):
        return [list(range(1, count))]
    groups, bit = [], 1
    if single_first and count > 1:
        groups, bit = [[1]], 2
    while bit < count:
        groups.append([bit] if 2 * bit >= count else [bit, 2 * bit, 3 * bit])
        bit *= 4
    return groups


def add_kernel(count, *refs):
    total = refs[0][...]
    for ref in refs[1:count]:
        total = total + ref[...]
    refs[-1][...] = total


def add_after(terms, others):
    return pl.pallas_call(
        functools.partial(add_kernel, len(terms)),
        out_shape=jax.ShapeDtypeStruct(terms[0].shape, terms[0].dtype),
        in_specs=[whole_spec()] * len(terms) + [far_off_spec()] * len(others),
        out_specs=whole_spec(),
        compiler_params=params(16),
        cost_estimate=pl.CostEstimate(flops=10**4, bytes_accessed=10**5, transcendentals=0),
    )(*terms, *others)


def sum_over(value, axis, groups, others=None):
    count = lax.axis_size(axis)
    for g, steps in enumerate(groups):
        terms = [value] + [lax.ppermute(value, axis, partners(count, k)) for k in steps]
        if others is not None and g == len(groups) - 1:
            value = add_after(terms, others)
        else:
            value = sum(terms[1:], value)
    return value


def per_device(positions, tension, bending, moved_order, move_destination, move_target, far_range,
               old_basis, source_nodes):
    vesicles, _, nodes = positions.shape
    rows, sources = old_basis.shape
    rank = rows // 2
    clu_count, col_count = lax.axis_size("clu"), lax.axis_size("col")
    moves = move_target.shape[0]
    slot_cap = 2 * ((moves + clu_count - 1) // clu_count)
    flat = positions.reshape(2 * vesicles, nodes)

    columns = sources // nodes
    sent_rows = columns * rank + (2 * columns + 15) // 16 * 16
    deriv, table = spectral_tables(nodes)
    near_by = functools.partial(pltpu.with_memory_space_constraint, memory_space=pltpu.HBM)
    basis_here, nodes_here, flat_here = near_by(old_basis), near_by(source_nodes), near_by(flat)
    sent = pl.pallas_call(
        piece_kernel,
        out_shape=jax.ShapeDtypeStruct((sent_rows, nodes), BF16),
        in_specs=[far_off_spec()] * 2,
        out_specs=whole_spec(),
        scratch_shapes=[pltpu.VMEM(old_basis.shape, BF16), pltpu.VMEM(source_nodes.shape, BF16),
                        pltpu.SemaphoreType.DMA((2,))],
        compiler_params=params(16),
        cost_estimate=pl.CostEstimate(flops=10**5, bytes_accessed=10**5, transcendentals=0),
    )(basis_here, nodes_here)

    operands = [flat, tension, bending.reshape(1, vesicles), moved_order,
                move_destination.reshape(1, moves), move_target.reshape(1, moves),
                jnp.asarray(deriv), jnp.asarray(table)]
    operands = [flat_here] + [near_by(o) for o in operands[1:]]
    force, kept, leaving = pl.pallas_call(
        functools.partial(force_kernel, clu_count),
        out_shape=[jax.ShapeDtypeStruct((2 * vesicles, nodes), F32),
                   *[jax.ShapeDtypeStruct((clu_count // 2, BLOCK, 5 * nodes), F32)] * 2],
        in_specs=[far_off_spec()] * len(operands),
        out_specs=[whole_spec()] * 3,
        scratch_shapes=[pltpu.VMEM(o.shape, o.dtype) for o in operands]
        + [pltpu.SemaphoreType.DMA((len(operands),))],
        compiler_params=params(16),
        cost_estimate=pl.CostEstimate(flops=10**8, bytes_accessed=10**6, transcendentals=0),
    )(*operands)

    moved_halves = [lax.ppermute(sent, "col", partners(col_count, k)) for k in range(1, col_count)]
    arrived = cube_exchange(kept, leaving, "clu")
    pieces = []
    for mine in moved_halves:
        pieces += [mine, lax.ppermute(mine, "clu", [(i, i ^ 1) for i in range(clu_count)])]

    near_first = near_part(flat, arrived[:-1], [], slot_cap)
    near = near_part(flat, arrived[-1:], [near_first], slot_cap)

    high, low, gram = pl.pallas_call(
        functools.partial(far_kernel, col_count),
        out_shape=[jax.ShapeDtypeStruct((vesicles, rank, 2 * nodes), BF16)] * 2
        + [jax.ShapeDtypeStruct((rank // 2, 2 * rank), F32)],
        in_specs=[far_off_spec()] * 4 + [whole_spec()] * (2 * (col_count - 1)),
        out_specs=[whole_spec()] * 3,
        scratch_shapes=[
            pltpu.SMEM((1, vesicles), jnp.int32),
            pltpu.VMEM((2 * vesicles, nodes), F32),
            pltpu.VMEM((2, sources), BF16),
            pltpu.VMEM((rows, sources), BF16),
            pltpu.VMEM((col_count, rank, 2 * sources), BF16),
            pltpu.VMEM((col_count, 8, sources), F32),
            pltpu.VMEM((col_count, sources, DEPTH), BF16),
            pltpu.VMEM((4, vesicles * DEPTH, nodes), F32),
            pltpu.VMEM((rows, rows), F32),
            pltpu.SemaphoreType.DMA((4,))],
        compiler_params=params(32),
        cost_estimate=pl.CostEstimate(flops=10**10, bytes_accessed=10**7, transcendentals=10**7),
    )(near_by(far_range.reshape(1, vesicles)), flat_here, basis_here, nodes_here, *pieces)
    gram = sum_over(gram, "clu", step_groups(clu_count, True), [near_first, arrived[-1]])
    gram = sum_over(gram, "col", step_groups(col_count, False))

    scale_factor = -math.sqrt(2.0 * nodes * vesicles * clu_count * col_count)
    groups = math.gcd(vesicles, 8)
    new_basis = pl.pallas_call(
        functools.partial(basis_kernel, scale_factor, groups),
        out_shape=jax.ShapeDtypeStruct((vesicles, rows, nodes), F32),
        in_specs=[whole_spec()] * 3 + [far_off_spec()],
        out_specs=far_off_spec(),
        scratch_shapes=[pltpu.VMEM((vesicles, rows, nodes), F32),
                        pltpu.SemaphoreType.DMA((groups,))],
        compiler_params=params(16),
        cost_estimate=pl.CostEstimate(flops=10**9, bytes_accessed=10**7, transcendentals=0),
    )(gram, high, low, near_by(near))

    return (force.reshape(vesicles, 2, nodes), near.reshape(vesicles, 2, nodes),
            new_basis.reshape(vesicles, rank, 2, nodes))


def solution(mesh):
    both = ("clu", "col")
    placed = (
        P(both, None, None), P(both, None), P(both), P(both, None), P(both, None), P(both),
        P(both, None), P(None, "col"), P(None, "col"),
    )
    return jax.shard_map(
        per_device,
        mesh=mesh,
        in_specs=placed,
        out_specs=(P(both, None, None), P(both, None, None), P(both, None, None, None)),
        check_vma=False,
    )
```

```python
import functools
import math

import jax
import jax.numpy as jnp
import numpy as np
from jax import lax
from jax.experimental import pallas as pl
from jax.experimental.pallas import tpu as pltpu
from jax.sharding import PartitionSpec as P

EPS_SQUARED = 0.01
F32 = jnp.float32
BF16 = jnp.bfloat16
HIGHEST = lax.Precision.HIGHEST
BLOCK = 8
MIB = 1 << 20

NT = (((1,), (1,)), ((), ()))
NN = (((1,), (0,)), ((), ()))


def spectral_tables(node_count):
    half = node_count // 2
    j = np.arange(node_count)[:, None]
    k = np.arange(half + 1)[None, :]
    phase = (j * k % node_count) * (2.0 * math.pi / node_count)
    c, s = np.cos(phase), np.sin(phase)
    k = np.arange(half + 1, dtype=np.float64)
    inside = (k > 0) & (k < half)
    u = np.where(inside, 2.0 * k / half, 0.0)
    w = np.where(inside, 2.0 * (k / half) ** 4, np.where(k == half, 1.0, 0.0))
    derivative = ((c * u) @ s.T - (s * u) @ c.T) / node_count
    bending_table = ((c * w) @ c.T + (s * w) @ s.T) / node_count
    return derivative.T.astype(np.float32), bending_table.T.astype(np.float32)


def iota(shape, axis):
    return lax.broadcasted_iota(jnp.int32, shape, axis)


def dot(a, b, dims=NN, precision=None):
    return lax.dot_general(a, b, dims, precision=precision, preferred_element_type=F32)


def reciprocal(x):
    return pl.reciprocal(x, approx=True)


def fetch(sources, targets, sems, meanwhile=None):
    copies = [pltpu.make_async_copy(s, t, sems.at[i])
              for i, (s, t) in enumerate(zip(sources, targets))]
    for copy in copies:
        copy.start()
    if meanwhile is not None:
        meanwhile()
    for copy in copies:
        copy.wait()


def piece_kernel(own_in, nodes_in, sent_ref, own_ref, nodes_ref, sems):
    fetch([own_in, nodes_in], [own_ref, nodes_ref], sems)
    half = own_ref.shape[0] // 2
    core = lax.rem(lax.axis_index("clu"), 2)
    mine = own_ref[pl.ds(pl.multiple_of(core * half, half), half), :]
    spots = nodes_ref[...].astype(F32)
    lanes = sent_ref.shape[1]
    columns = own_ref.shape[1] // lanes
    for c in range(columns):
        sent_ref[c * half:(c + 1) * half] = mine[:, c * lanes:(c + 1) * lanes]
    spots = jnp.concatenate([spots[:, c * lanes:(c + 1) * lanes] for c in range(columns)], axis=0)
    tail = sent_ref.shape[0] - columns * half
    spots = jnp.concatenate([spots, jnp.zeros((tail - 2 * columns, lanes), F32)], axis=0)
    sent_ref[columns * half:] = spots.astype(BF16)


def cube_place(destination, own, count):
    relative = jnp.bitwise_xor(destination, own)
    place = jnp.zeros_like(relative)
    bit = 1
    while bit < count:
        place = 2 * place + jnp.bitwise_and(relative, bit) // bit
        bit *= 2
    return place


def cube_exchange(kept, leaving, axis):
    count = lax.axis_size(axis)
    assert power_of_two(count)
    held = [kept]
    bit = 1
    while True:
        held.append(lax.ppermute(leaving, axis, partners(count, bit)))
        bit *= 2
        if bit >= count:
            return held
        span = count // bit
        tails = []
        for h, part in enumerate(held):
            cut = part.reshape(-1, span, *part.shape[-2:])
            tails.append(cut[:, span // 2:].reshape(-1, *part.shape[-2:]))
            held[h] = cut[:, :span // 2].reshape(-1, *part.shape[-2:])
        leaving = jnp.concatenate(tails, axis=0)


def force_kernel(clu_count, *refs):
    sources, targets, sems = refs[:8], refs[11:19], refs[19]
    force_ref, kept_ref, leaving_ref = refs[8:11]
    fetch(sources, targets, sems)
    (pos_ref, ten_ref, bend_ref, order_ref, dest_ref, target_ref, deriv_ref, table_ref) = targets
    vesicles = ten_ref.shape[0]
    moves = target_ref.shape[1]
    x = pos_ref[pl.ds(0, vesicles, stride=2), :]
    y = pos_ref[pl.ds(1, vesicles, stride=2), :]
    rows = jnp.concatenate([x, y], axis=0)
    deriv = deriv_ref[...]
    tension = jnp.concatenate([ten_ref[...]] * 2, axis=0)
    eye = iota((vesicles, vesicles), 0) == iota((vesicles, vesicles), 1)
    bend = jnp.sum(jnp.where(eye, bend_ref[...], 0.0), axis=1, keepdims=True)
    bend = jnp.concatenate([bend] * 2, axis=0)
    slope = dot(rows, deriv, precision=HIGHEST)
    fourth = dot(rows, table_ref[...], precision=HIGHEST)
    force = dot(tension * slope, deriv, precision=HIGHEST) - bend * fourth
    force_x, force_y = force[:vesicles], force[vesicles:]
    force_ref[pl.ds(0, vesicles, stride=2), :] = force_x
    force_ref[pl.ds(1, vesicles, stride=2), :] = force_y

    slots = clu_count * BLOCK
    place = cube_place(dest_ref[...], lax.axis_index("clu"), clu_count)
    hot = (iota((clu_count, moves), 0) == place).astype(F32)
    earlier = (iota((moves, moves), 0) < iota((moves, moves), 1)).astype(F32)
    rank = jnp.sum(dot(hot, earlier) * hot, axis=0, keepdims=True).astype(jnp.int32)
    slot = place * BLOCK + rank
    pack = (iota((slots, moves), 0) == slot).astype(F32)
    pick = (iota((vesicles, moves), 0) == order_ref[:, :moves]).astype(F32)
    select = dot(pack, pick, NT)
    carried = jnp.concatenate([x, y, force_x, force_y], axis=1)
    packed = dot(select, carried, precision=HIGHEST)
    tag = jnp.sum(pack * (target_ref[...] + 1).astype(F32), axis=1, keepdims=True)
    tag = jnp.broadcast_to(tag, (slots, x.shape[1]))
    packed = jnp.concatenate([packed, tag], axis=1)
    packed = packed.reshape(clu_count, BLOCK, packed.shape[1])
    kept_ref[...] = packed[:clu_count // 2]
    leaving_ref[...] = packed[clu_count // 2:]


def near_slot(turned, tx, ty):
    nodes = tx.shape[1]
    chunk = 32 if nodes % 32 == 0 else nodes

    def fold(value):
        return jnp.sum(value.reshape(-1, 8, nodes), axis=0)

    logs_x = logs_y = pulls_x = pulls_y = jnp.zeros((8, nodes), F32)
    for start in range(0, nodes, chunk):
        sx, sy, fx, fy = [
            jnp.broadcast_to(t[start:start + chunk], (chunk, nodes)) for t in turned]
        dx = tx - sx
        dy = ty - sy
        spread = dx * dx + dy * dy + EPS_SQUARED
        logs = jnp.log(spread)
        along = (dx * fx + dy * fy) * reciprocal(spread)
        logs_x, logs_y = logs_x + fold(logs * fx), logs_y + fold(logs * fy)
        pulls_x, pulls_y = pulls_x + fold(dx * along), pulls_y + fold(dy * along)
    return (jnp.sum(pulls_x - 0.5 * logs_x, axis=0, keepdims=True),
            jnp.sum(pulls_y - 0.5 * logs_y, axis=0, keepdims=True))


def near_piece(data, tx, ty, slot_cap):
    nodes = tx.shape[1]
    turned = [data[:, c * nodes:(c + 1) * nodes].T for c in range(4)]
    return [functools.partial(near_slot, [t[:, h:h + 1] for t in turned], tx[h:h + 1], ty[h:h + 1])
            for h in range(slot_cap)]


def gather_rows(slots, axis):
    nodes = slots[0][axis].shape[1]
    rest = [jnp.zeros((BLOCK - len(slots), nodes), F32)] if len(slots) < BLOCK else []
    return jnp.concatenate([slot[axis] for slot in slots] + rest, axis=0)


def target_table(tag, vesicles):
    tag = tag.reshape(-1, tag.shape[-1])[:, :vesicles]
    return (tag == (iota(tag.shape, 1) + 1).astype(F32)).astype(F32)


def axis_rows(vesicles, axis):
    return pl.ds(axis, vesicles, stride=2)


def near_kernel(slot_cap, piece_count, pos_ref, *refs):
    piece_refs, before_refs = refs[:piece_count], refs[piece_count:-6]
    near_ref, arrived, aim_x, aim_y, speed_x, speed_y = refs[-6:]
    vesicles, nodes = pos_ref.shape[0] // 2, pos_ref.shape[1]
    here = 0
    for ref in piece_refs:
        arrived[here:here + ref.shape[0]] = ref[...]
        here += ref.shape[0]
    pieces = arrived.shape[0]
    hot = target_table(arrived[:, :, 4 * nodes:], vesicles)
    for axis, aim in enumerate((aim_x, aim_y)):
        aim[...] = dot(hot, pos_ref[axis_rows(vesicles, axis), :], precision=HIGHEST).reshape(
            pieces, BLOCK, nodes)
    many = math.gcd(pieces, 4)

    def group(i, _):
        calls = [near_piece(arrived[i * many + c], aim_x[i * many + c], aim_y[i * many + c],
                            slot_cap) for c in range(many)]
        slots = [[call() for call in piece] for piece in calls]
        for c, piece in enumerate(slots):
            speed_x[i * many + c] = gather_rows(piece, 0)
            speed_y[i * many + c] = gather_rows(piece, 1)
        return 0

    lax.fori_loop(0, pieces // many, group, 0)
    turned_hot = hot.T
    for axis, speed in enumerate((speed_x, speed_y)):
        rows = axis_rows(vesicles, axis)
        near = dot(turned_hot, speed[...].reshape(-1, nodes), precision=HIGHEST) / nodes
        for before_ref in before_refs:
            near = near + before_ref[rows, :]
        near_ref[rows, :] = near


def near_part(flat, pieces, before, slot_cap):
    vesicles, nodes = flat.shape[0] // 2, flat.shape[1]
    count = sum(p.shape[0] for p in pieces)
    return pl.pallas_call(
        functools.partial(near_kernel, slot_cap, len(pieces)),
        out_shape=jax.ShapeDtypeStruct((2 * vesicles, nodes), F32),
        in_specs=[whole_spec()] * (1 + len(pieces) + len(before)),
        out_specs=whole_spec(),
        scratch_shapes=[pltpu.VMEM((count, BLOCK, 5 * nodes), F32)]
        + [pltpu.VMEM((count, BLOCK, nodes), F32)] * 4,
        compiler_params=params(16),
        cost_estimate=pl.CostEstimate(
            flops=10**9, bytes_accessed=10**7, transcendentals=10**6),
    )(flat, *pieces, *before)


def far_kernel(col_count, range_in, pos_in, own_in, nodes_in, *refs):
    count = col_count
    piece_refs = refs[:count]
    (high_ref, low_ref, gram_ref, range_ref, pos_ref, own_nodes, own_rows, basis, spots, wide,
     sums, sems) = refs[count:]
    vesicles = pos_ref.shape[0] // 2
    nodes = pos_ref.shape[1]
    rank, sources = own_rows.shape[0] // 2, own_rows.shape[1]
    rows = 2 * rank
    core, col = lax.rem(lax.axis_index("clu"), 2), lax.axis_index("col")
    columns = sources // nodes

    def widen(r):
        turned = spots[r].T
        for c in range(2):
            wide[r, c] = jnp.broadcast_to(turned[:, c:c + 1], (sources, nodes))

    def lay_out_received():
        for k in range(1, col_count):
            where = origin(col, k, col_count)
            mine = piece_refs[k - 1]
            height = mine.shape[0]
            other = piece_refs[-1].at[(k - 1) * height:k * height]
            ends = mine[columns * rank:].astype(F32)
            for c in range(columns):
                lanes = slice(c * nodes, (c + 1) * nodes)
                from_rows = slice(c * rank, (c + 1) * rank)
                for ref, part in ((mine, core), (other, 1 - core)):
                    there = pl.multiple_of(part * sources + c * nodes, nodes)
                    basis[where, :, pl.ds(there, nodes)] = ref[from_rows]
                spots[where, 0:2, lanes] = ends[2 * c:2 * c + 2]
            widen(where)

    fetch([range_in, pos_in, nodes_in, own_in], [range_ref, pos_ref, own_nodes, own_rows], sems,
          lay_out_received)
    basis[col, :, :sources] = own_rows[:rank]
    basis[col, :, sources:] = own_rows[rank:]
    spots[col, 0:2] = own_nodes[...].astype(F32)
    widen(col)
    sums[...] = jnp.zeros_like(sums)

    chunk = 32 if sources % 32 == 0 else sources
    depth = 256 if sources % 256 == 0 else sources

    def evaluate(v, start):
        r = range_ref[0, v]
        tx = pos_ref[pl.ds(2 * v, 1), :]
        ty = pos_ref[pl.ds(2 * v + 1, 1), :]
        dx = tx - wide[r, 0, start:start + chunk]
        dy = ty - wide[r, 1, start:start + chunk]
        xx, yy = dx * dx, dy * dy
        spread = xx + yy + EPS_SQUARED
        log_part = -0.5 * jnp.log(spread)
        inverse = reciprocal(spread)
        return ((log_part + xx * inverse).astype(BF16), (dx * dy * inverse).astype(BF16),
                (log_part + yy * inverse).astype(BF16))

    def sketch(v):
        r = range_ref[0, v]
        total = None
        for start in range(0, sources, depth):
            ff, fs, ss = [jnp.concatenate(p, axis=0) for p in zip(
                *[evaluate(v, start + c) for c in range(0, depth, chunk)])]
            part = dot(basis[r, :, start:start + depth], jnp.concatenate([ff, fs], axis=1))
            part += dot(basis[r, :, sources + start:sources + start + depth],
                        jnp.concatenate([fs, ss], axis=1))
            total = part if total is None else total + part
        return total

    many = math.gcd(vesicles, 8)

    def group_gram(v):
        both = jnp.concatenate([
            jnp.concatenate([ref[v + c] for c in range(many)], axis=1)
            for ref in (high_ref, low_ref)], axis=0)
        return dot(both, both, NT)

    high_ref[0:many] = jnp.zeros((many, rank, 2 * nodes), BF16)
    low_ref[0:many] = jnp.zeros((many, rank, 2 * nodes), BF16)

    def group(i, _):
        v = many * i
        before = group_gram(jnp.maximum(v - many, 0))
        made = [sketch(v + c) for c in range(many)]
        sums[...] += before
        for c, value in enumerate(made):
            high = value.astype(BF16)
            high_ref[v + c] = high
            low_ref[v + c] = (value - high.astype(F32)).astype(BF16)
        return 0

    lax.fori_loop(0, vesicles // many, group, 0)
    sums[...] += group_gram(vesicles - many)
    total = sums[...]
    gram = total[:rank, :rank] + total[rank:, rank:] + (total[:rank, rank:] + total[rank:, :rank])
    gram_ref[...] = jnp.concatenate([gram[:rank // 2], gram[rank // 2:]], axis=1)


def lower_inverse(gram):
    size = gram.shape[0]
    eye = (iota((size, size), 0) == iota((size, size), 1)).astype(F32)
    rest = jnp.concatenate([gram, eye], axis=1)
    done = []
    step = 8
    for start in range(0, size, step):
        height = size - start
        columns = [jnp.broadcast_to(rest[:, start + j:start + j + 1], (height, 2 * size))
                   for j in range(step)]
        row_number = iota((height, 2 * size), 0)
        scale = jnp.zeros((step, 2 * size), F32)
        for j in range(step):
            column = columns[j]
            pivot = column[j:j + 1]
            factor = jnp.where(row_number > j, column * reciprocal(pivot), 0.0)
            for later in range(j + 1, step):
                columns[later] = columns[later] - factor * column[later:later + 1]
            rest = rest - factor * rest[j:j + 1]
            root = lax.rsqrt(pivot)
            root = root * (1.5 - 0.5 * pivot * root * root)
            scale = jnp.where(row_number[:step] == j, root, scale)
        done.append(rest[:step] * scale)
        rest = rest[step:]
    return jnp.concatenate(done, axis=0)[:, size:]


def basis_kernel(scale_factor, groups, gram_ref, high_ref, low_ref, _, out_ref, made, sems):
    vesicles, rank, nodes = high_ref.shape[0], high_ref.shape[1], high_ref.shape[2] // 2
    folded = gram_ref[...]
    gram = jnp.concatenate([folded[:, :rank], folded[:, rank:]], axis=0)
    inverse = lower_inverse(gram) * scale_factor
    high = inverse.astype(BF16)
    low = (inverse - high.astype(F32)).astype(BF16)
    weight = jnp.concatenate([high, high, low], axis=1)
    size = vesicles // groups
    many = math.gcd(size, 4)
    copies = []
    for g in range(groups):
        for v in range(g * size, (g + 1) * size, many):
            fresh = [dot(weight, jnp.concatenate([high_ref[u], low_ref[u], high_ref[u]], axis=0))
                     for u in range(v, v + many)]
            for u, value in enumerate(fresh):
                for d in range(2):
                    made[v + u, pl.ds(d, rank, stride=2), :] = value[:, d * nodes:(d + 1) * nodes]
        here = slice(g * size, (g + 1) * size)
        copies.append(pltpu.make_async_copy(made.at[here], out_ref.at[here], sems.at[g]))
        copies[-1].start()
    for copy in copies:
        copy.wait()


def whole_spec():
    return pl.BlockSpec(memory_space=pltpu.VMEM)


def far_off_spec():
    return pl.BlockSpec(memory_space=pltpu.HBM)


def params(mib):
    return pltpu.CompilerParams(vmem_limit_bytes=mib * MIB)


def power_of_two(count):
    return count & (count - 1) == 0


def partners(count, step):
    if power_of_two(count):
        return [(i, i ^ step) for i in range(count)]
    return [(i, (i + step) % count) for i in range(count)]


def origin(index, step, count):
    if power_of_two(count):
        return jnp.bitwise_xor(index, step)
    return lax.rem(index - step + count, count)


def step_groups(count, single_first):
    if not power_of_two(count):
        return [list(range(1, count))]
    groups, bit = [], 1
    if single_first and count > 1:
        groups, bit = [[1]], 2
    while bit < count:
        groups.append([bit] if 2 * bit >= count else [bit, 2 * bit, 3 * bit])
        bit *= 4
    return groups


def add_kernel(count, *refs):
    total = refs[0][...]
    for ref in refs[1:count]:
        total = total + ref[...]
    refs[-1][...] = total


def add_after(terms, others):
    return pl.pallas_call(
        functools.partial(add_kernel, len(terms)),
        out_shape=jax.ShapeDtypeStruct(terms[0].shape, terms[0].dtype),
        in_specs=[whole_spec()] * len(terms) + [far_off_spec()] * len(others),
        out_specs=whole_spec(),
        compiler_params=params(16),
        cost_estimate=pl.CostEstimate(flops=10**4, bytes_accessed=10**5, transcendentals=0),
    )(*terms, *others)


def sum_over(value, axis, groups, others=None):
    count = lax.axis_size(axis)
    for g, steps in enumerate(groups):
        terms = [value] + [lax.ppermute(value, axis, partners(count, k)) for k in steps]
        if others is not None and g == len(groups) - 1:
            value = add_after(terms, others)
        else:
            value = sum(terms[1:], value)
    return value


def per_device(positions, tension, bending, moved_order, move_destination, move_target, far_range,
               old_basis, source_nodes):
    vesicles, _, nodes = positions.shape
    rows, sources = old_basis.shape
    rank = rows // 2
    clu_count, col_count = lax.axis_size("clu"), lax.axis_size("col")
    moves = move_target.shape[0]
    slot_cap = 2 * ((moves + clu_count - 1) // clu_count)
    flat = positions.reshape(2 * vesicles, nodes)

    columns = sources // nodes
    sent_rows = columns * rank + (2 * columns + 15) // 16 * 16
    deriv, table = spectral_tables(nodes)
    near_by = functools.partial(pltpu.with_memory_space_constraint, memory_space=pltpu.HBM)
    basis_here, nodes_here, flat_here = near_by(old_basis), near_by(source_nodes), near_by(flat)
    sent = pl.pallas_call(
        piece_kernel,
        out_shape=jax.ShapeDtypeStruct((sent_rows, nodes), BF16),
        in_specs=[far_off_spec()] * 2,
        out_specs=whole_spec(),
        scratch_shapes=[pltpu.VMEM(old_basis.shape, BF16), pltpu.VMEM(source_nodes.shape, BF16),
                        pltpu.SemaphoreType.DMA((2,))],
        compiler_params=params(16),
        cost_estimate=pl.CostEstimate(flops=10**5, bytes_accessed=10**5, transcendentals=0),
    )(basis_here, nodes_here)

    operands = [flat, tension, bending.reshape(1, vesicles), moved_order,
                move_destination.reshape(1, moves), move_target.reshape(1, moves),
                jnp.asarray(deriv), jnp.asarray(table)]
    operands = [flat_here] + [near_by(o) for o in operands[1:]]
    force, kept, leaving = pl.pallas_call(
        functools.partial(force_kernel, clu_count),
        out_shape=[jax.ShapeDtypeStruct((2 * vesicles, nodes), F32),
                   *[jax.ShapeDtypeStruct((clu_count // 2, BLOCK, 5 * nodes), F32)] * 2],
        in_specs=[far_off_spec()] * len(operands),
        out_specs=[whole_spec()] * 3,
        scratch_shapes=[pltpu.VMEM(o.shape, o.dtype) for o in operands]
        + [pltpu.SemaphoreType.DMA((len(operands),))],
        compiler_params=params(16),
        cost_estimate=pl.CostEstimate(flops=10**8, bytes_accessed=10**6, transcendentals=0),
    )(*operands)

    moved_halves = [lax.ppermute(sent, "col", partners(col_count, k)) for k in range(1, col_count)]
    arrived = cube_exchange(kept, leaving, "clu")
    swapped = lax.ppermute(jnp.concatenate(moved_halves, axis=0), "clu",
                           [(i, i ^ 1) for i in range(clu_count)])
    pieces = [*moved_halves, swapped]

    near_first = near_part(flat, arrived[:-1], [], slot_cap)
    near = near_part(flat, arrived[-1:], [near_first], slot_cap)

    high, low, gram = pl.pallas_call(
        functools.partial(far_kernel, col_count),
        out_shape=[jax.ShapeDtypeStruct((vesicles, rank, 2 * nodes), BF16)] * 2
        + [jax.ShapeDtypeStruct((rank // 2, 2 * rank), F32)],
        in_specs=[far_off_spec()] * 4 + [whole_spec()] * col_count,
        out_specs=[whole_spec()] * 3,
        scratch_shapes=[
            pltpu.SMEM((1, vesicles), jnp.int32),
            pltpu.VMEM((2 * vesicles, nodes), F32),
            pltpu.VMEM((2, sources), BF16),
            pltpu.VMEM((rows, sources), BF16),
            pltpu.VMEM((col_count, rank, 2 * sources), BF16),
            pltpu.VMEM((col_count, 8, sources), F32),
            pltpu.VMEM((col_count, 2, sources, nodes), F32),
            pltpu.VMEM((rows, rows), F32),
            pltpu.SemaphoreType.DMA((4,))],
        compiler_params=params(32),
        cost_estimate=pl.CostEstimate(flops=10**10, bytes_accessed=10**7, transcendentals=10**7),
    )(near_by(far_range.reshape(1, vesicles)), flat_here, basis_here, nodes_here, *pieces)
    gram = sum_over(gram, "clu", step_groups(clu_count, True), [near_first, arrived[-1]])
    gram = sum_over(gram, "col", step_groups(col_count, False))

    scale_factor = math.sqrt(2.0 * nodes * vesicles * clu_count * col_count)
    groups = math.gcd(vesicles, 8)
    new_basis = pl.pallas_call(
        functools.partial(basis_kernel, scale_factor, groups),
        out_shape=jax.ShapeDtypeStruct((vesicles, rows, nodes), F32),
        in_specs=[whole_spec()] * 3 + [far_off_spec()],
        out_specs=far_off_spec(),
        scratch_shapes=[pltpu.VMEM((vesicles, rows, nodes), F32),
                        pltpu.SemaphoreType.DMA((groups,))],
        compiler_params=params(16),
        cost_estimate=pl.CostEstimate(flops=10**9, bytes_accessed=10**7, transcendentals=0),
    )(gram, high, low, near_by(near))

    return (force.reshape(vesicles, 2, nodes), near.reshape(vesicles, 2, nodes),
            new_basis.reshape(vesicles, rank, 2, nodes))


def solution(mesh):
    both = ("clu", "col")
    placed = (
        P(both, None, None), P(both, None), P(both), P(both, None), P(both, None), P(both),
        P(both, None), P(None, "col"), P(None, "col"),
    )
    return jax.shard_map(
        per_device,
        mesh=mesh,
        in_specs=placed,
        out_specs=(P(both, None, None), P(both, None, None), P(both, None, None, None)),
        check_vma=False,
    )
```

```python
import functools
import math

import jax
import jax.numpy as jnp
import numpy as np
from jax import lax
from jax.experimental import pallas as pl
from jax.experimental.pallas import tpu as pltpu
from jax.sharding import PartitionSpec as P

EPS_SQUARED = 0.01
F32 = jnp.float32
BF16 = jnp.bfloat16
HIGHEST = lax.Precision.HIGHEST
BLOCK = 8
MIB = 1 << 20

NT = (((1,), (1,)), ((), ()))
NN = (((1,), (0,)), ((), ()))


def spectral_tables(node_count):
    half = node_count // 2
    j = np.arange(node_count)[:, None]
    k = np.arange(half + 1)[None, :]
    phase = (j * k % node_count) * (2.0 * math.pi / node_count)
    c, s = np.cos(phase), np.sin(phase)
    k = np.arange(half + 1, dtype=np.float64)
    inside = (k > 0) & (k < half)
    u = np.where(inside, 2.0 * k / half, 0.0)
    w = np.where(inside, 2.0 * (k / half) ** 4, np.where(k == half, 1.0, 0.0))
    derivative = ((c * u) @ s.T - (s * u) @ c.T) / node_count
    bending_table = ((c * w) @ c.T + (s * w) @ s.T) / node_count
    return derivative.T.astype(np.float32), bending_table.T.astype(np.float32)


def iota(shape, axis):
    return lax.broadcasted_iota(jnp.int32, shape, axis)


def dot(a, b, dims=NN, precision=None):
    return lax.dot_general(a, b, dims, precision=precision, preferred_element_type=F32)


def reciprocal(x):
    return pl.reciprocal(x, approx=True)


def fetch(sources, targets, sems, meanwhile=None):
    copies = [pltpu.make_async_copy(s, t, sems.at[i])
              for i, (s, t) in enumerate(zip(sources, targets))]
    for copy in copies:
        copy.start()
    if meanwhile is not None:
        meanwhile()
    for copy in copies:
        copy.wait()


def piece_kernel(own_in, nodes_in, sent_ref, own_ref, nodes_ref, sems):
    fetch([own_in, nodes_in], [own_ref, nodes_ref], sems)
    half = own_ref.shape[0] // 2
    core = lax.rem(lax.axis_index("clu"), 2)
    mine = own_ref[pl.ds(pl.multiple_of(core * half, half), half), :]
    spots = nodes_ref[...].astype(F32)
    lanes = sent_ref.shape[1]
    columns = own_ref.shape[1] // lanes
    for c in range(columns):
        sent_ref[c * half:(c + 1) * half] = mine[:, c * lanes:(c + 1) * lanes]
    spots = jnp.concatenate([spots[:, c * lanes:(c + 1) * lanes] for c in range(columns)], axis=0)
    tail = sent_ref.shape[0] - columns * half
    spots = jnp.concatenate([spots, jnp.zeros((tail - 2 * columns, lanes), F32)], axis=0)
    sent_ref[columns * half:] = spots.astype(BF16)


def cube_place(destination, own, count):
    relative = jnp.bitwise_xor(destination, own)
    place = jnp.zeros_like(relative)
    bit = 1
    while bit < count:
        place = 2 * place + jnp.bitwise_and(relative, bit) // bit
        bit *= 2
    return place


def cube_exchange(kept, leaving, axis):
    count = lax.axis_size(axis)
    assert power_of_two(count)
    held = [kept]
    bit = 1
    while True:
        held.append(lax.ppermute(leaving, axis, partners(count, bit)))
        bit *= 2
        if bit >= count:
            return held
        span = count // bit
        tails = []
        for h, part in enumerate(held):
            cut = part.reshape(-1, span, *part.shape[-2:])
            tails.append(cut[:, span // 2:].reshape(-1, *part.shape[-2:]))
            held[h] = cut[:, :span // 2].reshape(-1, *part.shape[-2:])
        leaving = jnp.concatenate(tails, axis=0)


def force_kernel(clu_count, *refs):
    sources, targets, sems = refs[:8], refs[11:19], refs[19]
    force_ref, kept_ref, leaving_ref = refs[8:11]
    fetch(sources, targets, sems)
    (pos_ref, ten_ref, bend_ref, order_ref, dest_ref, target_ref, deriv_ref, table_ref) = targets
    vesicles = ten_ref.shape[0]
    moves = target_ref.shape[1]
    x = pos_ref[pl.ds(0, vesicles, stride=2), :]
    y = pos_ref[pl.ds(1, vesicles, stride=2), :]
    rows = jnp.concatenate([x, y], axis=0)
    deriv = deriv_ref[...]
    tension = jnp.concatenate([ten_ref[...]] * 2, axis=0)
    eye = iota((vesicles, vesicles), 0) == iota((vesicles, vesicles), 1)
    bend = jnp.sum(jnp.where(eye, bend_ref[...], 0.0), axis=1, keepdims=True)
    bend = jnp.concatenate([bend] * 2, axis=0)
    slope = dot(rows, deriv, precision=HIGHEST)
    fourth = dot(rows, table_ref[...], precision=HIGHEST)
    force = dot(tension * slope, deriv, precision=HIGHEST) - bend * fourth
    force_x, force_y = force[:vesicles], force[vesicles:]
    force_ref[pl.ds(0, vesicles, stride=2), :] = force_x
    force_ref[pl.ds(1, vesicles, stride=2), :] = force_y

    slots = clu_count * BLOCK
    place = cube_place(dest_ref[...], lax.axis_index("clu"), clu_count)
    hot = (iota((clu_count, moves), 0) == place).astype(F32)
    earlier = (iota((moves, moves), 0) < iota((moves, moves), 1)).astype(F32)
    rank = jnp.sum(dot(hot, earlier) * hot, axis=0, keepdims=True).astype(jnp.int32)
    slot = place * BLOCK + rank
    pack = (iota((slots, moves), 0) == slot).astype(F32)
    pick = (iota((vesicles, moves), 0) == order_ref[:, :moves]).astype(F32)
    select = dot(pack, pick, NT)
    carried = jnp.concatenate([x, y, force_x, force_y], axis=1)
    packed = dot(select, carried, precision=HIGHEST)
    tag = jnp.sum(pack * (target_ref[...] + 1).astype(F32), axis=1, keepdims=True)
    tag = jnp.broadcast_to(tag, (slots, x.shape[1]))
    packed = jnp.concatenate([packed, tag], axis=1)
    packed = packed.reshape(clu_count, BLOCK, packed.shape[1])
    kept_ref[...] = packed[:clu_count // 2]
    leaving_ref[...] = packed[clu_count // 2:]


def near_slot(turned, tx, ty):
    nodes = tx.shape[1]
    chunk = 32 if nodes % 32 == 0 else nodes

    def fold(value):
        return jnp.sum(value.reshape(-1, 8, nodes), axis=0)

    logs_x = logs_y = pulls_x = pulls_y = jnp.zeros((8, nodes), F32)
    for start in range(0, nodes, chunk):
        sx, sy, fx, fy = [
            jnp.broadcast_to(t[start:start + chunk], (chunk, nodes)) for t in turned]
        dx = tx - sx
        dy = ty - sy
        spread = dx * dx + dy * dy + EPS_SQUARED
        logs = jnp.log(spread)
        along = (dx * fx + dy * fy) * reciprocal(spread)
        logs_x, logs_y = logs_x + fold(logs * fx), logs_y + fold(logs * fy)
        pulls_x, pulls_y = pulls_x + fold(dx * along), pulls_y + fold(dy * along)
    return (jnp.sum(pulls_x - 0.5 * logs_x, axis=0, keepdims=True),
            jnp.sum(pulls_y - 0.5 * logs_y, axis=0, keepdims=True))


def near_piece(data, tx, ty, slot_cap):
    nodes = tx.shape[1]
    turned = [data[:, c * nodes:(c + 1) * nodes].T for c in range(4)]
    return [functools.partial(near_slot, [t[:, h:h + 1] for t in turned], tx[h:h + 1], ty[h:h + 1])
            for h in range(slot_cap)]


def gather_rows(slots, axis):
    nodes = slots[0][axis].shape[1]
    rest = [jnp.zeros((BLOCK - len(slots), nodes), F32)] if len(slots) < BLOCK else []
    return jnp.concatenate([slot[axis] for slot in slots] + rest, axis=0)


def target_table(tag, vesicles):
    tag = tag.reshape(-1, tag.shape[-1])[:, :vesicles]
    return (tag == (iota(tag.shape, 1) + 1).astype(F32)).astype(F32)


def axis_rows(vesicles, axis):
    return pl.ds(axis, vesicles, stride=2)


def near_kernel(slot_cap, piece_count, pos_ref, *refs):
    piece_refs, before_refs = refs[:piece_count], refs[piece_count:-6]
    near_ref, arrived, aim_x, aim_y, speed_x, speed_y = refs[-6:]
    vesicles, nodes = pos_ref.shape[0] // 2, pos_ref.shape[1]
    here = 0
    for ref in piece_refs:
        arrived[here:here + ref.shape[0]] = ref[...]
        here += ref.shape[0]
    pieces = arrived.shape[0]
    hot = target_table(arrived[:, :, 4 * nodes:], vesicles)
    for axis, aim in enumerate((aim_x, aim_y)):
        aim[...] = dot(hot, pos_ref[axis_rows(vesicles, axis), :], precision=HIGHEST).reshape(
            pieces, BLOCK, nodes)
    many = math.gcd(pieces, 4)

    def group(i, _):
        calls = [near_piece(arrived[i * many + c], aim_x[i * many + c], aim_y[i * many + c],
                            slot_cap) for c in range(many)]
        slots = [[call() for call in piece] for piece in calls]
        for c, piece in enumerate(slots):
            speed_x[i * many + c] = gather_rows(piece, 0)
            speed_y[i * many + c] = gather_rows(piece, 1)
        return 0

    lax.fori_loop(0, pieces // many, group, 0)
    turned_hot = hot.T
    for axis, speed in enumerate((speed_x, speed_y)):
        rows = axis_rows(vesicles, axis)
        near = dot(turned_hot, speed[...].reshape(-1, nodes), precision=HIGHEST) / nodes
        for before_ref in before_refs:
            near = near + before_ref[rows, :]
        near_ref[rows, :] = near


def near_part(flat, pieces, before, slot_cap):
    vesicles, nodes = flat.shape[0] // 2, flat.shape[1]
    count = sum(p.shape[0] for p in pieces)
    return pl.pallas_call(
        functools.partial(near_kernel, slot_cap, len(pieces)),
        out_shape=jax.ShapeDtypeStruct((2 * vesicles, nodes), F32),
        in_specs=[whole_spec()] * (1 + len(pieces) + len(before)),
        out_specs=whole_spec(),
        scratch_shapes=[pltpu.VMEM((count, BLOCK, 5 * nodes), F32)]
        + [pltpu.VMEM((count, BLOCK, nodes), F32)] * 4,
        compiler_params=params(16),
        cost_estimate=pl.CostEstimate(
            flops=10**9, bytes_accessed=10**7, transcendentals=10**6),
    )(flat, *pieces, *before)


def far_kernel(col_count, range_in, pos_in, own_in, nodes_in, *refs):
    count = 2 * (col_count - 1)
    piece_refs = refs[:count]
    (high_ref, low_ref, gram_ref, range_ref, pos_ref, own_nodes, own_rows, basis, spots, wide,
     sums, sems) = refs[count:]
    vesicles = pos_ref.shape[0] // 2
    nodes = pos_ref.shape[1]
    rank, sources = own_rows.shape[0] // 2, own_rows.shape[1]
    rows = 2 * rank
    core, col = lax.rem(lax.axis_index("clu"), 2), lax.axis_index("col")
    columns = sources // nodes

    def widen(r):
        turned = spots[r].T
        for c in range(2):
            wide[r, c] = jnp.broadcast_to(turned[:, c:c + 1], (sources, nodes))

    def lay_out_received():
        for k in range(1, col_count):
            where = origin(col, k, col_count)
            mine, other = piece_refs[2 * k - 2], piece_refs[2 * k - 1]
            ends = mine[columns * rank:].astype(F32)
            for c in range(columns):
                lanes = slice(c * nodes, (c + 1) * nodes)
                from_rows = slice(c * rank, (c + 1) * rank)
                for ref, part in ((mine, core), (other, 1 - core)):
                    there = pl.multiple_of(part * sources + c * nodes, nodes)
                    basis[where, :, pl.ds(there, nodes)] = ref[from_rows]
                spots[where, 0:2, lanes] = ends[2 * c:2 * c + 2]
            widen(where)

    fetch([range_in, pos_in, nodes_in, own_in], [range_ref, pos_ref, own_nodes, own_rows], sems,
          lay_out_received)
    basis[col, :, :sources] = own_rows[:rank]
    basis[col, :, sources:] = own_rows[rank:]
    spots[col, 0:2] = own_nodes[...].astype(F32)
    widen(col)
    sums[...] = jnp.zeros_like(sums)

    chunk = 32 if sources % 32 == 0 else sources
    depth = 256 if sources % 256 == 0 else sources

    def evaluate(v, start):
        r = range_ref[0, v]
        tx = pos_ref[pl.ds(2 * v, 1), :]
        ty = pos_ref[pl.ds(2 * v + 1, 1), :]
        dx = tx - wide[r, 0, start:start + chunk]
        dy = ty - wide[r, 1, start:start + chunk]
        xx, yy = dx * dx, dy * dy
        spread = xx + yy + EPS_SQUARED
        log_part = -0.5 * jnp.log(spread)
        inverse = reciprocal(spread)
        return ((log_part + xx * inverse).astype(BF16), (dx * dy * inverse).astype(BF16),
                (log_part + yy * inverse).astype(BF16))

    def sketch(v):
        r = range_ref[0, v]
        total = None
        for start in range(0, sources, depth):
            ff, fs, ss = [jnp.concatenate(p, axis=0) for p in zip(
                *[evaluate(v, start + c) for c in range(0, depth, chunk)])]
            part = dot(basis[r, :, start:start + depth], jnp.concatenate([ff, fs], axis=1))
            part += dot(basis[r, :, sources + start:sources + start + depth],
                        jnp.concatenate([fs, ss], axis=1))
            total = part if total is None else total + part
        return total

    many = math.gcd(vesicles, 8)

    def group_gram(v):
        both = jnp.concatenate([
            jnp.concatenate([ref[v + c] for c in range(many)], axis=1)
            for ref in (high_ref, low_ref)], axis=0)
        return dot(both, both, NT)

    high_ref[0:many] = jnp.zeros((many, rank, 2 * nodes), BF16)
    low_ref[0:many] = jnp.zeros((many, rank, 2 * nodes), BF16)

    def group(i, _):
        v = many * i
        before = group_gram(jnp.maximum(v - many, 0))
        made = [sketch(v + c) for c in range(many)]
        sums[...] += before
        for c, value in enumerate(made):
            high = value.astype(BF16)
            high_ref[v + c] = high
            low_ref[v + c] = (value - high.astype(F32)).astype(BF16)
        return 0

    lax.fori_loop(0, vesicles // many, group, 0)
    sums[...] += group_gram(vesicles - many)
    total = sums[...]
    gram = total[:rank, :rank] + total[rank:, rank:] + (total[:rank, rank:] + total[rank:, :rank])
    gram_ref[...] = jnp.concatenate([gram[:rank // 2], gram[rank // 2:]], axis=1)


def lower_inverse(gram):
    size = gram.shape[0]
    eye = (iota((size, size), 0) == iota((size, size), 1)).astype(F32)
    rest = jnp.concatenate([gram, eye], axis=1)
    done = []
    step = 16
    for start in range(0, size, step):
        height = size - start
        columns = [jnp.broadcast_to(rest[:, start + j:start + j + 1], (height, 2 * size))
                   for j in range(step)]
        row_number = iota((height, 2 * size), 0)
        scale = jnp.zeros((step, 2 * size), F32)
        for j in range(step):
            column = columns[j]
            pivot = column[j:j + 1]
            factor = jnp.where(row_number > j, column * reciprocal(pivot), 0.0)
            for later in range(j + 1, step):
                columns[later] = columns[later] - factor * column[later:later + 1]
            rest = rest - factor * rest[j:j + 1]
            root = lax.rsqrt(pivot)
            root = root * (1.5 - 0.5 * pivot * root * root)
            scale = jnp.where(row_number[:step] == j, root, scale)
        done.append(rest[:step] * scale)
        rest = rest[step:]
    return jnp.concatenate(done, axis=0)[:, size:]


def basis_kernel(scale_factor, groups, gram_ref, high_ref, low_ref, _, out_ref, made, sems):
    vesicles, rank, nodes = high_ref.shape[0], high_ref.shape[1], high_ref.shape[2] // 2
    folded = gram_ref[...]
    gram = jnp.concatenate([folded[:, :rank], folded[:, rank:]], axis=0)
    inverse = lower_inverse(gram) * scale_factor
    high = inverse.astype(BF16)
    low = (inverse - high.astype(F32)).astype(BF16)
    weight = jnp.concatenate([high, high, low], axis=1)
    size = vesicles // groups
    many = math.gcd(size, 4)
    copies = []
    for g in range(groups):
        for v in range(g * size, (g + 1) * size, many):
            fresh = [dot(weight, jnp.concatenate([high_ref[u], low_ref[u], high_ref[u]], axis=0))
                     for u in range(v, v + many)]
            for u, value in enumerate(fresh):
                for d in range(2):
                    made[v + u, pl.ds(d, rank, stride=2), :] = value[:, d * nodes:(d + 1) * nodes]
        here = slice(g * size, (g + 1) * size)
        copies.append(pltpu.make_async_copy(made.at[here], out_ref.at[here], sems.at[g]))
        copies[-1].start()
    for copy in copies:
        copy.wait()


def whole_spec():
    return pl.BlockSpec(memory_space=pltpu.VMEM)


def far_off_spec():
    return pl.BlockSpec(memory_space=pltpu.HBM)


def params(mib):
    return pltpu.CompilerParams(vmem_limit_bytes=mib * MIB)


def power_of_two(count):
    return count & (count - 1) == 0


def partners(count, step):
    if power_of_two(count):
        return [(i, i ^ step) for i in range(count)]
    return [(i, (i + step) % count) for i in range(count)]


def origin(index, step, count):
    if power_of_two(count):
        return jnp.bitwise_xor(index, step)
    return lax.rem(index - step + count, count)


def step_groups(count, single_first):
    if not power_of_two(count):
        return [list(range(1, count))]
    groups, bit = [], 1
    if single_first and count > 1:
        groups, bit = [[1]], 2
    while bit < count:
        groups.append([bit] if 2 * bit >= count else [bit, 2 * bit, 3 * bit])
        bit *= 4
    return groups


def add_kernel(count, *refs):
    total = refs[0][...]
    for ref in refs[1:count]:
        total = total + ref[...]
    refs[-1][...] = total


def add_after(terms, others):
    return pl.pallas_call(
        functools.partial(add_kernel, len(terms)),
        out_shape=jax.ShapeDtypeStruct(terms[0].shape, terms[0].dtype),
        in_specs=[whole_spec()] * len(terms) + [far_off_spec()] * len(others),
        out_specs=whole_spec(),
        compiler_params=params(16),
        cost_estimate=pl.CostEstimate(flops=10**4, bytes_accessed=10**5, transcendentals=0),
    )(*terms, *others)


def sum_over(value, axis, groups, others=None):
    count = lax.axis_size(axis)
    for g, steps in enumerate(groups):
        terms = [value] + [lax.ppermute(value, axis, partners(count, k)) for k in steps]
        if others is not None and g == len(groups) - 1:
            value = add_after(terms, others)
        else:
            value = sum(terms[1:], value)
    return value


def per_device(positions, tension, bending, moved_order, move_destination, move_target, far_range,
               old_basis, source_nodes):
    vesicles, _, nodes = positions.shape
    rows, sources = old_basis.shape
    rank = rows // 2
    clu_count, col_count = lax.axis_size("clu"), lax.axis_size("col")
    moves = move_target.shape[0]
    slot_cap = 2 * ((moves + clu_count - 1) // clu_count)
    flat = positions.reshape(2 * vesicles, nodes)

    columns = sources // nodes
    sent_rows = columns * rank + (2 * columns + 15) // 16 * 16
    deriv, table = spectral_tables(nodes)
    near_by = functools.partial(pltpu.with_memory_space_constraint, memory_space=pltpu.HBM)
    basis_here, nodes_here, flat_here = near_by(old_basis), near_by(source_nodes), near_by(flat)
    sent = pl.pallas_call(
        piece_kernel,
        out_shape=jax.ShapeDtypeStruct((sent_rows, nodes), BF16),
        in_specs=[far_off_spec()] * 2,
        out_specs=whole_spec(),
        scratch_shapes=[pltpu.VMEM(old_basis.shape, BF16), pltpu.VMEM(source_nodes.shape, BF16),
                        pltpu.SemaphoreType.DMA((2,))],
        compiler_params=params(16),
        cost_estimate=pl.CostEstimate(flops=10**5, bytes_accessed=10**5, transcendentals=0),
    )(basis_here, nodes_here)

    operands = [flat, tension, bending.reshape(1, vesicles), moved_order,
                move_destination.reshape(1, moves), move_target.reshape(1, moves),
                jnp.asarray(deriv), jnp.asarray(table)]
    operands = [flat_here] + [near_by(o) for o in operands[1:]]
    force, kept, leaving = pl.pallas_call(
        functools.partial(force_kernel, clu_count),
        out_shape=[jax.ShapeDtypeStruct((2 * vesicles, nodes), F32),
                   *[jax.ShapeDtypeStruct((clu_count // 2, BLOCK, 5 * nodes), F32)] * 2],
        in_specs=[far_off_spec()] * len(operands),
        out_specs=[whole_spec()] * 3,
        scratch_shapes=[pltpu.VMEM(o.shape, o.dtype) for o in operands]
        + [pltpu.SemaphoreType.DMA((len(operands),))],
        compiler_params=params(16),
        cost_estimate=pl.CostEstimate(flops=10**8, bytes_accessed=10**6, transcendentals=0),
    )(*operands)

    moved_halves = [lax.ppermute(sent, "col", partners(col_count, k)) for k in range(1, col_count)]
    arrived = cube_exchange(kept, leaving, "clu")
    pieces = []
    for mine in moved_halves:
        pieces += [mine, lax.ppermute(mine, "clu", [(i, i ^ 1) for i in range(clu_count)])]

    near_first = near_part(flat, arrived[:-1], [], slot_cap)
    near = near_part(flat, arrived[-1:], [near_first], slot_cap)

    high, low, gram = pl.pallas_call(
        functools.partial(far_kernel, col_count),
        out_shape=[jax.ShapeDtypeStruct((vesicles, rank, 2 * nodes), BF16)] * 2
        + [jax.ShapeDtypeStruct((rank // 2, 2 * rank), F32)],
        in_specs=[far_off_spec()] * 4 + [whole_spec()] * (2 * (col_count - 1)),
        out_specs=[whole_spec()] * 3,
        scratch_shapes=[
            pltpu.SMEM((1, vesicles), jnp.int32),
            pltpu.VMEM((2 * vesicles, nodes), F32),
            pltpu.VMEM((2, sources), BF16),
            pltpu.VMEM((rows, sources), BF16),
            pltpu.VMEM((col_count, rank, 2 * sources), BF16),
            pltpu.VMEM((col_count, 8, sources), F32),
            pltpu.VMEM((col_count, 2, sources, nodes), F32),
            pltpu.VMEM((rows, rows), F32),
            pltpu.SemaphoreType.DMA((4,))],
        compiler_params=params(32),
        cost_estimate=pl.CostEstimate(flops=10**10, bytes_accessed=10**7, transcendentals=10**7),
    )(near_by(far_range.reshape(1, vesicles)), flat_here, basis_here, nodes_here, *pieces)
    gram = sum_over(gram, "clu", step_groups(clu_count, True), [near_first, arrived[-1]])
    gram = sum_over(gram, "col", step_groups(col_count, False))

    scale_factor = math.sqrt(2.0 * nodes * vesicles * clu_count * col_count)
    groups = math.gcd(vesicles, 8)
    new_basis = pl.pallas_call(
        functools.partial(basis_kernel, scale_factor, groups),
        out_shape=jax.ShapeDtypeStruct((vesicles, rows, nodes), F32),
        in_specs=[whole_spec()] * 3 + [far_off_spec()],
        out_specs=far_off_spec(),
        scratch_shapes=[pltpu.VMEM((vesicles, rows, nodes), F32),
                        pltpu.SemaphoreType.DMA((groups,))],
        compiler_params=params(16),
        cost_estimate=pl.CostEstimate(flops=10**9, bytes_accessed=10**7, transcendentals=0),
    )(gram, high, low, near_by(near))

    return (force.reshape(vesicles, 2, nodes), near.reshape(vesicles, 2, nodes),
            new_basis.reshape(vesicles, rank, 2, nodes))


def solution(mesh):
    both = ("clu", "col")
    placed = (
        P(both, None, None), P(both, None), P(both), P(both, None), P(both, None), P(both),
        P(both, None), P(None, "col"), P(None, "col"),
    )
    return jax.shard_map(
        per_device,
        mesh=mesh,
        in_specs=placed,
        out_specs=(P(both, None, None), P(both, None, None), P(both, None, None, None)),
        check_vma=False,
    )
```
